32 devices in a mesh: wide: 8 (over z, x), head: 4 (over y, core).
Axes of the slice: x: 2, y: 2, z: 4, core: 2. Of those that a mesh axis runs over, the one named last changes fastest.
Arguments:
- tokens_a: bfloat16 [1024, 768], P(('wide', 'head')), may hold values from -6 to 6
- tokens_b: bfloat16 [2048, 768], P(('wide', 'head')), may hold values from -6 to 6
- tokens_c: bfloat16 [4096, 768], P(('wide', 'head')), may hold values from -6 to 6
- lengths_a: int32 [8], P('wide'), may hold values from 65 to 128, as said below
- lengths_b: int32 [8], P('wide'), may hold values from 129 to 256, as said below
- lengths_c: int32 [8], P('wide'), may hold values from 257 to 512, as said below
- cotan_a: bfloat16 [1024, 768], P(('wide', 'head')), may hold values from -6 to 6
- cotan_b: bfloat16 [2048, 768], P(('wide', 'head')), may hold values from -6 to 6
- cotan_c: bfloat16 [4096, 768], P(('wide', 'head')), may hold values from -6 to 6
- ln_gain: float32 [2, 2, 768], replicated, may hold values from 0.5 to 1.5
- ln_bias: float32 [2, 2, 768], replicated, may hold values from -1.2 to 1.2
- row_bias: float32 [2, 2, 768], replicated, may hold values from -1.2 to 1.2
- out_weight: bfloat16 [2, 768, 768], P(None, ('wide', 'head')), may hold values from -1.75 to 1.75
- up_weight: bfloat16 [2, 3072, 768], P(None, ('wide', 'head')), may hold values from -0.21875 to 0.21875
- up_bias: float32 [2, 3072], P(None, ('wide', 'head')), may hold values from -1.2 to 1.2
- down_weight: bfloat16 [2, 3072, 768], P(None, ('wide', 'head')), may hold values from -0.109375 to 0.109375
- synth_first: bfloat16 [12, 64, 64], P('head'), may hold values from -0.75 to 0.75
- synth_first_bias: float32 [12, 64], P('head'), may hold values from -3 to 3
- synth_second: bfloat16 [12, 64, 512], P('head'), may hold values from -1.5 to 1.5
- synth_second_bias: float32 [12, 512], P('head'), may hold values from -3 to 3
- random_scores: bfloat16 [12, 512, 512], P('head'), may hold values from -9 to 9
- value_weight: bfloat16 [2, 12, 64, 64], P(None, 'head'), may hold values from -0.75 to 0.75
Outputs:
- out_a: bfloat16 [1024, 768], P(('wide', 'head'))
- out_b: bfloat16 [2048, 768], P(('wide', 'head'))
- out_c: bfloat16 [4096, 768], P(('wide', 'head'))
- grad_a: float32 [1024, 768], P(('wide', 'head'))
- grad_b: float32 [2048, 768], P(('wide', 'head'))
- grad_c: float32 [4096, 768], P(('wide', 'head'))
- grad_ln_gain: float32 [2, 2, 768], replicated
- grad_ln_bias: float32 [2, 2, 768], replicated
- grad_row_bias: float32 [2, 2, 768], replicated
- grad_out_weight: float32 [2, 768, 768], P(None, ('wide', 'head'))
- grad_up_weight: float32 [2, 3072, 768], P(None, ('wide', 'head'))
- grad_up_bias: float32 [2, 3072], P(None, ('wide', 'head'))
- grad_down_weight: float32 [2, 3072, 768], P(None, ('wide', 'head'))
- grad_synth_first: float32 [12, 64, 64], P('head', 'wide')
- grad_synth_first_bias: float32 [12, 64], P('head', 'wide')
- grad_synth_second: float32 [12, 64, 512], P('head', 'wide')
- grad_synth_second_bias: float32 [12, 512], P('head', 'wide')
- grad_random_scores: float32 [12, 512, 512], P('head', 'wide')
- grad_value_weight: float32 [2, 12, 64, 64], P(None, 'head', 'wide')
The draws below stay inside these ranges and needn't reach their ends.
Inputs may be any that keep to these rules, and one draw needn't show every extreme that they name: `lengths_a`: each item's valid length is more than half of its bucket's padded length 128; in each aligned group of 1 items one item has length exactly 128. `lengths_b`: each item's valid length is more than half of 256; in each aligned group of 1 items one item has length exactly 256. `lengths_c`: each item's valid length is more than half of 512; in each aligned group of 1 items one item has length exactly 512.
All inputs are finite; a program needn't handle non-finite values.
Results may differ from the reference program's by a relative error of at most 0.019.
Values may be sent and summed in bfloat16 or wider, within the bound.
No kernel may reach another device: no remote copies, remote signals or barrier semaphores. Data moves between devices by JAX's collectives and lax.ppermute only.
A program may use at most 256 MiB of HBM per device.

```python
import jax
import jax.numpy as jnp
from jax import lax

D = 768
H = 12
HD = 64
FF = 3072
LC = 512
LA = 128
LB = 256
LAYERS = 2
ITEMS = 1
ITEMS_ALL = 8
TOK_A = 1024
TOK_B = 2048
TOK_C = 4096
N_WIDE = 8


def draw_bucket(key, span_len):
    short_key, pick_key = jax.random.split(key)
    varied = jax.random.randint(short_key, (ITEMS_ALL // ITEMS, ITEMS), span_len // 2 + 1, span_len + 1)
    chosen = jax.random.randint(pick_key, (ITEMS_ALL // ITEMS, 1), 0, ITEMS)
    full_item = jnp.arange(ITEMS)[None, :] == chosen
    return jnp.where(full_item, span_len, varied).reshape(ITEMS_ALL).astype(jnp.int32)


def draw_lengths_a(key, part):
    key = jax.random.fold_in(key, 11)
    return draw_bucket(key, LA)


def draw_lengths_b(key, part):
    key = jax.random.fold_in(key, 23)
    return draw_bucket(key, LB)


def draw_lengths_c(key, part):
    key = jax.random.fold_in(key, 37)
    return draw_bucket(key, LC)


def shard_levels(key, shape, shards, low, top_value):
    loudness, own = 1.0, jax.random.fold_in(key, 6)
    for dim, shards_of in shards:
        heights = jnp.exp(jax.random.uniform(jax.random.fold_in(own, dim), (shards_of,), jnp.float32, low / len(shards), top_value / len(shards)))
        loudness = loudness * jnp.repeat(heights, shape[dim] // shards_of).reshape([-1 if axis == dim else 1 for axis in range(len(shape))])
    return loudness


def noise(stream_key, extent, scale, bound, pieces=(), held_as=jnp.bfloat16):
    drawn = scale * jax.random.normal(stream_key, extent, jnp.float32)
    if pieces:
        drawn = drawn * shard_levels(stream_key, extent, pieces, -0.22, 0.18)
    return jnp.clip(drawn, -bound, bound).astype(held_as)


def setup_inputs(seed: int = 0) -> dict:
    keys = jax.random.split(jax.random.key(seed), 23)
    return {
        "tokens_a": noise(keys[0], (TOK_A, D), 1.0, 6.0, ((0, 32),)),
        "tokens_b": noise(keys[1], (TOK_B, D), 1.0, 6.0, ((0, 32),)),
        "tokens_c": noise(keys[2], (TOK_C, D), 1.0, 6.0, ((0, 32),)),
        "lengths_a": draw_lengths_a(jax.random.fold_in(keys[22], 71), 0),
        "lengths_b": draw_lengths_b(jax.random.fold_in(keys[22], 71), 0),
        "lengths_c": draw_lengths_c(jax.random.fold_in(keys[22], 71), 0),
        "cotan_a": noise(keys[6], (TOK_A, D), 1.0, 6.0, ((0, 32),)),
        "cotan_b": noise(keys[7], (TOK_B, D), 1.0, 6.0, ((0, 32),)),
        "cotan_c": noise(keys[8], (TOK_C, D), 1.0, 6.0, ((0, 32),)),
        "ln_gain": jnp.clip(1.0 + 0.1 * jax.random.normal(keys[9], (LAYERS, 2, D), jnp.float32), 0.5, 1.5),
        "ln_bias": noise(keys[10], (LAYERS, 2, D), 0.2, 1.2, (), jnp.float32),
        "row_bias": noise(keys[11], (LAYERS, 2, D), 0.2, 1.2, (), jnp.float32),
        "out_weight": noise(keys[12], (LAYERS, D, D), (D // 64) ** -0.5, 1.75, ((1, 32),)),
        "up_weight": noise(keys[13], (LAYERS, FF, D), D ** -0.5, 0.21875, ((1, 32),)),
        "up_bias": noise(keys[14], (LAYERS, FF), 0.2, 1.2, ((1, 32),), jnp.float32),
        "down_weight": noise(keys[15], (LAYERS, FF, D), FF ** -0.5, 0.109375, ((1, 32),)),
        "synth_first": noise(keys[16], (H, HD, HD), HD ** -0.5, 0.75, ((0, 4),)),
        "synth_first_bias": noise(keys[17], (H, HD), 0.5, 3.0, ((0, 4),), jnp.float32),
        "synth_second": noise(keys[18], (H, HD, LC), (HD // 4) ** -0.5, 1.5, ((0, 4),)),
        "synth_second_bias": noise(keys[19], (H, LC), 0.5, 3.0, ((0, 4),), jnp.float32),
        "random_scores": noise(keys[20], (H, LC, LC), 1.5, 9.0, ((0, 4),)),
        "value_weight": noise(keys[21], (LAYERS, H, HD, HD), HD ** -0.5, 0.75, ((1, 4),)),
    }


@jax.custom_vjp
def low(v):
    return lax.optimization_barrier(v.astype(jnp.bfloat16)).astype(jnp.float32)

@jax.custom_vjp
def low_back(v):
    return v

def low_keep(v):
    return (low(v), None)

def low_pass(kept, grad):
    return (grad,)

def back_keep(v):
    return (v, None)

def back_low(kept, grad):
    return (low(grad),)
low.defvjp(low_keep, low_pass)
low_back.defvjp(back_keep, back_low)
PRECISE = lax.Precision.HIGHEST
EPSILON = 1e-05
MASKED_SCORE = -1e+30

def normalize(token_rows, gain_row, shift_row):
    middle = lax.optimization_barrier(jnp.mean(token_rows, axis=-1, keepdims=True))
    centred = token_rows - middle
    spread = lax.optimization_barrier(jnp.mean(centred * centred, axis=-1, keepdims=True))
    return centred * lax.rsqrt(spread + EPSILON) * gain_row + shift_row

def synthesize(level_index, head_block, span_len, item_lengths, params):
    first = params[7]
    first_bias = params[8]
    second = params[9]
    second_bias = params[10]
    random_scores = params[11]
    value_weight = params[12]
    item_count = head_block.shape[0] // span_len
    head_grid = head_block.reshape(item_count, span_len, H, HD)
    if level_index == 0:
        pre_act = low_back(jnp.einsum('ilhd,hde->ilhe', head_grid, first, precision=PRECISE) + first_bias[None, None])
        activated = low(jax.nn.gelu(pre_act))
        raw_scores = low_back(jnp.einsum('ilhe,hej->ihlj', activated, second[:, :, :span_len], precision=PRECISE) + second_bias[None, :, None, :span_len])
    else:
        raw_scores = jnp.broadcast_to(random_scores[None, :, :span_len, :span_len], (item_count, H, span_len, span_len))
    key_mask = (jnp.arange(span_len)[None, :] < item_lengths[:, None])[:, None, None, :]
    masked = jnp.where(key_mask, raw_scores, MASKED_SCORE)
    softened = low(jax.nn.softmax(masked, axis=-1))
    values_low = low_back(low(jnp.einsum('ilhd,hde->ilhe', head_grid, value_weight[level_index], precision=PRECISE)))
    mixed = jnp.einsum('ihlj,ijhe->ilhe', softened, values_low, precision=PRECISE)
    return low_back(low(mixed)).reshape(item_count * span_len, H * HD)

def forward(group_rows, group_lengths, params):
    ln_gain = params[0]
    ln_bias = params[1]
    row_bias = params[2]
    out_weight = params[3]
    up_weight = params[4]
    up_bias = params[5]
    down_weight = params[6]
    spans = (LA, LB, LC)
    counts = [segment.shape[0] for segment in group_rows]
    token_rows = jnp.concatenate(group_rows, axis=0)
    for level_index in range(LAYERS):
        normed = low_back(low(normalize(token_rows, ln_gain[level_index, 0], ln_bias[level_index, 0])))
        mixed_parts = []
        offset = 0
        for bucket_index in range(3):
            segment = normed[offset:offset + counts[bucket_index]]
            offset = offset + counts[bucket_index]
            mixed_parts.append(synthesize(level_index, segment, spans[bucket_index], group_lengths[bucket_index], params))
        mixed_rows = jnp.concatenate(mixed_parts, axis=0)
        joined = low_back(jnp.dot(mixed_rows, out_weight[level_index], precision=PRECISE) + row_bias[level_index, 0])
        resid = token_rows + joined
        normed2 = low(normalize(resid, ln_gain[level_index, 1], ln_bias[level_index, 1]))
        pre_ffn = low_back(jnp.dot(normed2, up_weight[level_index].T, precision=PRECISE) + up_bias[level_index])
        hidden = low(jax.nn.gelu(pre_ffn))
        ffn_out = low_back(jnp.dot(hidden, down_weight[level_index], precision=PRECISE) + row_bias[level_index, 1])
        token_rows = resid + ffn_out
    first_end = counts[0]
    second_end = counts[0] + counts[1]
    return (token_rows[:first_end], token_rows[first_end:second_end], token_rows[second_end:])

def reference(tokens_a, tokens_b, tokens_c, lengths_a, lengths_b, lengths_c, cotan_a, cotan_b, cotan_c, ln_gain, ln_bias, row_bias, out_weight, up_weight, up_bias, down_weight, synth_first, synth_first_bias, synth_second, synth_second_bias, random_scores, value_weight):
    params = tuple((weight_item.astype(jnp.float32) for weight_item in (ln_gain, ln_bias, row_bias, out_weight, up_weight, up_bias, down_weight, synth_first, synth_first_bias, synth_second, synth_second_bias, random_scores, value_weight)))
    group_inputs = (tokens_a.astype(jnp.float32).reshape(N_WIDE, ITEMS * LA, D), tokens_b.astype(jnp.float32).reshape(N_WIDE, ITEMS * LB, D), tokens_c.astype(jnp.float32).reshape(N_WIDE, ITEMS * LC, D), lengths_a.reshape(N_WIDE, ITEMS), lengths_b.reshape(N_WIDE, ITEMS), lengths_c.reshape(N_WIDE, ITEMS), cotan_a.astype(jnp.float32).reshape(N_WIDE, ITEMS * LA, D), cotan_b.astype(jnp.float32).reshape(N_WIDE, ITEMS * LB, D), cotan_c.astype(jnp.float32).reshape(N_WIDE, ITEMS * LC, D))

    def group_step(totals, group_item):
        rows_first, rows_second, rows_third, lens_first, lens_second, lens_third, cot_first, cot_second, cot_third = group_item

        def group_forward(in_first, in_second, in_third, weights_all):
            return forward((in_first, in_second, in_third), (lens_first, lens_second, lens_third), weights_all)
        outputs, pull_back = jax.vjp(group_forward, rows_first, rows_second, rows_third, params)
        grad_first, grad_second, grad_third, grad_params = pull_back((cot_first, cot_second, cot_third))
        totals = jax.tree.map(lambda total_part, grad_part: total_part + grad_part, totals, grad_params)
        return (totals, (outputs[0].astype(jnp.bfloat16), outputs[1].astype(jnp.bfloat16), outputs[2].astype(jnp.bfloat16), grad_first, grad_second, grad_third))
    zero_tree = jax.tree.map(jnp.zeros_like, params)
    totals, stacked = lax.scan(group_step, zero_tree, group_inputs)
    return (stacked[0].reshape(TOK_A, D), stacked[1].reshape(TOK_B, D), stacked[2].reshape(TOK_C, D), stacked[3].reshape(TOK_A, D), stacked[4].reshape(TOK_B, D), stacked[5].reshape(TOK_C, D), totals[0], totals[1], totals[2], totals[3], totals[4], totals[5], totals[6], totals[7], totals[8], totals[9], totals[10], totals[11], totals[12])
```

```python
from functools import partial

import jax
import jax.numpy as jnp
import numpy as np
from jax import lax
from jax.sharding import PartitionSpec as P

HD = 64
LC = 512
LA = 128
LB = 256
LAYERS = 2
D = 768

EPSILON = 1e-05
MASKED_SCORE = -1e30
AXES = ("wide", "head")
f32 = jnp.float32
bf16 = jnp.bfloat16


class Links:
    def __init__(self, n_wide, n_head):
        self.nx, self.nc = 2, 2
        self.nz, self.ny = n_wide // 2, n_head // 2
        self.n_head = n_head
        self.n_wide = n_wide
        self.digits = []
        stride, left = 1, self.nz
        while left > 1:
            count = 4 if left % 4 == 0 else 2 if left % 2 == 0 else left
            self.digits.append((stride, count))
            stride, left = stride * count, left // count

    def number(self, z, x, y, c):
        return ((z * self.nx + x) * self.ny + y) * self.nc + c

    def places(self):
        wide, head = lax.axis_index("wide"), lax.axis_index("head")
        return wide // self.nx, wide % self.nx, head // self.nc, head % self.nc

    def grid(self):
        return np.ndindex(self.nz, self.nx, self.ny, self.nc)

    def take(self, v, z=0, x=0, y=0, c=0):
        pairs = [
            (
                self.number(
                    (i + z) % self.nz, (j + x) % self.nx, (k + y) % self.ny, (m + c) % self.nc
                ),
                self.number(i, j, k, m),
            )
            for i, j, k, m in self.grid()
        ]
        return lax.ppermute(v, AXES, pairs)

    def give(self, v, z=0, x=0, y=0, c=0):
        return self.take(v, -z, -x, -y, -c)

    def take_bit(self, v, bit):
        pairs = [
            (self.number(i ^ bit, j, k, m), self.number(i, j, k, m)) for i, j, k, m in self.grid()
        ]
        return lax.ppermute(v, AXES, pairs)

    def total(self, v):
        v = v + self.take(v, x=1)
        v = v + self.take(v, y=1)
        bit = 1
        while bit < self.nz:
            v = v + self.take_bit(v, bit)
            bit = bit * 2
        return 0.5 * (v + self.take(v, c=1))

    def spread_z(self, v):
        v = v[None]
        for stride, count in self.digits:
            v = jnp.concatenate([v] + [self.take(v, z=stride * k) for k in range(1, count)], axis=0)
        return v

    def gather_z(self, v):
        for stride, count in reversed(self.digits):
            parts = v.reshape(count, v.shape[0] // count, *v.shape[1:])
            total = parts[0].astype(f32)
            for k in range(1, count):
                total = total + self.give(parts[k], z=stride * k).astype(f32)
            v = total if stride == 1 else total.astype(bf16)
        return v.reshape(v.shape[1:])

    def spread(self, v):
        half = v.shape[0] // 2
        zs = self.spread_z(v)
        a, b = zs[:, :half], zs[:, half:]
        a = jnp.stack([a, self.take(a, x=1)])
        b = jnp.stack([b, self.take(b, y=1)])
        return [a, self.take(a, y=1), b, self.take(b, x=1)]

    def fold(self, own, other, **step):
        return (own.astype(f32) + self.give(other, **step).astype(f32)).astype(bf16)

    def collect(self, blocks):
        a = self.fold(blocks[0], blocks[1], y=1)
        b = self.fold(blocks[2], blocks[3], x=1)
        a = self.fold(a[0], a[1], x=1)
        b = self.fold(b[0], b[1], y=1)
        return jnp.concatenate([self.gather_z(a), self.gather_z(b)], axis=0)

    def spread_one(self, v):
        v = self.spread_z(v)
        v = jnp.stack([v, self.take(v, x=1)])
        return jnp.stack([v, self.take(v, y=1)])

    def collect_one(self, v):
        v = self.fold(v[0], v[1], y=1)
        v = self.fold(v[0], v[1], x=1)
        return self.gather_z(v)

    def collect_wide(self, v, z, x):
        v = v.reshape(self.nz, self.nx, *v.shape[1:])
        own = lax.dynamic_index_in_dim(v, x, 1, keepdims=False)
        other = lax.dynamic_index_in_dim(v, 1 - x, 1, keepdims=False)
        v = self.fold(own, other, x=1)
        v = lax.dynamic_slice_in_dim(jnp.concatenate([v, v], axis=0), z, self.nz, axis=0)
        return self.gather_z(v)


def normalize(token_rows, gain_row, shift_row):
    middle = jnp.mean(token_rows, axis=-1, keepdims=True)
    centred = token_rows - middle
    spread = jnp.mean(centred * centred, axis=-1, keepdims=True)
    return centred * lax.rsqrt(spread + EPSILON) * gain_row + shift_row


def score_parts(level_index, head_block, span_len, item_lengths, head_weights):
    first, first_bias, second, second_bias, random_scores, value_weight = head_weights
    item_count = head_block.shape[0] // span_len
    head_grid = head_block.reshape(item_count, span_len, first.shape[0], HD)
    if level_index == 0:
        pre_act = (
            jnp.einsum("ilhd,hde->ilhe", head_grid, first, preferred_element_type=jnp.float32)
            + first_bias[None, None]
        )
        activated = jax.nn.gelu(pre_act).astype(jnp.bfloat16)
        raw_scores = (
            jnp.einsum(
                "ilhe,hej->ihlj",
                activated,
                second[:, :, :span_len],
                preferred_element_type=jnp.float32,
            )
            + second_bias[None, :, None, :span_len]
        )
    else:
        pre_act = None
        activated = None
        raw_scores = random_scores[None, :, :span_len, :span_len].astype(jnp.float32)
    key_mask = (jnp.arange(span_len)[None, :] < item_lengths[:, None])[:, None, None, :]
    masked = jnp.where(key_mask, raw_scores, MASKED_SCORE)
    highest = jnp.max(masked, axis=-1, keepdims=True)
    expanded = jnp.exp(masked - highest)
    softened = expanded / jnp.sum(expanded, axis=-1, keepdims=True)
    values_low = jnp.einsum(
        "ilhd,hde->ilhe", head_grid, value_weight[level_index], preferred_element_type=jnp.float32
    ).astype(jnp.bfloat16)
    return (head_grid, pre_act, activated, softened, values_low)


def synth_forward(level_index, head_block, span_len, item_lengths, head_weights):
    head_grid, pre_act, activated, softened, values_low = score_parts(
        level_index, head_block, span_len, item_lengths, head_weights
    )
    mixed = jnp.einsum(
        "ihlj,ijhe->ilhe",
        softened.astype(jnp.bfloat16),
        values_low,
        preferred_element_type=jnp.float32,
    )
    return mixed.astype(jnp.bfloat16).reshape(head_block.shape[0], -1)


def synth_backward(level_index, head_block, d_mixed, span_len, item_lengths, head_weights):
    first, first_bias, second, second_bias, random_scores, value_weight = head_weights
    head_grid, pre_act, activated, softened, values_low = score_parts(
        level_index, head_block, span_len, item_lengths, head_weights
    )
    d_grid_out = d_mixed.reshape(head_grid.shape)
    d_soft = jnp.einsum(
        "ilhe,ijhe->ihlj", d_grid_out, values_low, preferred_element_type=jnp.float32
    )
    d_values = jnp.einsum(
        "ihlj,ilhe->ijhe",
        softened.astype(jnp.bfloat16),
        d_grid_out,
        preferred_element_type=jnp.float32,
    ).astype(jnp.bfloat16)
    d_scores = softened * (d_soft - jnp.sum(softened * d_soft, axis=-1, keepdims=True))
    grad_value = jnp.einsum(
        "ilhd,ilhe->hde", head_grid, d_values, preferred_element_type=jnp.float32
    )
    d_grid = jnp.einsum(
        "ilhe,hde->ilhd", d_values, value_weight[level_index], preferred_element_type=jnp.float32
    )
    pad_cols = second.shape[2] - span_len
    if level_index == 0:
        d_scores_low = d_scores.astype(jnp.bfloat16)
        grad_second_bias = jnp.pad(
            jnp.einsum("ihlj->hj", d_scores_low, preferred_element_type=jnp.float32),
            ((0, 0), (0, pad_cols)),
        )
        grad_second = jnp.pad(
            jnp.einsum(
                "ilhe,ihlj->hej", activated, d_scores_low, preferred_element_type=jnp.float32
            ),
            ((0, 0), (0, 0), (0, pad_cols)),
        )
        d_activated = jnp.einsum(
            "ihlj,hej->ilhe",
            d_scores_low,
            second[:, :, :span_len],
            preferred_element_type=jnp.float32,
        )
        d_pre = jax.vjp(jax.nn.gelu, pre_act)[1](d_activated)[0].astype(jnp.bfloat16)
        grad_first_bias = jnp.einsum("ilhe->he", d_pre, preferred_element_type=jnp.float32)
        grad_first = jnp.einsum(
            "ilhd,ilhe->hde", head_grid, d_pre, preferred_element_type=jnp.float32
        )
        d_grid = d_grid + jnp.einsum(
            "ilhe,hde->ilhd", d_pre, first, preferred_element_type=jnp.float32
        )
        dense_grads = (grad_first, grad_first_bias, grad_second, grad_second_bias)
        return (d_grid.astype(jnp.bfloat16).reshape(head_block.shape), dense_grads, grad_value)
    grad_random = jnp.pad(jnp.sum(d_scores, axis=0), ((0, 0), (0, pad_cols), (0, pad_cols)))
    return (d_grid.astype(jnp.bfloat16).reshape(head_block.shape), grad_random, grad_value)


def per_device(
    links,
    tokens_a,
    tokens_b,
    tokens_c,
    lengths_a,
    lengths_b,
    lengths_c,
    cotan_a,
    cotan_b,
    cotan_c,
    ln_gain,
    ln_bias,
    row_bias,
    out_weight,
    up_weight,
    up_bias,
    down_weight,
    synth_first,
    synth_first_bias,
    synth_second,
    synth_second_bias,
    random_scores,
    value_weight,
):
    spans = (LA, LB, LC)
    bucket_lengths = (lengths_a, lengths_b, lengths_c)
    counts = [tokens_a.shape[0], tokens_b.shape[0], tokens_c.shape[0]]
    starts = [0, counts[0], counts[0] + counts[1]]
    rows = sum(counts)
    head_weights = (
        synth_first,
        synth_first_bias,
        synth_second,
        synth_second_bias,
        random_scores,
        value_weight,
    )
    z, x, y, c = links.places()
    nz = links.nz
    cols = synth_first.shape[0] * HD
    own_block = links.nc * y + c
    far_block = links.nc * (1 - y) + c

    own_rows = jnp.concatenate([tokens_a, tokens_b, tokens_c, cotan_a, cotan_b, cotan_c], axis=0)
    peer_rows = links.take(own_rows, c=1)
    both = jnp.where(
        c == 0, jnp.stack([own_rows, peer_rows]), jnp.stack([peer_rows, own_rows])
    )
    token_rows = both[:, :rows].reshape(2 * rows, D).astype(f32)
    grad_rows = both[:, rows:].reshape(2 * rows, D).astype(f32)

    out_rows, ff_rows = out_weight.shape[1], up_weight.shape[1]
    half_ff = ff_rows // 2
    misc_rows = -(-(out_rows + 1) // 16) * 16

    def misc_pack(level):
        high = up_bias[level].astype(bf16)
        low = (up_bias[level] - high.astype(f32)).astype(bf16)
        line = jnp.pad(jnp.concatenate([high, low])[None], ((0, 0), (0, D - 2 * ff_rows)))
        return jnp.pad(
            jnp.concatenate([out_weight[level], line], axis=0),
            ((0, misc_rows - out_rows - 1), (0, 0)),
        )

    def chip_numbers(core):
        iy = (y + jnp.arange(2)) % 2
        ix = (x + jnp.arange(2)) % 2
        iz = (z + jnp.arange(nz)) % nz
        device = links.number(
            iz[None, None, :], ix[None, :, None], iy[:, None, None], core
        )
        return (device[..., None] * out_rows + jnp.arange(out_rows)).reshape(-1)

    row_numbers = jnp.concatenate([chip_numbers(c), chip_numbers(1 - c)])
    wanted = jnp.concatenate(
        [own_block * cols + jnp.arange(cols), far_block * cols + jnp.arange(cols)]
    )
    pick_rows = (wanted[:, None] == row_numbers[None, :]).astype(bf16)
    pick_cols = (jnp.arange(D)[:, None] == wanted[None, :]).astype(bf16)

    weights = []
    for level in range(LAYERS):
        misc = links.spread_one(misc_pack(level))
        up_blocks = links.spread(up_weight[level])
        down_blocks = links.spread(down_weight[level])
        w_own = misc[:, :, :, :out_rows].reshape(-1, D)
        w_peer = links.take(w_own, c=1)
        w_out = jnp.dot(
            pick_rows, jnp.concatenate([w_own, w_peer]), preferred_element_type=f32
        ).astype(bf16)
        lines = misc[:, :, :, out_rows, : 2 * ff_rows].astype(f32)
        bias = lines[..., :ff_rows] + lines[..., ff_rows:]
        bias_blocks = [
            bias[0, :, :, :half_ff],
            bias[1, :, :, :half_ff],
            bias[:, 0, :, half_ff:],
            bias[:, 1, :, half_ff:],
        ]
        weights.append(
            (
                w_out,
                [w.reshape(-1, D) for w in up_blocks],
                [b.reshape(-1) for b in bias_blocks],
                [w.reshape(-1, D) for w in down_blocks],
            )
        )

    def to_heads(own, far):
        got = links.take(far, y=1)
        whole = jnp.where(y == 0, jnp.stack([own, got]), jnp.stack([got, own]))
        whole = whole.reshape(2, 2, rows, cols)
        return [
            whole[:, :, s : s + n].reshape(4 * n, cols) for s, n in zip(starts, counts)
        ]

    def to_tokens(parts):
        whole = jnp.concatenate(
            [p.reshape(2, 2, n, cols) for p, n in zip(parts, counts)], axis=2
        ).reshape(2, 2 * rows, cols)
        own = lax.dynamic_index_in_dim(whole, y, 0, keepdims=False)
        far = lax.dynamic_index_in_dim(whole, 1 - y, 0, keepdims=False)
        return own, links.take(far, y=1)

    def core_sum(part):
        return part + links.take(part.astype(bf16), c=1).astype(f32)

    stored = []
    for level in range(LAYERS):
        w_out, up_blocks, bias_blocks, down_blocks = weights[level]
        normed = normalize(token_rows, ln_gain[level, 0], ln_bias[level, 0]).astype(bf16)
        picked = jnp.dot(normed, pick_cols, preferred_element_type=f32).astype(bf16)
        head_parts = to_heads(picked[:, :cols], picked[:, cols:])
        mixed_parts = [
            synth_forward(level, head_parts[k], spans[k], bucket_lengths[k], head_weights)
            for k in range(3)
        ]
        mixed = jnp.concatenate(to_tokens(mixed_parts), axis=1)
        joined = core_sum(jnp.dot(mixed, w_out, preferred_element_type=f32)) + row_bias[level, 0]
        resid = token_rows + joined
        normed2 = normalize(resid, ln_gain[level, 1], ln_bias[level, 1]).astype(bf16)
        pre_blocks = [
            jnp.einsum("rd,fd->rf", normed2, w, preferred_element_type=f32) + b
            for w, b in zip(up_blocks, bias_blocks)
        ]
        hidden_blocks = [jax.nn.gelu(p).astype(bf16) for p in pre_blocks]
        ffn = sum(
            jnp.dot(h, w, preferred_element_type=f32) for h, w in zip(hidden_blocks, down_blocks)
        )
        stored.append((token_rows, head_parts, mixed, resid, normed2, pre_blocks, hidden_blocks))
        token_rows = resid + core_sum(ffn) + row_bias[level, 1]

    def own_parts(whole):
        mine = lax.dynamic_index_in_dim(whole.reshape(2, rows, D), c, 0, keepdims=False)
        return [mine[s : s + n] for s, n in zip(starts, counts)]

    out_parts = own_parts(token_rows.astype(bf16))

    stats = [None] * LAYERS
    out_grads, up_grads, bias_grads, down_grads = [], [], [], []
    head_grads = [None] * LAYERS
    for level in (1, 0):
        w_out, up_blocks, bias_blocks, down_blocks = weights[level]
        rows_in, head_parts, mixed, resid, normed2, pre_blocks, hidden_blocks = stored[level]
        d_ffn = grad_rows.astype(bf16)
        ffn_bias_grad = jnp.sum(d_ffn.astype(f32), axis=0)
        down_terms, up_terms, bias_terms = [], [], []
        d_normed2 = None
        for w_up, w_down, pre, hidden in zip(up_blocks, down_blocks, pre_blocks, hidden_blocks):
            shape = (2, nz, half_ff, D)
            down_terms.append(
                jnp.einsum("rf,rd->fd", hidden, d_ffn, preferred_element_type=f32)
                .astype(bf16)
                .reshape(shape)
            )
            d_hidden = jnp.einsum("rd,fd->rf", d_ffn, w_down, preferred_element_type=f32)
            d_pre = jax.vjp(jax.nn.gelu, pre)[1](d_hidden)[0].astype(bf16)
            bias_terms.append(jnp.sum(d_pre.astype(f32), axis=0).reshape(2, nz, half_ff))
            up_terms.append(
                jnp.einsum("rf,rd->fd", d_pre, normed2, preferred_element_type=f32)
                .astype(bf16)
                .reshape(shape)
            )
            term = jnp.dot(d_pre, w_up, preferred_element_type=f32)
            d_normed2 = term if d_normed2 is None else d_normed2 + term
        d_normed2 = core_sum(d_normed2)
        down_grads.insert(0, links.collect(down_terms))
        up_grads.insert(0, links.collect(up_terms))
        norm_pull = jax.vjp(normalize, resid, ln_gain[level, 1], ln_bias[level, 1])[1]
        d_resid_norm, gain_second, shift_second = norm_pull(d_normed2)
        d_resid = grad_rows + d_resid_norm
        d_join = d_resid.astype(bf16)
        join_bias_grad = jnp.sum(d_join.astype(f32), axis=0)
        d_mixed = jnp.einsum("re,de->rd", d_join, w_out, preferred_element_type=f32).astype(bf16)
        d_parts = to_heads(d_mixed[:, :cols], d_mixed[:, cols:])

        grad_out = jnp.einsum("rd,re->de", mixed, d_join, preferred_element_type=f32).astype(bf16)
        grad_out = jnp.einsum("wk,wd->kd", pick_rows, grad_out, preferred_element_type=f32)
        grad_out = grad_out.astype(bf16)
        near, far = grad_out[: grad_out.shape[0] // 2], grad_out[grad_out.shape[0] // 2 :]
        near = near + links.give(far, c=1)
        first = jnp.stack([bias_terms[0], bias_terms[1]])
        second = jnp.stack([bias_terms[2], bias_terms[3]], axis=1)
        line = jnp.pad(
            jnp.concatenate([first, second], axis=-1).astype(bf16)[..., None, :],
            ((0, 0),) * 4 + ((0, D - ff_rows),),
        )
        misc = jnp.concatenate([near.reshape(2, 2, nz, out_rows, D), line], axis=3)
        misc = jnp.pad(misc, ((0, 0),) * 3 + ((0, misc_rows - out_rows - 1), (0, 0)))
        misc = links.collect_one(misc)
        out_grads.insert(0, misc[:out_rows])
        bias_grads.insert(0, misc[out_rows, :ff_rows])

        d_head_parts = []
        totals = None
        for k in range(3):
            d_block, level_grads, grad_value = synth_backward(
                level, head_parts[k], d_parts[k], spans[k], bucket_lengths[k], head_weights
            )
            d_head_parts.append(d_block)
            found = (level_grads, grad_value)
            totals = found if totals is None else jax.tree.map(jnp.add, totals, found)
        n_wide = links.n_wide

        def by_wide(v, dim):
            shape = v.shape
            v = v.reshape(*shape[:dim], n_wide, shape[dim] // n_wide, *shape[dim + 1 :])
            return jnp.moveaxis(v, dim, 0).reshape(n_wide, -1)

        if level == 1:
            parts = [by_wide(totals[0], 1), by_wide(totals[1], 1)]
        else:
            parts = [by_wide(v, 1) for v in (*totals[0], totals[1])]
        widths = [p.shape[1] for p in parts]
        padded = -(-sum(widths) // LC) * LC
        packed = jnp.pad(
            jnp.concatenate(parts, axis=1).astype(bf16), ((0, 0), (0, padded - sum(widths)))
        ).reshape(n_wide, -1, LC)
        summed = links.collect_wide(packed, z, x).reshape(-1)
        head_grads[level] = [
            summed[sum(widths[:k]) : sum(widths[: k + 1])] for k in range(len(widths))
        ]

        own, far = to_tokens(d_head_parts)
        ours = jnp.concatenate([own, far], axis=1)
        theirs = links.take(ours, c=1)
        other_cols = jnp.concatenate(
            [
                (links.nc * y + 1 - c) * cols + jnp.arange(cols),
                (links.nc * (1 - y) + 1 - c) * cols + jnp.arange(cols),
            ]
        )
        places = jnp.concatenate([wanted, other_cols])
        place_cols = (places[:, None] == jnp.arange(D)[None, :]).astype(bf16)
        d_normed = jnp.dot(
            jnp.concatenate([ours, theirs], axis=1), place_cols, preferred_element_type=f32
        )
        norm_pull = jax.vjp(normalize, rows_in, ln_gain[level, 0], ln_bias[level, 0])[1]
        d_rows_norm, gain_first, shift_first = norm_pull(d_normed)
        grad_rows = d_resid + d_rows_norm
        stats[level] = jnp.stack(
            [gain_first, gain_second, shift_first, shift_second, join_bias_grad, ffn_bias_grad]
        )
    summed = links.total(jnp.stack(stats))
    grad_parts = own_parts(grad_rows)
    heads = synth_first.shape[0]
    first, first_bias, second, second_bias, value_low = head_grads[0]
    random, value_high = head_grads[1]
    return (
        *out_parts,
        *grad_parts,
        summed[:, 0:2],
        summed[:, 2:4],
        summed[:, 4:6],
        jnp.stack(out_grads),
        jnp.stack(up_grads),
        jnp.stack(bias_grads),
        jnp.stack(down_grads),
        first.reshape(heads, -1, HD),
        first_bias.reshape(heads, -1),
        second.reshape(heads, -1, LC),
        second_bias.reshape(heads, -1),
        random.reshape(heads, -1, LC),
        jnp.stack([value_low.reshape(heads, -1, HD), value_high.reshape(heads, -1, HD)]),
    )


def solution(mesh):
    placed = (
        P(("wide", "head"), None),
        P(("wide", "head"), None),
        P(("wide", "head"), None),
        P("wide"),
        P("wide"),
        P("wide"),
        P(("wide", "head"), None),
        P(("wide", "head"), None),
        P(("wide", "head"), None),
        P(),
        P(),
        P(),
        P(None, ("wide", "head"), None),
        P(None, ("wide", "head"), None),
        P(None, ("wide", "head")),
        P(None, ("wide", "head"), None),
        P("head", None, None),
        P("head", None),
        P("head", None, None),
        P("head", None),
        P("head", None, None),
        P(None, "head", None, None),
    )
    return jax.shard_map(
        partial(per_device, Links(mesh.shape["wide"], mesh.shape["head"])),
        mesh=mesh,
        in_specs=placed,
        out_specs=(
            P(("wide", "head"), None),
            P(("wide", "head"), None),
            P(("wide", "head"), None),
            P(("wide", "head"), None),
            P(("wide", "head"), None),
            P(("wide", "head"), None),
            P(),
            P(),
            P(),
            P(None, ("wide", "head"), None),
            P(None, ("wide", "head"), None),
            P(None, ("wide", "head")),
            P(None, ("wide", "head"), None),
            P("head", "wide", None),
            P("head", "wide"),
            P("head", "wide", None),
            P("head", "wide"),
            P("head", "wide", None),
            P(None, "head", "wide", None),
        ),
        check_vma=False,
    )
```

```python
import math
from functools import partial

import jax
import jax.numpy as jnp
import numpy as np
from jax import lax
from jax.experimental import pallas as pl
from jax.experimental.pallas import tpu as pltpu
from jax.sharding import PartitionSpec as P

HD = 64
LC = 512
LA = 128
LB = 256
LAYERS = 2
D = 768

EPSILON = 1e-05
MASKED_SCORE = -1e30
AXES = ("wide", "head")
ROW_TILE = 112
SCORE_TILE = 256
VMEM_LIMIT = 56 * 1024 * 1024
f32 = jnp.float32
bf16 = jnp.bfloat16


class Links:
    def __init__(self, n_wide, n_head):
        self.nx, self.nc = 2, 2
        self.nz, self.ny = n_wide // 2, n_head // 2
        self.n_head = n_head
        self.n_wide = n_wide
        self.digits = []
        stride, left = 1, self.nz
        while left > 1:
            count = 4 if left % 4 == 0 else 2 if left % 2 == 0 else left
            self.digits.append((stride, count))
            stride, left = stride * count, left // count

    def number(self, z, x, y, c):
        return ((z * self.nx + x) * self.ny + y) * self.nc + c

    def places(self):
        wide, head = lax.axis_index("wide"), lax.axis_index("head")
        return wide // self.nx, wide % self.nx, head // self.nc, head % self.nc

    def grid(self):
        return np.ndindex(self.nz, self.nx, self.ny, self.nc)

    def take(self, v, z=0, x=0, y=0, c=0):
        pairs = [
            (
                self.number(
                    (i + z) % self.nz, (j + x) % self.nx, (k + y) % self.ny, (m + c) % self.nc
                ),
                self.number(i, j, k, m),
            )
            for i, j, k, m in self.grid()
        ]
        return lax.ppermute(v, AXES, pairs)

    def give(self, v, z=0, x=0, y=0, c=0):
        return self.take(v, -z, -x, -y, -c)

    def take_bit(self, v, bit):
        pairs = [
            (self.number(i ^ bit, j, k, m), self.number(i, j, k, m)) for i, j, k, m in self.grid()
        ]
        return lax.ppermute(v, AXES, pairs)

    def total(self, v):
        v = v + self.take(v, x=1)
        v = v + self.take(v, y=1)
        bit = 1
        while bit < self.nz:
            v = v + self.take_bit(v, bit)
            bit = bit * 2
        return 0.5 * (v + self.take(v, c=1))

    def spread_z(self, v):
        v = v[None]
        for stride, count in self.digits:
            v = jnp.concatenate([v] + [self.take(v, z=stride * k) for k in range(1, count)], axis=0)
        return v

    def gather_z(self, v):
        for stride, count in reversed(self.digits):
            parts = v.reshape(count, v.shape[0] // count, *v.shape[1:])
            total = parts[0].astype(f32)
            for k in range(1, count):
                total = total + self.give(parts[k], z=stride * k).astype(f32)
            v = total if stride == 1 else total.astype(bf16)
        return v.reshape(v.shape[1:])

    def spread(self, v):
        half = v.shape[0] // 2
        zs = self.spread_z(v)
        a, b = zs[:, :half], zs[:, half:]
        a = jnp.stack([a, self.take(a, x=1)])
        b = jnp.stack([b, self.take(b, y=1)])
        return [a, self.take(a, y=1), b, self.take(b, x=1)]

    def fold(self, own, other, **step):
        return (own.astype(f32) + self.give(other, **step).astype(f32)).astype(bf16)

    def collect(self, blocks):
        a = self.fold(blocks[0], blocks[1], y=1)
        b = self.fold(blocks[2], blocks[3], x=1)
        a = self.fold(a[0], a[1], x=1)
        b = self.fold(b[0], b[1], y=1)
        return jnp.concatenate([self.gather_z(a), self.gather_z(b)], axis=0)

    def spread_one(self, v):
        v = self.spread_z(v)
        v = jnp.stack([v, self.take(v, x=1)])
        return jnp.stack([v, self.take(v, y=1)])

    def collect_one(self, v):
        v = self.fold(v[0], v[1], y=1)
        v = self.fold(v[0], v[1], x=1)
        return self.gather_z(v)

    def collect_wide(self, v, z, x):
        v = v.reshape(self.nz, self.nx, *v.shape[1:])
        own = lax.dynamic_index_in_dim(v, x, 1, keepdims=False)
        other = lax.dynamic_index_in_dim(v, 1 - x, 1, keepdims=False)
        v = self.fold(own, other, x=1)
        v = lax.dynamic_slice_in_dim(jnp.concatenate([v, v], axis=0), z, self.nz, axis=0)
        return self.gather_z(v)


def stage(kernel, outs, args, scratch=(), smem=0, flops=0):
    spaces = [pltpu.SMEM] * smem + [pltpu.VMEM] * (len(args) - smem)
    size = sum(a.size * a.dtype.itemsize for a in args[smem:])
    size = size + sum(math.prod(s) * jnp.dtype(d).itemsize for s, d in outs)
    return pl.pallas_call(
        kernel,
        out_shape=[jax.ShapeDtypeStruct(s, d) for s, d in outs],
        in_specs=[pl.BlockSpec(memory_space=s) for s in spaces],
        out_specs=[pl.BlockSpec(memory_space=pltpu.VMEM) for _ in outs],
        scratch_shapes=list(scratch),
        compiler_params=pltpu.CompilerParams(vmem_limit_bytes=VMEM_LIMIT),
        cost_estimate=pl.CostEstimate(flops=flops, bytes_accessed=size, transcendentals=0),
    )(*args)


def mm(a, b):
    return lax.dot_general(a, b, (((1,), (0,)), ((), ())), preferred_element_type=f32)


def mm_nt(a, b):
    return lax.dot_general(a, b, (((1,), (1,)), ((), ())), preferred_element_type=f32)


def mm_tn(a, b):
    return lax.dot_general(a, b, (((0,), (0,)), ((), ())), preferred_element_type=f32)


def tiles(rows):
    return [pl.ds(i, ROW_TILE) for i in range(0, rows, ROW_TILE)]


def centre(v):
    middle = jnp.mean(v, axis=-1, keepdims=True)
    centred = v - middle
    scale = lax.rsqrt(jnp.mean(centred * centred, axis=-1, keepdims=True) + EPSILON)
    return centred * scale, scale


def norm_back(v, gain, d_out):
    unit, scale = centre(v)
    inner = d_out * gain
    flat = jnp.mean(inner, axis=-1, keepdims=True)
    along = jnp.mean(inner * unit, axis=-1, keepdims=True)
    d_rows = scale * (inner - flat - unit * along)
    return d_rows, jnp.sum(d_out * unit, axis=0, keepdims=True), jnp.sum(d_out, 0, keepdims=True)


def gelu_both(v):
    k = math.sqrt(2.0 / math.pi)
    square = v * v
    t = jnp.tanh(k * v * (1.0 + 0.044715 * square))
    half = 0.5 * (1.0 + t)
    slope = half + 0.5 * v * (1.0 - t * t) * (k * (1.0 + 3 * 0.044715 * square))
    return v * half, slope


def first_norm_kernel(tokens, gain, shift, pick, own, far):
    for t in tiles(tokens.shape[0]):
        unit, _ = centre(tokens[t, :].astype(f32))
        normed = (unit * gain[...] + shift[...]).astype(bf16)
        picked = mm(normed, pick[...]).astype(bf16)
        own[t, :] = picked[:, : own.shape[1]]
        far[t, :] = picked[:, own.shape[1] :]


def next_norm_kernel(resid, part, got, bias, gain, shift, pick, rows, own, far):
    for t in tiles(resid.shape[0]):
        v = resid[t, :] + part[t, :].astype(f32) + got[t, :].astype(f32) + bias[...]
        rows[t, :] = v
        unit, _ = centre(v)
        normed = (unit * gain[...] + shift[...]).astype(bf16)
        picked = mm(normed, pick[...]).astype(bf16)
        own[t, :] = picked[:, : own.shape[1]]
        far[t, :] = picked[:, own.shape[1] :]


def join_kernel(near, far, weight, part):
    cols = near.shape[1]
    total = mm(near[...], weight[:cols, :]) + mm(far[...], weight[cols:, :])
    part[...] = total.astype(bf16)


def ffn_kernel(n, rows, part, got, bias, gain, shift, *refs):
    ups, biases, downs = refs[:n], refs[n : 2 * n], refs[2 * n : 3 * n]
    resid, normed, ffn = refs[3 * n : 3 * n + 3]
    hiddens, slopes = refs[3 * n + 3 : 4 * n + 3], refs[4 * n + 3 :]
    for t in tiles(rows.shape[0]):
        v = rows[t, :].astype(f32) + part[t, :].astype(f32) + got[t, :].astype(f32) + bias[...]
        resid[t, :] = v
        unit, _ = centre(v)
        normed[t, :] = (unit * gain[...] + shift[...]).astype(bf16)
    total = None
    for up, b, down, hidden, slope in zip(ups, biases, downs, hiddens, slopes):
        value, grad = gelu_both(mm_nt(normed[...], up[...]) + b[...])
        hidden[...] = value.astype(bf16)
        slope[...] = grad.astype(bf16)
        term = mm(hidden[...], down[...])
        total = term if total is None else total + term
    ffn[...] = total.astype(bf16)


def ffn_back_kernel(n, grad_rows, normed, *refs):
    ups, downs, hiddens, slopes = (refs[i * n : (i + 1) * n] for i in range(4))
    d_normed, bias_grad = refs[4 * n : 4 * n + 2]
    down_grads, up_grads, hidden_bias = (
        refs[4 * n + 2 + i * n : 4 * n + 2 + (i + 1) * n] for i in range(3)
    )
    d_ffn = grad_rows[...].astype(bf16)
    bias_grad[...] = jnp.sum(d_ffn.astype(f32), axis=0, keepdims=True)
    total = None
    for k in range(n):
        d_pre = (mm_nt(d_ffn, downs[k][...]) * slopes[k][...].astype(f32)).astype(bf16)
        down_grads[k][...] = mm_tn(hiddens[k][...], d_ffn).astype(bf16)
        hidden_bias[k][...] = jnp.sum(d_pre.astype(f32), axis=0, keepdims=True)
        up_grads[k][...] = mm_tn(d_pre, normed[...]).astype(bf16)
        term = mm(d_pre, ups[k][...])
        total = term if total is None else total + term
    d_normed[...] = total.astype(bf16)


def join_back_kernel(
    grad_rows, part, got, resid, gain, weight, near, far, pick,
    d_resid, d_near, d_far, gain_grad, shift_grad, bias_grad, out_near, out_far, d_join,
):
    gain_grad[...] = jnp.zeros_like(gain_grad)
    shift_grad[...] = jnp.zeros_like(shift_grad)
    bias_grad[...] = jnp.zeros_like(bias_grad)
    for t in tiles(resid.shape[0]):
        d_out = part[t, :].astype(f32) + got[t, :].astype(f32)
        d_rows, d_gain, d_shift = norm_back(resid[t, :], gain[...], d_out)
        gain_grad[...] += d_gain
        shift_grad[...] += d_shift
        d_rows = d_rows + grad_rows[t, :].astype(f32)
        d_resid[t, :] = d_rows
        low = d_rows.astype(bf16)
        d_join[t, :] = low
        bias_grad[...] += jnp.sum(low.astype(f32), axis=0, keepdims=True)
    cols = near.shape[1]
    d_near[...] = mm_nt(d_join[...], weight[:cols, :]).astype(bf16)
    d_far[...] = mm_nt(d_join[...], weight[cols:, :]).astype(bf16)
    grad = mm_tn(pick[:cols, :], mm_tn(near[...], d_join[...]).astype(bf16))
    grad = grad + mm_tn(pick[cols:, :], mm_tn(far[...], d_join[...]).astype(bf16))
    half = out_near.shape[0]
    out_near[...] = grad[:half].astype(bf16)
    out_far[...] = grad[half:].astype(bf16)


def rows_back_kernel(
    d_resid, near, far, peer_near, peer_far, place, rows, gain, grad_rows, gain_grad, shift_grad
):
    cols = near.shape[1]
    gain_grad[...] = jnp.zeros_like(gain_grad)
    shift_grad[...] = jnp.zeros_like(shift_grad)
    for t in tiles(rows.shape[0]):
        d_out = mm(near[t, :], place[:cols, :]) + mm(far[t, :], place[cols : 2 * cols, :])
        d_out = d_out + mm(peer_near[t, :], place[2 * cols : 3 * cols, :])
        d_out = d_out + mm(peer_far[t, :], place[3 * cols :, :])
        d_rows, d_gain, d_shift = norm_back(rows[t, :].astype(f32), gain[...], d_out)
        gain_grad[...] += d_gain
        shift_grad[...] += d_shift
        grad_rows[t, :] = d_resid[t, :] + d_rows


def group_pieces(counts):
    total = sum(counts)
    start = 0
    found = []
    for bucket, n in enumerate(counts):
        for chip in range(2):
            for core in range(2):
                found.append((bucket, chip, core * total + start, (2 * chip + core) * n, n))
        start = start + n
    return found


def load_groups(counts, y, near, far, whole, buckets):
    whole[y] = near[...]
    whole[1 - y] = far[...]
    for bucket, chip, source, target, n in group_pieces(counts):
        buckets[bucket][target : target + n, :] = whole[chip, source : source + n, :]


def store_groups(counts, y, buckets, whole, near, far):
    for bucket, chip, source, target, n in group_pieces(counts):
        whole[chip, source : source + n, :] = buckets[bucket][target : target + n, :]
    near[...] = whole[y]
    far[...] = whole[1 - y]


def head_lanes(shape, h):
    return lax.broadcasted_iota(jnp.int32, shape, 1) // HD == h


def only_head(v, h):
    return jnp.where(head_lanes(v.shape, h), v, jnp.zeros_like(v))


def soft(level, h, act, length, span, second, second_bias, random, tile):
    if level == 0:
        scores = mm(only_head(act, h), second[:, :span]) + second_bias[h : h + 1, :span]
    else:
        scores = random[h, tile, :span].astype(f32)
    keys = lax.broadcasted_iota(jnp.int32, scores.shape, 1) < length
    scores = jnp.where(keys, scores, MASKED_SCORE)
    e = jnp.exp(scores - jnp.max(scores, axis=-1, keepdims=True))
    return e * (1.0 / jnp.sum(e, axis=-1, keepdims=True))


def score_tiles(span):
    size = min(span, SCORE_TILE)
    return [pl.ds(i, size) for i in range(0, span, size)]


def synth_kernel(level, counts, scalars, near, far, first, first_bias, second, second_bias,
                 random, value, mixed_near, mixed_far, whole, rows_a, rows_b, rows_c,
                 mixed_a, mixed_b, mixed_c):
    y = scalars[0]
    rows, mixed = (rows_a, rows_b, rows_c), (mixed_a, mixed_b, mixed_c)
    heads = near.shape[1] // HD
    load_groups(counts, y, near, far, whole, rows)
    for k, span in enumerate((LA, LB, LC)):
        values = mm(rows[k][...], value[...]).astype(bf16)
        by_head = [only_head(values, h) for h in range(heads)]
        for t in score_tiles(span):
            act = None
            if level == 0:
                act = gelu_both(mm(rows[k][t, :], first[...]) + first_bias[...])[0].astype(bf16)
            total = None
            for h in range(heads):
                p = soft(level, h, act, scalars[1 + k], span, second, second_bias, random, t)
                term = mm(p.astype(bf16), by_head[h])
                total = term if total is None else total + term
            mixed[k][t, :] = total.astype(bf16)
    store_groups(counts, y, mixed, whole, mixed_near, mixed_far)


def synth_back_kernel(level, counts, scalars, near, far, d_near, d_far, first, first_bias, second,
                      second_bias, random, value, *refs):
    y = scalars[0]
    if level == 0:
        (dx_near, dx_far, value_grad, second_grad, second_bias_grad, first_grad, first_bias_grad,
         *scratch) = refs
        sums = (value_grad, second_grad, second_bias_grad, first_grad, first_bias_grad)
    else:
        dx_near, dx_far, value_grad, random_out, *scratch = refs
        *scratch, random_grad = scratch
        sums = (value_grad, random_grad)
    whole, dx, *rest = scratch
    rows, d_mixed = rest[:3], rest[3:6]
    d_values = rest[6]
    heads = near.shape[1] // HD
    load_groups(counts, y, near, far, whole, rows)
    load_groups(counts, y, d_near, d_far, whole, d_mixed)
    for s in sums:
        s[...] = jnp.zeros_like(s)
    for k, span in enumerate((LA, LB, LC)):
        values = mm(rows[k][...], value[...]).astype(bf16)
        d_values[:span, :] = jnp.zeros((span, heads * HD), f32)
        for t in score_tiles(span):
            x = rows[k][t, :]
            act = None
            if level == 0:
                act, slope = gelu_both(mm(x, first[...]) + first_bias[...])
                act = act.astype(bf16)
                d_act = None
            dm = d_mixed[k][t, :]
            for h in range(heads):
                p = soft(level, h, act, scalars[1 + k], span, second, second_bias, random, t)
                dm_h = only_head(dm, h)
                dp = mm_nt(dm_h, values)
                d_values[:span, :] += mm_tn(p.astype(bf16), dm_h)
                ds = p * (dp - jnp.sum(p * dp, axis=-1, keepdims=True))
                if level == 0:
                    low = ds.astype(bf16)
                    second_bias_grad[h : h + 1, :span] += jnp.sum(
                        low.astype(f32), axis=0, keepdims=True
                    )
                    second_grad[:, :span] += mm_tn(only_head(act, h), low)
                    term = only_head(mm_nt(low, second[:, :span]), h)
                    d_act = term if d_act is None else d_act + term
                else:
                    random_grad[h, t, :span] += ds
            if level == 0:
                d_pre = (d_act * slope).astype(bf16)
                first_bias_grad[...] += jnp.sum(d_pre.astype(f32), axis=0, keepdims=True)
                first_grad[...] += mm_tn(x, d_pre)
                dx[t, :] = mm_nt(d_pre, first[...])
        d_low = d_values[:span, :].astype(bf16)
        value_grad[...] += mm_tn(rows[k][...], d_low)
        back = mm_nt(d_low, value[...])
        if level == 0:
            back = back + dx[:span, :]
        d_mixed[k][...] = back.astype(bf16)
    store_groups(counts, y, d_mixed, whole, dx_near, dx_far)
    if level == 1:
        random_out[...] = random_grad[...].astype(bf16)


def per_device(
    links,
    tokens_a,
    tokens_b,
    tokens_c,
    lengths_a,
    lengths_b,
    lengths_c,
    cotan_a,
    cotan_b,
    cotan_c,
    ln_gain,
    ln_bias,
    row_bias,
    out_weight,
    up_weight,
    up_bias,
    down_weight,
    synth_first,
    synth_first_bias,
    synth_second,
    synth_second_bias,
    random_scores,
    value_weight,
):
    counts = (tokens_a.shape[0], tokens_b.shape[0], tokens_c.shape[0])
    starts = (0, counts[0], counts[0] + counts[1])
    rows = sum(counts)
    heads = synth_first.shape[0]
    z, x, y, c = links.places()
    nz = links.nz
    n_wide = links.n_wide
    cols = heads * HD
    own_block = links.nc * y + c
    far_block = links.nc * (1 - y) + c
    scalars = jnp.stack([y, lengths_a[0], lengths_b[0], lengths_c[0]]).astype(jnp.int32)

    own_rows = jnp.concatenate([tokens_a, tokens_b, tokens_c, cotan_a, cotan_b, cotan_c], axis=0)
    peer_rows = links.take(own_rows, c=1)
    both = jnp.where(c == 0, jnp.stack([own_rows, peer_rows]), jnp.stack([peer_rows, own_rows]))
    token_rows = both[:, :rows].reshape(2 * rows, D)
    cotan_rows = both[:, rows:].reshape(2 * rows, D)

    def block_lines(block):
        return block * cols + jnp.arange(cols)

    wanted = jnp.concatenate([block_lines(own_block), block_lines(far_block)])
    their_cols = jnp.concatenate(
        [block_lines(links.nc * y + 1 - c), block_lines(links.nc * (1 - y) + 1 - c)]
    )
    out_rows, ff_rows = out_weight.shape[1], up_weight.shape[1]

    def chip_numbers(core):
        iy = (y + jnp.arange(2)) % 2
        ix = (x + jnp.arange(2)) % 2
        iz = (z + jnp.arange(nz)) % nz
        device = links.number(iz[None, None, :], ix[None, :, None], iy[:, None, None], core)
        return (device[..., None] * out_rows + jnp.arange(out_rows)).reshape(-1)

    row_numbers = jnp.concatenate([chip_numbers(c), chip_numbers(1 - c)])
    pick_rows = (wanted[:, None] == row_numbers[None, :]).astype(bf16)
    pick_cols = (jnp.arange(D)[:, None] == wanted[None, :]).astype(bf16)
    places = jnp.concatenate([wanted, their_cols])
    place_cols = (places[:, None] == jnp.arange(D)[None, :]).astype(bf16)

    half_ff = ff_rows // 2
    misc_rows = -(-(out_rows + 1) // 16) * 16

    def misc_pack(level):
        high = up_bias[level].astype(bf16)
        low = (up_bias[level] - high.astype(f32)).astype(bf16)
        line = jnp.pad(jnp.concatenate([high, low])[None], ((0, 0), (0, D - 2 * ff_rows)))
        return jnp.pad(
            jnp.concatenate([out_weight[level], line], axis=0),
            ((0, misc_rows - out_rows - 1), (0, 0)),
        )

    weights = []
    for level in range(LAYERS):
        misc = links.spread_one(misc_pack(level))
        up_blocks = links.spread(up_weight[level])
        down_blocks = links.spread(down_weight[level])
        w_own = misc[:, :, :, :out_rows].reshape(-1, D)
        w_peer = links.take(w_own, c=1)
        w_out = jnp.dot(
            pick_rows, jnp.concatenate([w_own, w_peer]), preferred_element_type=f32
        ).astype(bf16)
        lines = misc[:, :, :, out_rows, : 2 * ff_rows].astype(f32)
        bias = lines[..., :ff_rows] + lines[..., ff_rows:]
        bias_blocks = [
            bias[0, :, :, :half_ff],
            bias[1, :, :, :half_ff],
            bias[:, 0, :, half_ff:],
            bias[:, 1, :, half_ff:],
        ]
        weights.append(
            (
                w_out,
                [w.reshape(-1, D) for w in up_blocks],
                [b.reshape(1, -1) for b in bias_blocks],
                [w.reshape(-1, D) for w in down_blocks],
            )
        )

    same_head = (jnp.arange(cols)[:, None] // HD) == (jnp.arange(cols)[None, :] // HD)

    def diagonal(w):
        return jnp.where(same_head, jnp.tile(w.reshape(cols, HD), (1, heads)), 0).astype(bf16)

    first = diagonal(synth_first)
    first_bias = synth_first_bias.reshape(1, cols)
    second = synth_second.reshape(cols, LC)
    values = [diagonal(value_weight[level]) for level in range(LAYERS)]
    head_weights = [
        (first, first_bias, second, synth_second_bias, first_bias, values[0]),
        (first_bias, first_bias, first_bias, first_bias, random_scores, values[1]),
    ]

    def line(v, level, which):
        return v[level, which][None]

    n = 4
    chip_rows = 2 * rows
    ffn_cols = [w.shape[0] for w in weights[0][1]]
    row_low = ((chip_rows, D), bf16)
    row_high = ((chip_rows, D), f32)
    head_low = ((chip_rows, cols), bf16)
    vector = ((1, D), f32)
    groups = [pltpu.VMEM((4 * k, cols), bf16) for k in counts]
    group_pair = pltpu.VMEM((2, chip_rows, cols), bf16)

    stored = []
    for level in range(LAYERS):
        w_out, up_blocks, bias_blocks, down_blocks = weights[level]
        gain, shift = line(ln_gain, level, 0), line(ln_bias, level, 0)
        if level == 0:
            rows_in = token_rows
            own, far = stage(
                first_norm_kernel, [head_low] * 2, (token_rows, gain, shift, pick_cols)
            )
        else:
            rows_in, own, far = stage(
                next_norm_kernel,
                [row_high, head_low, head_low],
                (resid, ffn, ffn_got, line(row_bias, level - 1, 1), gain, shift, pick_cols),
            )
        got = links.take(far, y=1)
        mixed_own, mixed_far = stage(
            partial(synth_kernel, level, counts),
            [head_low] * 2,
            (scalars, own, got, *head_weights[level]),
            scratch=[group_pair, *groups, *groups],
            smem=1,
        )
        mixed_got = links.take(mixed_far, y=1)
        (part,) = stage(join_kernel, [row_low], (mixed_own, mixed_got, w_out))
        part_got = links.take(part, c=1)
        resid, normed2, ffn, *saved = stage(
            partial(ffn_kernel, n),
            [row_high, row_low, row_low] + [((chip_rows, k), bf16) for k in ffn_cols] * 2,
            (
                rows_in,
                part,
                part_got,
                line(row_bias, level, 0),
                line(ln_gain, level, 1),
                line(ln_bias, level, 1),
                *up_blocks,
                *bias_blocks,
                *down_blocks,
            ),
        )
        ffn_got = links.take(ffn, c=1)
        stored.append((rows_in, own, got, mixed_own, mixed_got, resid, normed2, saved))

    def own_half(whole):
        return lax.dynamic_index_in_dim(whole.reshape(2, rows, D), c, 0, keepdims=False)

    def buckets(mine):
        return [mine[s : s + k] for s, k in zip(starts, counts)]

    last = own_half(resid) + own_half(ffn).astype(f32) + own_half(ffn_got).astype(f32)
    out_parts = buckets((last + row_bias[LAYERS - 1, 1]).astype(bf16))

    stats = [None] * LAYERS
    out_grads, up_grads, bias_grads, down_grads = [], [], [], []
    head_grads = [None] * LAYERS
    grad_rows = cotan_rows
    for level in (1, 0):
        w_out, up_blocks, bias_blocks, down_blocks = weights[level]
        rows_in, own, got, mixed_own, mixed_got, resid, normed2, saved = stored[level]
        d_normed2, ffn_bias_grad, *terms = stage(
            partial(ffn_back_kernel, n),
            [row_low, vector]
            + [((k, D), bf16) for k in ffn_cols] * 2
            + [((1, k), f32) for k in ffn_cols],
            (grad_rows, normed2, *up_blocks, *down_blocks, *saved),
        )
        d_got = links.take(d_normed2, c=1)
        shape = (2, nz, half_ff, D)
        down_grads.insert(0, links.collect([t.reshape(shape) for t in terms[:n]]))
        up_grads.insert(0, links.collect([t.reshape(shape) for t in terms[n : 2 * n]]))
        bias_terms = [t.reshape(2, nz, half_ff) for t in terms[2 * n :]]
        (
            d_resid,
            d_own,
            d_far,
            gain_second,
            shift_second,
            join_bias_grad,
            out_near,
            out_peer,
        ) = stage(
            join_back_kernel,
            [row_high, head_low, head_low, vector, vector, vector]
            + [((D // 2, D), bf16)] * 2,
            (
                grad_rows,
                d_normed2,
                d_got,
                resid,
                line(ln_gain, level, 1),
                w_out,
                mixed_own,
                mixed_got,
                pick_rows,
            ),
            scratch=[pltpu.VMEM((chip_rows, D), bf16)],
        )
        d_mixed_got = links.take(d_far, y=1)

        near = out_near + links.give(out_peer, c=1)
        first_terms = jnp.stack([bias_terms[0], bias_terms[1]])
        second_terms = jnp.stack([bias_terms[2], bias_terms[3]], axis=1)
        bias_line = jnp.pad(
            jnp.concatenate([first_terms, second_terms], axis=-1).astype(bf16)[..., None, :],
            ((0, 0),) * 4 + ((0, D - ff_rows),),
        )
        misc = jnp.concatenate([near.reshape(2, 2, nz, out_rows, D), bias_line], axis=3)
        misc = jnp.pad(misc, ((0, 0),) * 3 + ((0, misc_rows - out_rows - 1), (0, 0)))
        misc = links.collect_one(misc)
        out_grads.insert(0, misc[:out_rows])
        bias_grads.insert(0, misc[out_rows, :ff_rows])

        square = ((cols, cols), f32)
        scratch = [group_pair, pltpu.VMEM((LC, cols), f32), *groups, *groups]
        scratch = scratch + [pltpu.VMEM((LC, cols), f32)]
        if level == 0:
            outs = [square, ((cols, LC), f32), ((heads, LC), f32), square, ((1, cols), f32)]
        else:
            outs = [square, ((heads, LC, LC), bf16)]
            scratch = scratch + [pltpu.VMEM((heads, LC, LC), f32)]
        dx_own, dx_far, *found = stage(
            partial(synth_back_kernel, level, counts),
            [head_low] * 2 + outs,
            (scalars, own, got, d_own, d_mixed_got, *head_weights[level]),
            scratch=scratch,
            smem=1,
        )
        dx_peer = links.take(dx_own, c=1)
        dx_got = links.take(dx_far, y=1)
        dx_peer_got = links.take(dx_got, c=1)
        head_grads[level] = found
        grad_rows, gain_first, shift_first = stage(
            rows_back_kernel,
            [row_high, vector, vector],
            (
                d_resid,
                dx_own,
                dx_got,
                dx_peer,
                dx_peer_got,
                place_cols,
                rows_in,
                line(ln_gain, level, 0),
            ),
        )
        stats[level] = jnp.concatenate(
            [gain_first, gain_second, shift_first, shift_second, join_bias_grad, ffn_bias_grad]
        )

    def blocks(v):
        kept = jnp.where(same_head, v, 0).reshape(cols, heads, HD)
        return jnp.sum(kept, axis=1)

    def by_wide(v):
        return jnp.moveaxis(v.reshape(heads, n_wide, -1, v.shape[-1]), 1, 0)

    value_high, random = head_grads[1]
    random = by_wide(random.reshape(cols * LC // HD, LC)).reshape(n_wide, -1, LC)
    random = links.collect_wide(random, z, x)
    value_low, second_grad, second_bias_grad, first_grad, first_bias_grad = head_grads[0]
    bias_lines = second_bias_grad.reshape(heads, n_wide, 1, -1)
    bias_lines = jnp.pad(
        bias_lines,
        ((0, 0), (0, 0), (0, HD // n_wide - 1), (0, LC - bias_lines.shape[-1])),
    ).reshape(cols, LC)
    pack = jnp.concatenate(
        [
            second_grad,
            bias_lines,
            blocks(first_grad),
            blocks(value_low),
            blocks(value_high),
            first_bias_grad.reshape(cols, 1),
        ],
        axis=1,
    ).astype(bf16)
    pack = jnp.pad(pack, ((0, 0), (0, -pack.shape[1] % 128)))
    pack = by_wide(pack).reshape(n_wide, cols // n_wide, -1)
    pack = links.collect_wide(pack, z, x).reshape(heads, HD // n_wide, -1)
    at = 2 * LC

    summed = links.total(jnp.stack(stats))
    return (
        *out_parts,
        *buckets(own_half(grad_rows)),
        summed[:, 0:2],
        summed[:, 2:4],
        summed[:, 4:6],
        jnp.stack(out_grads),
        jnp.stack(up_grads),
        jnp.stack(bias_grads),
        jnp.stack(down_grads),
        pack[:, :, at : at + HD],
        pack[:, :, at + 3 * HD],
        pack[:, :, :LC],
        pack[:, 0, LC : LC + LC // n_wide],
        random.reshape(heads, -1, LC),
        jnp.stack(
            [pack[:, :, at + HD : at + 2 * HD], pack[:, :, at + 2 * HD : at + 3 * HD]]
        ),
    )


def solution(mesh):
    placed = (
        P(("wide", "head"), None),
        P(("wide", "head"), None),
        P(("wide", "head"), None),
        P("wide"),
        P("wide"),
        P("wide"),
        P(("wide", "head"), None),
        P(("wide", "head"), None),
        P(("wide", "head"), None),
        P(),
        P(),
        P(),
        P(None, ("wide", "head"), None),
        P(None, ("wide", "head"), None),
        P(None, ("wide", "head")),
        P(None, ("wide", "head"), None),
        P("head", None, None),
        P("head", None),
        P("head", None, None),
        P("head", None),
        P("head", None, None),
        P(None, "head", None, None),
    )
    return jax.shard_map(
        partial(per_device, Links(mesh.shape["wide"], mesh.shape["head"])),
        mesh=mesh,
        in_specs=placed,
        out_specs=(
            P(("wide", "head"), None),
            P(("wide", "head"), None),
            P(("wide", "head"), None),
            P(("wide", "head"), None),
            P(("wide", "head"), None),
            P(("wide", "head"), None),
            P(),
            P(),
            P(),
            P(None, ("wide", "head"), None),
            P(None, ("wide", "head"), None),
            P(None, ("wide", "head")),
            P(None, ("wide", "head"), None),
            P("head", "wide", None),
            P("head", "wide"),
            P("head", "wide", None),
            P("head", "wide"),
            P("head", "wide", None),
            P(None, "head", "wide", None),
        ),
        check_vma=False,
    )
```

```python
import math
from functools import partial

import jax
import jax.numpy as jnp
import numpy as np
from jax import lax
from jax.experimental import pallas as pl
from jax.experimental.pallas import tpu as pltpu
from jax.sharding import PartitionSpec as P

HD = 64
LC = 512
LA = 128
LB = 256
LAYERS = 2
D = 768

EPSILON = 1e-05
MASKED_SCORE = -1e30
AXES = ("wide", "head")
ROW_TILE = 112
SCORE_TILE = 256
SPARE = 12 * 1024 * 1024
FLOPS_PER_US = 1.1e9
SPACE_US = 8.0
f32 = jnp.float32
bf16 = jnp.bfloat16


class Links:
    def __init__(self, n_wide, n_head):
        self.nx, self.nc = 2, 2
        self.nz, self.ny = n_wide // 2, n_head // 2
        self.n_wide = n_wide
        self.bits = [1 << k for k in range(self.nz.bit_length() - 1)]

    def number(self, z, x, y, c):
        return ((z * self.nx + x) * self.ny + y) * self.nc + c

    def places(self):
        wide, head = lax.axis_index("wide"), lax.axis_index("head")
        return wide // self.nx, wide % self.nx, head // self.nc, head % self.nc

    def swap(self, v, z=0, x=0, y=0, c=0):
        pairs = [
            (self.number(i ^ z, j ^ x, k ^ y, m ^ c), self.number(i, j, k, m))
            for i, j, k, m in np.ndindex(self.nz, self.nx, self.ny, self.nc)
        ]
        return lax.ppermute(v, AXES, pairs)

    def total(self, v, *waits):
        steps = [{"z": bit} for bit in self.bits] + [{"x": 1}, {"y": 1}]
        for k, step in enumerate(steps):
            got = self.swap(v, **step)
            if k + len(waits) >= len(steps):
                got = after(got, waits[k + len(waits) - len(steps)])
            v = v + got
        return v


def nothing_kernel(*refs):
    pass


def after(v, *others):
    return pl.pallas_call(
        nothing_kernel,
        out_shape=jax.ShapeDtypeStruct(v.shape, v.dtype),
        in_specs=[pl.BlockSpec(memory_space=pl.ANY)] * (1 + len(others)),
        out_specs=pl.BlockSpec(memory_space=pl.ANY),
        input_output_aliases={0: 0},
        compiler_params=pltpu.CompilerParams(vmem_limit_bytes=1 << 20),
        cost_estimate=pl.CostEstimate(flops=1, bytes_accessed=0, transcendentals=0),
    )(v, *others)


class Spread:
    def __init__(self, links, v):
        self.links, self.v = links, v

    def start_z(self, *wait):
        for bit in self.links.bits[1:-1]:
            self.v = jnp.concatenate([self.v, self.links.swap(self.v, z=bit)], axis=0)
        v = after(self.v, *wait) if wait else self.v
        self.got = self.links.swap(v, z=self.links.bits[-1])

    def end_z(self, cuts, *wait):
        n = self.v.shape[0]
        plans = []
        for a, b, rows in cuts:
            for start in (a, b):
                plans.append(((2 * n, rows), [(0, start, rows, 0, 0), (1, start, rows, n, 0)]))
        halves = assemble([self.v, self.got], plans, wait)
        return [Near(self.links, a, b) for a, b in zip(halves[::2], halves[1::2])]


class Near:
    def __init__(self, links, a, b):
        self.links, self.a, self.b = links, a, b

    def start_near(self, *wait):
        a, b = (after(v, *wait) if wait else v for v in (self.a, self.b))
        self.got_a, self.got_b = self.links.swap(a, x=1), self.links.swap(b, y=1)

    def start_far(self, *wait):
        n, rows = self.a.shape[:2]
        wait = (*wait, space(self.a))
        plan = [
            ((2 * n, rows), [(k, 0, rows, 0, 0), (k + 1, 0, rows, n, 0)]) for k in (0, 2)
        ]
        self.a, self.b = assemble([self.a, self.got_a, self.b, self.got_b], plan, wait)
        self.far_a, self.far_b = self.links.swap(self.a, y=1), self.links.swap(self.b, x=1)

    def blocks(self):
        return [self.a, self.far_a, self.b, self.far_b]


def fold_first(own, got, *wait):
    out = ((own.shape[0] // 2, *own.shape[1:]), bf16)
    return stage(1.0, fold_first_kernel, [out, out], (own, got), wait=wait)


class Fold:
    def __init__(self, links, pairs, *wait):
        self.links = links
        flat = [v for pair in pairs for v in pair]
        n = links.nz if links.nz <= 4 else 2
        rows = sum(own.shape[1] for own, _ in pairs)
        shape = (links.nz // n, rows, flat[0].shape[2])
        self.keep, *self.sends = stage(
            1.0,
            partial(fold_second_kernel, n),
            [(shape, f32)] + [(shape, bf16)] * (n - 1),
            flat,
            wait=wait,
        )
        self.bits = list(reversed(links.bits))[1:] if n == 2 else []

    def start(self, *wait, chain=False):
        sends = [after(v, *wait) if wait else v for v in self.sends]
        if len(sends) == 1:
            self.gots = [self.links.swap(sends[0], z=self.links.nz // 2)]
        else:
            self.gots = []
            for k, v in enumerate(sends):
                v = after(v, self.gots[0]) if chain and k > 0 else v
                self.gots.append(self.links.swap(v, z=k + 1))

    def steps(self):
        keep, gots = self.keep, self.gots
        for bit in self.bits:
            shape = (bit, *keep.shape[1:])
            send, keep = stage(
                1.0, fold_z_kernel, [(shape, bf16), (shape, f32)], (keep, *gots)
            )
            gots = [self.links.swap(send, z=bit)]
        return keep, gots

    def finish(self, *wait):
        keep, gots = self.steps()
        (total,) = stage(
            1.0, fold_last_kernel, [(keep.shape, f32)], (keep, *gots), wait=wait
        )
        return total[0]


def stage(us, kernel, outs, args, scratch=(), smem=0, wait=()):
    count = len(args)
    spaces = [pltpu.SMEM] * smem + [pltpu.VMEM] * (count - smem) + [pl.ANY] * len(wait)
    size = sum(a.size * a.dtype.itemsize for a in args[smem:])
    size = size + sum(math.prod(s) * jnp.dtype(d).itemsize for s, d in outs)
    held = sum(math.prod(s.shape) * jnp.dtype(s.dtype).itemsize for s in scratch)

    def body(*refs):
        kernel(*refs[:count], *refs[count + len(wait) :])

    return pl.pallas_call(
        body,
        out_shape=[jax.ShapeDtypeStruct(s, d) for s, d in outs],
        in_specs=[pl.BlockSpec(memory_space=s) for s in spaces],
        out_specs=[pl.BlockSpec(memory_space=pltpu.VMEM) for _ in outs],
        scratch_shapes=list(scratch),
        compiler_params=pltpu.CompilerParams(vmem_limit_bytes=size + held + SPARE),
        cost_estimate=pl.CostEstimate(
            flops=int(us * FLOPS_PER_US), bytes_accessed=0, transcendentals=0
        ),
    )(*args, *wait)


def space_kernel(out):
    out[...] = jnp.zeros_like(out)


def space(*deps):
    return stage(SPACE_US, space_kernel, [((8, 128), f32)], (), wait=deps)[0]


def mm(a, b):
    return lax.dot_general(a, b, (((1,), (0,)), ((), ())), preferred_element_type=f32)


def mm_nt(a, b):
    return lax.dot_general(a, b, (((1,), (1,)), ((), ())), preferred_element_type=f32)


def mm_tn(a, b):
    return lax.dot_general(a, b, (((0,), (0,)), ((), ())), preferred_element_type=f32)


def one_hot(mask):
    return mask.astype(f32).astype(bf16)


def tiles(rows):
    return [pl.ds(i, ROW_TILE) for i in range(0, rows, ROW_TILE)]


def centre(v):
    middle = jnp.mean(v, axis=-1, keepdims=True)
    centred = v - middle
    scale = lax.rsqrt(jnp.mean(centred * centred, axis=-1, keepdims=True) + EPSILON)
    return centred * scale, scale


def norm_back(v, gain, d_out):
    unit, scale = centre(v)
    inner = d_out * gain
    flat = jnp.mean(inner, axis=-1, keepdims=True)
    along = jnp.mean(inner * unit, axis=-1, keepdims=True)
    d_rows = scale * (inner - flat - unit * along)
    return d_rows, jnp.sum(d_out * unit, axis=0, keepdims=True), jnp.sum(d_out, 0, keepdims=True)


def gelu_both(v):
    k = math.sqrt(2.0 / math.pi)
    square = v * v
    t = jnp.tanh(k * v * (1.0 + 0.044715 * square))
    half = 0.5 * (1.0 + t)
    slope = half + 0.5 * v * (1.0 - t * t) * (k * (1.0 + 3 * 0.044715 * square))
    return v * half, slope


def move(moves, sems):
    copies = [pltpu.make_async_copy(a, b, sems.at[i]) for i, (a, b) in enumerate(moves)]
    for copy in copies:
        copy.start()
    for copy in copies:
        copy.wait()


def pack_rows_kernel(*refs):
    *parts, rows, sems = refs
    moves, start = [], 0
    for ref in parts:
        moves.append((ref, rows.at[pl.ds(start, ref.shape[0])]))
        start = start + ref.shape[0]
    move(moves, sems)


def pack_weights_kernel(size, misc, up, down, first, rest, sems):
    lead = misc.shape[2]
    wide, narrow = lead + size, size
    half = wide + 2 * narrow
    moves = []
    for side in range(2):
        part = pl.ds(side * size, size)
        moves.append((misc.at[0, side], first.at[pl.ds(side * wide, lead)]))
        moves.append((up.at[0, part], first.at[pl.ds(side * wide + lead, size)]))
        at = side * half
        moves.append((misc.at[1, side], rest.at[pl.ds(at, lead)]))
        moves.append((down.at[0, part], rest.at[pl.ds(at + lead, size)]))
        moves.append((up.at[1, part], rest.at[pl.ds(at + wide, size)]))
        moves.append((down.at[1, part], rest.at[pl.ds(at + wide + narrow, size)]))
    move(moves, sems)


def lay_out(kernel, outs, args, copies):
    return pl.pallas_call(
        kernel,
        out_shape=[jax.ShapeDtypeStruct((k, D), bf16) for k in outs],
        in_specs=[pl.BlockSpec(memory_space=pltpu.HBM)] * len(args),
        out_specs=[pl.BlockSpec(memory_space=pltpu.VMEM)] * len(outs),
        scratch_shapes=[pltpu.SemaphoreType.DMA((copies,))],
        compiler_params=pltpu.CompilerParams(vmem_limit_bytes=SPARE),
    )(*args)


def assemble_kernel(plans, n, *refs):
    for out, pieces in zip(refs[n:], plans):
        for source, start, rows, place, row in pieces:
            piece = refs[source][:, start : start + rows, :]
            out[place : place + piece.shape[0], row : row + rows, :] = piece


def assemble(sources, outs, wait=()):
    whole = all(
        start % 16 == 0 and rows % 16 == 0 and row % 16 == 0
        for _, pieces in outs
        for _, start, rows, _, row in pieces
    )
    if whole:
        plans = [pieces for _, pieces in outs]
        shapes = [((*shape, D), bf16) for shape, _ in outs]
        return stage(
            0.7, partial(assemble_kernel, plans, len(sources)), shapes, sources, wait=wait
        )
    found = []
    for shape, pieces in outs:
        columns = {}
        for source, start, rows, place, row in sorted(pieces, key=lambda p: (p[4], p[3])):
            columns.setdefault(row, []).append(sources[source][:, start : start + rows])
        columns = [jnp.concatenate(v, axis=0) for _, v in sorted(columns.items())]
        found.append(jnp.concatenate(columns, axis=1))
    return found


def first_norm_kernel(scalars, mine, peer, gain, shift, pick, tokens, cotans, own, far):
    c = scalars[4]
    rows, cols = mine.shape[0] // 2, own.shape[1]
    for ref, core in ((mine, c), (peer, 1 - c)):
        for i in range(0, rows, ROW_TILE):
            t = pl.ds(pl.multiple_of(core * rows + i, 16), ROW_TILE)
            v = ref[i : i + ROW_TILE, :]
            tokens[t, :] = v
            cotans[t, :] = ref[rows + i : rows + i + ROW_TILE, :]
            unit, _ = centre(v.astype(f32))
            normed = (unit * gain[...] + shift[...]).astype(bf16)
            picked = mm(normed, pick[...]).astype(bf16)
            own[t, :] = picked[:, :cols]
            far[t, :] = picked[:, cols:]


def next_norm_kernel(resid, part, got, bias, gain, shift, pick, rows, own, far):
    for t in tiles(resid.shape[0]):
        v = resid[t, :] + (part[t, :].astype(f32) + got[t, :].astype(f32)) + bias[...]
        rows[t, :] = v
        unit, _ = centre(v)
        normed = (unit * gain[...] + shift[...]).astype(bf16)
        picked = mm(normed, pick[...]).astype(bf16)
        own[t, :] = picked[:, : own.shape[1]]
        far[t, :] = picked[:, own.shape[1] :]


def pick_kernel(at, size, mine_pick, their_pick, *refs):
    blocks, (mine, theirs) = refs[:-2], refs[-2:]
    for pick, out in ((mine_pick, mine), (their_pick, theirs)):
        total = None
        for k, ref in enumerate(blocks):
            lines = block(ref, at, size)
            n = lines.shape[0]
            term = mm(pick[:, k * n : (k + 1) * n], lines)
            total = term if total is None else total + term
        out[...] = total.astype(bf16)


def join_kernel(near, far, mine, got, part, weight):
    cols = near.shape[1]
    weight[...] = (mine[...].astype(f32) + got[...].astype(f32)).astype(bf16)
    total = mm(near[...], weight[:cols, :]) + mm(far[...], weight[cols:, :])
    part[...] = total.astype(bf16)


def block(ref, start, rows):
    if start is None:
        return ref[...]
    return ref[:, start : start + rows, :].reshape(-1, D)


def line_mask(shape, lead, line, size):
    row = lax.broadcasted_iota(jnp.int32, shape, 0)
    unit = lax.broadcasted_iota(jnp.int32, shape, 1)
    return (row % lead == line) & (row // lead == unit // size)


def ffn_up_kernel(n, at, misc_at, size, lead, line, rows, part, got, bias, gain, shift, *refs):
    ups, miscs = refs[:n], refs[n : 2 * n]
    resid, normed, hidden, slope = refs[2 * n :]
    for t in tiles(rows.shape[0]):
        v = rows[t, :].astype(f32) + (part[t, :].astype(f32) + got[t, :].astype(f32)) + bias[...]
        resid[t, :] = v
        unit, _ = centre(v)
        normed[t, :] = (unit * gain[...] + shift[...]).astype(bf16)
    units = hidden.shape[2]
    lane = lax.broadcasted_iota(jnp.int32, (128, units), 0)
    column = lax.broadcasted_iota(jnp.int32, (128, units), 1)
    place = ((lane % size == column % size) & (lane < 2 * size)).astype(f32).astype(bf16)
    for k in range(n):
        lines = mm(block(miscs[k], misc_at, lead)[:, :128], place)
        lines = jnp.where(line_mask(lines.shape, lead, line, size), lines, 0.0)
        lines = jnp.sum(lines, axis=0, keepdims=True)
        value, grad = gelu_both(mm_nt(normed[...], block(ups[k], at, size)) + lines)
        hidden[k] = value.astype(bf16)
        slope[k] = grad.astype(bf16)


def ffn_down_kernel(n, at, size, hidden, *refs):
    downs, ffn = refs[:n], refs[n]
    total = None
    for k in range(n):
        term = mm(hidden[k], block(downs[k], at, size))
        total = term if total is None else total + term
    ffn[...] = total.astype(bf16)


def ffn_back_kernel(n, up_at, down_at, size, grad_rows, normed, hidden, slope, *refs):
    ups, downs = refs[:n], refs[n : 2 * n]
    d_normed, bias_grad, hidden_bias = refs[2 * n : 2 * n + 3]
    grads = refs[2 * n + 3 :]
    d_ffn = grad_rows[...].astype(bf16)
    bias_grad[...] = jnp.sum(d_ffn.astype(f32), axis=0, keepdims=True)
    total = None
    for k in range(n):
        d_hidden = mm_nt(d_ffn, block(downs[k], down_at, size))
        d_pre = (d_hidden * slope[k].astype(f32)).astype(bf16)
        hidden_bias[k : k + 1, :] = jnp.sum(d_pre.astype(f32), axis=0, keepdims=True)
        down_grad = mm_tn(hidden[k], d_ffn).astype(bf16)
        up_grad = mm_tn(d_pre, normed[...]).astype(bf16)
        if up_at is None:
            grads[k][0] = down_grad
            grads[k][1] = up_grad
        else:
            grads[k][:, :size, :] = down_grad.reshape(-1, size, D)
            grads[k][:, size:, :] = up_grad.reshape(-1, size, D)
        term = mm(d_pre, block(ups[k], up_at, size))
        total = term if total is None else total + term
    d_normed[...] = total.astype(bf16)


def fold_first_kernel(own, got, send, keep):
    n = send.shape[0]
    for out, half in ((keep, slice(0, n)), (send, slice(n, 2 * n))):
        out[...] = (own[half].astype(f32) + got[half].astype(f32)).astype(bf16)


def misc_kernel(first, first_got, second, second_got, *refs):
    n = len(refs) // 2
    for k, (source, out) in enumerate(zip(refs[:n], refs[n:])):
        chips, start = source.shape[:2]
        lead = (out.shape[1] - start) // 2
        out[:, :start, :] = source[...]
        part = slice(k * chips * lead, (k + 1) * chips * lead)
        for i, (own, got) in enumerate(((first, first_got), (second, second_got))):
            at = start + i * lead
            total = own[part, :].astype(f32) + got[part, :].astype(f32)
            out[:, at : at + lead, :] = total.astype(bf16).reshape(chips, lead, D)


def fold_second_kernel(n, *refs):
    count = len(refs) - n
    keep, sends = refs[count], refs[count + 1 :]
    start = 0
    for i in range(count // 2):
        own, got = refs[2 * i], refs[2 * i + 1]
        lines, rows = own.shape[0] // n, slice(start, start + own.shape[1])
        start = start + own.shape[1]
        for k in range(n):
            part = slice(k * lines, (k + 1) * lines)
            total = own[part].astype(f32) + got[part].astype(f32)
            if k == 0:
                keep[:, rows, :] = total
            else:
                sends[k - 1][:, rows, :] = total.astype(bf16)


def fold_z_kernel(own, got, send, keep):
    n = send.shape[0]
    keep[...] = own[:n] + got[:n].astype(f32)
    send[...] = (own[n:] + got[n:].astype(f32)).astype(bf16)


def fold_last_kernel(own, *refs):
    *gots, out = refs
    total = own[...]
    for got in gots:
        total = total + got[...].astype(f32)
    out[...] = total


def finish_kernel(size, lead, first, second, *refs):
    n = (len(refs) - 3) // 2
    first_gots, second_gots, (down, up, misc) = refs[:n], refs[n : 2 * n], refs[2 * n :]
    for level, (own, gots) in enumerate(((first, first_gots), (second, second_gots))):
        total = own[0]
        for got in gots:
            total = total + got[0].astype(f32)
        each = total.shape[0] // 2
        for side in range(2):
            at, part = side * each, slice(side * size, (side + 1) * size)
            down[level, part, :] = total[at : at + size]
            up[level, part, :] = total[at + size : at + 2 * size]
            if level == 0:
                for i in range(2):
                    start = at + 2 * size + i * lead
                    misc[i, side] = total[start : start + lead]


def last_kernel(counts, scalars, resid, part, got, bias, *outs):
    start = scalars[4] * sum(counts)
    for out, n in zip(outs, counts):
        t = pl.ds(pl.multiple_of(start, 16), n)
        v = resid[t, :] + (part[t, :].astype(f32) + got[t, :].astype(f32)) + bias[...]
        out[...] = v.astype(bf16)
        start = start + n


def rows_last_kernel(counts, scalars, *refs):
    *given, grad_a, grad_b, grad_c, gain_grad, shift_grad, rows = refs
    rows_back_kernel(*given, rows, gain_grad, shift_grad)
    start = scalars[4] * sum(counts)
    for out, n in zip((grad_a, grad_b, grad_c), counts):
        out[...] = rows[pl.ds(pl.multiple_of(start, 16), n), :]
        start = start + n


def join_back_kernel(
    lead, line, size, grad_rows, part, got, resid, gain, weight, near, far, near_pick, far_pick,
    hidden_bias, d_resid, d_near, d_far, gain_grad, shift_grad, bias_grad, out_near, out_far,
    d_join,
):
    gain_grad[...] = jnp.zeros_like(gain_grad)
    shift_grad[...] = jnp.zeros_like(shift_grad)
    bias_grad[...] = jnp.zeros_like(bias_grad)
    for t in tiles(resid.shape[0]):
        d_out = part[t, :].astype(f32) + got[t, :].astype(f32)
        d_rows, d_gain, d_shift = norm_back(resid[t, :], gain[...], d_out)
        gain_grad[...] += d_gain
        shift_grad[...] += d_shift
        d_rows = d_rows + grad_rows[t, :].astype(f32)
        d_resid[t, :] = d_rows
        low = d_rows.astype(bf16)
        d_join[t, :] = low
        bias_grad[...] += jnp.sum(low.astype(f32), axis=0, keepdims=True)
    cols = near.shape[1]
    d_near[...] = mm_nt(d_join[...], weight[:cols, :]).astype(bf16)
    d_far[...] = mm_nt(d_join[...], weight[cols:, :]).astype(bf16)
    grad_near = mm_tn(near[...], d_join[...]).astype(bf16)
    grad_far = mm_tn(far[...], d_join[...]).astype(bf16)
    for pick, out in ((near_pick, out_near), (far_pick, out_far)):
        total = mm_tn(pick[:cols, :], grad_near) + mm_tn(pick[cols:, :], grad_far)
        out[...] = total.astype(bf16)
    n, units = hidden_bias.shape
    rows = out_near.shape[0] // n
    unit = lax.broadcasted_iota(jnp.int32, (units, 128), 0)
    lane = lax.broadcasted_iota(jnp.int32, (units, 128), 1)
    place = (unit % size == lane).astype(f32).astype(bf16)
    mask = line_mask((rows, units), lead, line, size)
    for k in range(n):
        lines = jnp.where(mask, hidden_bias[k : k + 1, :], 0.0).astype(bf16)
        part_rows = slice(k * rows, (k + 1) * rows)
        lines = mm(lines, place) + out_near[part_rows, :128].astype(f32)
        out_near[part_rows, :128] = lines.astype(bf16)


def rows_back_kernel(
    d_resid, near, far, peer_near, peer_far, place, rows, gain, grad_rows, gain_grad, shift_grad
):
    cols = near.shape[1]
    gain_grad[...] = jnp.zeros_like(gain_grad)
    shift_grad[...] = jnp.zeros_like(shift_grad)
    for t in tiles(rows.shape[0]):
        d_out = mm(near[t, :], place[:cols, :]) + mm(far[t, :], place[cols : 2 * cols, :])
        d_out = d_out + mm(peer_near[t, :], place[2 * cols : 3 * cols, :])
        d_out = d_out + mm(peer_far[t, :], place[3 * cols :, :])
        d_rows, d_gain, d_shift = norm_back(rows[t, :].astype(f32), gain[...], d_out)
        gain_grad[...] += d_gain
        shift_grad[...] += d_shift
        grad_rows[t, :] = d_resid[t, :] + d_rows


def group_pieces(counts):
    total = sum(counts)
    start = 0
    found = []
    for bucket, n in enumerate(counts):
        for chip in range(2):
            for core in range(2):
                found.append((bucket, chip, core * total + start, (2 * chip + core) * n, n))
        start = start + n
    return found


def load_groups(counts, y, near, far, whole, buckets):
    whole[y] = near[...]
    whole[1 - y] = far[...]
    for bucket, chip, source, target, n in group_pieces(counts):
        buckets[bucket][target : target + n, :] = whole[chip, source : source + n, :]


def store_groups(counts, y, buckets, whole, near, far):
    for bucket, chip, source, target, n in group_pieces(counts):
        whole[chip, source : source + n, :] = buckets[bucket][target : target + n, :]
    near[...] = whole[y]
    far[...] = whole[1 - y]


def head_lanes(shape, h):
    return lax.broadcasted_iota(jnp.int32, shape, 1) // HD == h


def only_head(v, h):
    return jnp.where(head_lanes(v.shape, h), v, jnp.zeros_like(v))


def soft(level, h, act, length, span, second, second_bias, random, tile):
    if level == 0:
        scores = mm(only_head(act, h), second[:, :span]) + second_bias[h : h + 1, :span]
    else:
        scores = random[h, tile, :span].astype(f32)
    keys = lax.broadcasted_iota(jnp.int32, scores.shape, 1) < length
    scores = jnp.where(keys, scores, MASKED_SCORE)
    e = jnp.exp(scores - jnp.max(scores, axis=-1, keepdims=True))
    return e * (1.0 / jnp.sum(e, axis=-1, keepdims=True))


def score_tiles(span):
    size = min(span, SCORE_TILE)
    return [pl.ds(i, size) for i in range(0, span, size)]


def diagonal(ref):
    cols = ref.shape[0]
    row = lax.broadcasted_iota(jnp.int32, (HD, cols), 0)
    col = lax.broadcasted_iota(jnp.int32, (HD, cols), 1)
    wide = mm(ref[...], one_hot(col % HD == row))
    row = lax.broadcasted_iota(jnp.int32, (cols, cols), 0)
    col = lax.broadcasted_iota(jnp.int32, (cols, cols), 1)
    return jnp.where(row // HD == col // HD, wide, 0.0).astype(bf16)


def synth_kernel(level, counts, scalars, near, far, first, first_bias, second, second_bias,
                 random, value, mixed_near, mixed_far, whole, rows_a, rows_b, rows_c,
                 mixed_a, mixed_b, mixed_c):
    y = scalars[0]
    rows, mixed = (rows_a, rows_b, rows_c), (mixed_a, mixed_b, mixed_c)
    heads = near.shape[1] // HD
    value = diagonal(value)
    if level == 0:
        first = diagonal(first)
    load_groups(counts, y, near, far, whole, rows)
    for k, span in enumerate((LA, LB, LC)):
        values = mm(rows[k][...], value).astype(bf16)
        by_head = [only_head(values, h) for h in range(heads)]
        for t in score_tiles(span):
            act = None
            if level == 0:
                act = gelu_both(mm(rows[k][t, :], first) + first_bias[...])[0].astype(bf16)
            total = None
            for h in range(heads):
                p = soft(level, h, act, scalars[1 + k], span, second, second_bias, random, t)
                term = mm(p.astype(bf16), by_head[h])
                total = term if total is None else total + term
            mixed[k][t, :] = total.astype(bf16)
    store_groups(counts, y, mixed, whole, mixed_near, mixed_far)


def pack_grads(heads, n_wide, value_high, value_low, second, second_bias, first, first_bias):
    cols = heads * HD

    def grid(shape):
        return [lax.broadcasted_iota(jnp.int32, shape, k) for k in range(2)]

    row, col = grid((cols, cols))
    same = row // HD == col // HD
    source, lane = grid((cols, 128))
    left = one_hot((source % HD == lane) & (lane < HD))
    right = one_hot((source % HD == lane - HD) & (lane >= HD))

    def blocks(v, place):
        return mm(jnp.where(same, v[...], 0.0).astype(bf16), place)

    column = jnp.sum(jnp.where(row == col, first_bias[...], 0.0), axis=1, keepdims=True)
    tail = blocks(value_high, left) + jnp.where(lane == HD, column, 0.0)
    row, col = grid((cols, second_bias.shape[0]))
    lines = mm(one_hot(row // HD == col), second_bias[...].astype(bf16))
    wide = LC // n_wide
    row, col = grid((cols, LC))
    lines = jnp.where(col // wide == (row % HD) // (HD // n_wide), lines, 0.0).astype(bf16)
    source, lane = grid((LC, 128))
    lines = mm(lines, one_hot((source % wide == lane) & (lane < wide)))
    rest = jnp.concatenate(
        [
            (blocks(first, left) + blocks(value_low, right)).astype(bf16),
            tail.astype(bf16),
            lines.astype(bf16),
            jnp.zeros((cols, LC - 3 * 128), bf16),
        ],
        axis=1,
    )
    return second[...].astype(bf16), rest


def wide_rows(shape, heads, z, x):
    n, lines = shape[0], shape[1]
    row = lax.broadcasted_iota(jnp.int32, (n * lines, heads * HD), 0)
    col = lax.broadcasted_iota(jnp.int32, (n * lines, heads * HD), 1)
    per = HD // (2 * n)
    wide = 2 * (z ^ (row // lines)) + x
    i = row % lines
    source = (i // per) * HD + wide * per + i % per
    return one_hot((source == col) & (i < heads * per))


def synth_back_kernel(level, counts, random_parts, scalars, near, far, d_near, d_far, first, first_bias, second,
                      second_bias, random, value, *refs):
    y = scalars[0]
    if level == 0:
        (value_high, dx_near, dx_far, pack_own, pack_other, *scratch) = refs
        *scratch, value_grad, second_grad, second_bias_grad, first_grad, first_bias_grad = scratch
        sums = (value_grad, second_grad, second_bias_grad, first_grad, first_bias_grad)
    else:
        dx_near, dx_far, value_grad, random_outs = *refs[:3], refs[3 : 3 + random_parts]
        *scratch, random_grad = refs[3 + random_parts :]
        sums = (value_grad, random_grad)
    whole, dx, *rest = scratch
    rows, d_mixed = rest[:3], rest[3:6]
    d_values = rest[6]
    heads = near.shape[1] // HD
    value = diagonal(value)
    if level == 0:
        first = diagonal(first)
    load_groups(counts, y, near, far, whole, rows)
    load_groups(counts, y, d_near, d_far, whole, d_mixed)
    for s in sums:
        s[...] = jnp.zeros_like(s)
    for k, span in enumerate((LA, LB, LC)):
        values = mm(rows[k][...], value).astype(bf16)
        d_values[:span, :] = jnp.zeros((span, heads * HD), f32)
        for t in score_tiles(span):
            x = rows[k][t, :]
            act = None
            if level == 0:
                act, slope = gelu_both(mm(x, first) + first_bias[...])
                act = act.astype(bf16)
                d_act = None
            dm = d_mixed[k][t, :]
            for h in range(heads):
                p = soft(level, h, act, scalars[1 + k], span, second, second_bias, random, t)
                dm_h = only_head(dm, h)
                dp = mm_nt(dm_h, values)
                d_values[:span, :] += mm_tn(p.astype(bf16), dm_h)
                ds = p * (dp - jnp.sum(p * dp, axis=-1, keepdims=True))
                if level == 0:
                    low = ds.astype(bf16)
                    second_bias_grad[h : h + 1, :span] += jnp.sum(
                        low.astype(f32), axis=0, keepdims=True
                    )
                    second_grad[:, :span] += mm_tn(only_head(act, h), low)
                    term = only_head(mm_nt(low, second[:, :span]), h)
                    d_act = term if d_act is None else d_act + term
                else:
                    random_grad[h, t, :span] += ds
            if level == 0:
                d_pre = (d_act * slope).astype(bf16)
                first_bias_grad[...] += jnp.sum(d_pre.astype(f32), axis=0, keepdims=True)
                first_grad[...] += mm_tn(x, d_pre)
                dx[t, :] = mm_nt(d_pre, first)
        d_low = d_values[:span, :].astype(bf16)
        value_grad[...] += mm_tn(rows[k][...], d_low)
        back = mm_nt(d_low, value)
        if level == 0:
            back = back + dx[:span, :]
        d_mixed[k][...] = back.astype(bf16)
    store_groups(counts, y, d_mixed, whole, dx_near, dx_far)
    if level == 0:
        packed = pack_grads(
            heads, 2 * pack_own.shape[0], value_high, value_grad, second_grad, second_bias_grad, first_grad,
            first_bias_grad,
        )
        for side, out in enumerate((pack_own, pack_other)):
            half = out.shape[1] // 2
            shape = (out.shape[0], half, LC)
            pick = wide_rows(shape, heads, scalars[6], scalars[5] ^ side)
            for i, part in enumerate(packed):
                picked = mm(pick, part).astype(bf16).reshape(shape)
                out[:, i * half : (i + 1) * half, :] = picked
    if level == 1 and random_parts == 1:
        random_outs[0][...] = random_grad[...].astype(bf16)
    elif level == 1:
        n, lines = random_outs[0].shape[0], random_outs[0].shape[1] // heads
        for side, out in enumerate(random_outs):
            for i in range(n):
                wide = 2 * (scalars[6] ^ i) + (scalars[5] ^ side)
                at = pl.ds(pl.multiple_of(wide * lines, 16), lines)
                for h in range(heads):
                    out[i, h * lines : (h + 1) * lines, :] = random_grad[h, at, :].astype(bf16)


def per_device(
    links,
    tokens_a,
    tokens_b,
    tokens_c,
    lengths_a,
    lengths_b,
    lengths_c,
    cotan_a,
    cotan_b,
    cotan_c,
    ln_gain,
    ln_bias,
    row_bias,
    out_weight,
    up_weight,
    up_bias,
    down_weight,
    synth_first,
    synth_first_bias,
    synth_second,
    synth_second_bias,
    random_scores,
    value_weight,
):
    counts = (tokens_a.shape[0], tokens_b.shape[0], tokens_c.shape[0])
    starts = (0, counts[0], counts[0] + counts[1])
    rows = sum(counts)
    heads = synth_first.shape[0]
    z, x, y, c = links.places()
    nz, n_wide = links.nz, links.n_wide
    chips = 2 * nz
    cols = heads * HD
    out_rows, ff_rows = out_weight.shape[1], up_weight.shape[1]
    size = ff_rows // 2
    units = chips * size
    lead = 16
    half_out = -(-out_rows // 2)
    aligned = size % 16 == 0
    n = 4
    scalars = jnp.stack([y, lengths_a[0], lengths_b[0], lengths_c[0], c, x, z]).astype(jnp.int32)

    def misc_halves(level):
        high = up_bias[level].astype(bf16)
        low = (up_bias[level] - high.astype(f32)).astype(bf16)
        found = []
        for side in range(2):
            w = out_weight[level, side * half_out : (side + 1) * half_out]
            part = slice(side * size, (side + 1) * size)
            line = jnp.pad(jnp.concatenate([high[part], low[part]])[None], ((0, 0), (0, D - ff_rows)))
            w = jnp.pad(w, ((0, half_out - w.shape[0]), (0, 0)))
            found.append(
                jnp.pad(jnp.concatenate([w, line], axis=0), ((0, lead - half_out - 1), (0, 0)))
            )
        return jnp.stack(found)

    misc = jnp.stack([misc_halves(level) for level in range(LAYERS)])
    tokens = (tokens_a, tokens_b, tokens_c, cotan_a, cotan_b, cotan_c)
    wide, half = lead + size, lead + 3 * size
    if aligned:
        (mine,) = lay_out(pack_rows_kernel, [2 * rows], tokens, len(tokens))
        first_rows, rest_rows = lay_out(
            partial(pack_weights_kernel, size),
            [2 * wide, 2 * half],
            (misc, up_weight, down_weight),
            12,
        )
    else:
        mine = jnp.concatenate(tokens, axis=0)
        parts = [slice(0, size), slice(size, 2 * size)]
        first_rows = jnp.concatenate(
            [v for k, p in enumerate(parts) for v in (misc[0, k], up_weight[0, p])]
        )
        rest_rows = jnp.concatenate(
            [
                v
                for k, p in enumerate(parts)
                for v in (misc[1, k], down_weight[0, p], up_weight[1, p], down_weight[1, p])
            ]
        )
    peer = links.swap(mine, c=1)
    first_rows, rest_rows = first_rows[None], rest_rows[None]
    first_got = links.swap(first_rows, z=1)
    rest_got = links.swap(rest_rows, z=1)

    def block_lines(block):
        return block * cols + jnp.arange(cols)

    wanted = jnp.concatenate([block_lines(links.nc * y + c), block_lines(links.nc * (1 - y) + c)])
    their_wanted = jnp.concatenate(
        [block_lines(links.nc * y + 1 - c), block_lines(links.nc * (1 - y) + 1 - c)]
    )

    def misc_numbers(core):
        iz, ix, iy = z ^ jnp.arange(nz), x ^ jnp.arange(2), y ^ jnp.arange(2)
        device = links.number(iz[:, None, None], ix[None, :, None], iy[None, None, :], core)
        i = jnp.arange(lead)
        a_rows = jnp.where(i < half_out, i, -1)
        b_rows = jnp.where(i < out_rows - half_out, half_out + i, -1)
        found = []
        for side, lines in ((0, a_rows), (1, a_rows), (2, b_rows), (3, b_rows)):
            at = device[:, :, side].T if side < 2 else device[:, side - 2, :].T
            found.append(jnp.where(lines < 0, -1, at[..., None] * out_rows + lines).reshape(-1))
        return jnp.concatenate(found)

    own_numbers, peer_numbers = misc_numbers(c), misc_numbers(1 - c)
    near_pick = (wanted[:, None] == own_numbers[None, :]).astype(bf16)
    far_pick = (wanted[:, None] == peer_numbers[None, :]).astype(bf16)
    their_pick = (their_wanted[:, None] == own_numbers[None, :]).astype(bf16)
    pick_cols = (jnp.arange(D)[:, None] == wanted[None, :]).astype(bf16)
    places = jnp.concatenate([wanted, their_wanted])
    place_cols = (places[:, None] == jnp.arange(D)[None, :]).astype(bf16)

    first_bias = synth_first_bias.reshape(1, cols)
    second = synth_second.reshape(cols, LC)
    values = [value_weight[level].reshape(cols, HD) for level in range(LAYERS)]
    first = synth_first.reshape(cols, HD)
    head_weights = [
        (first, first_bias, second, synth_second_bias, first_bias, values[0]),
        (first_bias, first_bias, first_bias, first_bias, random_scores, values[1]),
    ]

    def line(v, level, which):
        return v[level, which][None]

    chip_rows = 2 * rows
    row_low, row_high = ((chip_rows, D), bf16), ((chip_rows, D), f32)
    head_low, vector = ((chip_rows, cols), bf16), ((1, D), f32)
    hidden_low = ((n, chip_rows, units), bf16)
    groups = [pltpu.VMEM((4 * k, cols), bf16) for k in counts]
    group_pair = pltpu.VMEM((2, chip_rows, cols), bf16)

    def refs(blocks, at, length):
        if aligned:
            return list(blocks), at
        return [b[:, at : at + length].reshape(-1, D) for b in blocks], None

    def synthesis(level, own, got, *wait):
        return stage(
            4.5 if level == 0 else 2.3,
            partial(synth_kernel, level, counts),
            [head_low] * 2,
            (scalars, own, got, *head_weights[level]),
            scratch=[group_pair, *groups, *groups],
            smem=1,
            wait=wait,
        )

    def pick(blocks, *wait):
        blocks, at = refs(blocks, 0, lead)
        out = ((2 * cols, D), bf16)
        mine, theirs = stage(
            1.4,
            partial(pick_kernel, at, lead),
            [out, out],
            (near_pick, their_pick, *blocks),
            wait=wait,
        )
        return mine, links.swap(theirs, c=1)

    def join(near, far, mine, got):
        part, weight = stage(
            0.6,
            join_kernel,
            [row_low, ((2 * cols, D), bf16)],
            (near, far, mine, got),
            wait=[space(mine)],
        )
        return part, links.swap(part, c=1), weight

    def ffn_up(level, rows_in, part, got, ups, miscs, *wait):
        ups, at = refs(ups, lead if level == 0 else 0, size)
        miscs, misc_at = refs(miscs, 0, lead)
        return stage(
            3.6,
            partial(ffn_up_kernel, n, at, misc_at, size, lead, half_out),
            [row_high, row_low, hidden_low, hidden_low],
            (
                rows_in,
                part,
                got,
                line(row_bias, level, 0),
                line(ln_gain, level, 1),
                line(ln_bias, level, 1),
                *ups,
                *miscs,
            ),
            wait=[space(part), *wait],
        )

    def ffn_down(level, hidden, downs, *wait):
        downs, at = refs(downs, lead if level == 0 else size, size)
        (ffn,) = stage(1.6, partial(ffn_down_kernel, n, at, size), [row_low], (hidden, *downs), wait=wait)
        return ffn, links.swap(ffn, c=1)

    gain, shift = line(ln_gain, 0, 0), line(ln_bias, 0, 0)
    token_rows, cotan_rows, own_first, far_first = stage(
        1.6,
        first_norm_kernel,
        [row_low, row_low, head_low, head_low],
        (scalars, mine, peer, gain, shift, pick_cols),
        smem=1,
    )
    got_first = links.swap(far_first, y=1)
    def whole(length):
        return [(0, 0, length, 0, 0), (1, 0, length, 1, 0)]

    (first_rows,) = assemble(
        [first_rows, first_got], [((2, 2 * wide), whole(2 * wide))]
    )
    first_z = Spread(links, first_rows)
    first_z.start_z()
    mixed_first, mixed_far = synthesis(0, own_first, got_first, space(own_first))
    mixed_got_first = links.swap(mixed_far, y=1)

    def pieces(start, length):
        return [
            (source, start + side * half, length, source, side * length)
            for source in range(2)
            for side in range(2)
        ]

    second_rows, last_rows = assemble(
        [rest_rows, rest_got],
        [((2, 2 * wide), pieces(0, wide)), ((2, 4 * size), pieces(wide, 2 * size))],
        [mixed_first],
    )
    second_z, last_z = Spread(links, second_rows), Spread(links, last_rows)
    second_z.start_z()
    (first_chunk,) = first_z.end_z([(0, wide, wide)], mixed_first)
    first_chunk.start_near()
    first_chunk.start_far()
    last_z.start_z(second_z.got)
    mine_first, got_weight = pick(first_chunk.blocks())
    (second_chunk,) = second_z.end_z([(0, wide, wide)], first_chunk.a)
    second_chunk.start_near()
    part, part_got, out_first = join(mixed_first, mixed_got_first, mine_first, got_weight)
    (last_chunk,) = last_z.end_z([(0, 2 * size, 2 * size)], part)
    second_chunk.start_far()
    last_chunk.start_near()
    resid_first, normed_first, *saved_first = ffn_up(
        0, token_rows, part, part_got, first_chunk.blocks(), first_chunk.blocks()
    )
    ffn, ffn_got = ffn_down(0, saved_first[0], second_chunk.blocks())

    rows_second, own_second, far_second = stage(
        1.1,
        next_norm_kernel,
        [row_high, head_low, head_low],
        (
            resid_first,
            ffn,
            ffn_got,
            line(row_bias, 0, 1),
            line(ln_gain, 1, 0),
            line(ln_bias, 1, 0),
            pick_cols,
        ),
        wait=[space(ffn)],
    )
    got_second = links.swap(far_second, y=1)
    mine_second, got_weight = pick(second_chunk.blocks(), rows_second)
    mixed_second, mixed_far = synthesis(1, own_second, got_second, space(own_second))
    mixed_got_second = links.swap(mixed_far, y=1)
    last_chunk.start_far(mixed_got_second)
    part, part_got, out_second = join(mixed_second, mixed_got_second, mine_second, got_weight)
    resid_second, normed_second, *saved_second = ffn_up(
        1, rows_second, part, part_got, last_chunk.blocks(), second_chunk.blocks()
    )

    def ffn_back(level, grad_rows, normed, saved, ups, downs, *wait):
        ups, up_at = refs(ups, lead if level == 0 else 0, size)
        downs, down_at = refs(downs, lead if level == 0 else size, size)
        out = ((chips, 2 * size, D) if aligned else (2, units, D), bf16)
        d_normed, bias_grad, hidden_bias, *terms = stage(
            6.5,
            partial(ffn_back_kernel, n, up_at, down_at, size),
            [row_low, vector, ((n, units), f32)] + [out] * n,
            (grad_rows, normed, *saved, *ups, *downs),
            wait=wait,
        )
        if not aligned:
            terms = [jnp.concatenate(list(t.reshape(2, chips, size, D)), axis=1) for t in terms]
        return d_normed, links.swap(d_normed, c=1), bias_grad, hidden_bias, terms

    def join_back(level, grad_rows, part, got, resid, weight, near, far, hidden_bias, *wait):
        misc_out = ((n * chips * lead, D), bf16)
        d_resid, d_own, d_far, gain, shift, bias, out_near, out_far = stage(
            3.2,
            partial(join_back_kernel, lead, half_out, size),
            [row_high, head_low, head_low, vector, vector, vector, misc_out, misc_out],
            (
                grad_rows,
                part,
                got,
                resid,
                line(ln_gain, level, 1),
                weight,
                near,
                far,
                near_pick,
                far_pick,
                hidden_bias,
            ),
            scratch=[pltpu.VMEM((chip_rows, D), bf16)],
            wait=wait,
        )
        return d_resid, d_own, links.swap(d_far, y=1), (gain, shift, bias), out_near, out_far

    lines = LC // n_wide
    random_parts = 2 if lines % 16 == 0 else 1
    lines_each = -(-heads * HD // n_wide // 16) * 16

    def synth_back(level, own, got, d_own, d_got, value_high=(), wait=()):
        square = pltpu.VMEM((cols, cols), f32)
        scratch = [group_pair, pltpu.VMEM((LC, cols), f32), *groups, *groups]
        scratch = scratch + [pltpu.VMEM((LC, cols), f32)]
        if level == 0:
            outs = [((nz, 2 * lines_each, LC), bf16)] * 2
            scratch = scratch + [
                square,
                pltpu.VMEM((cols, LC), f32),
                pltpu.VMEM((8, LC), f32),
                square,
                pltpu.VMEM((1, cols), f32),
            ]
        else:
            random_out = (nz, heads * lines, LC) if random_parts == 2 else (heads, LC, LC)
            outs = [((cols, cols), f32)] + [(random_out, bf16)] * random_parts
            scratch = scratch + [pltpu.VMEM((heads, LC, LC), f32)]
        dx_own, dx_far, *found = stage(
            10.4 if level == 0 else 4.6,
            partial(synth_back_kernel, level, counts, random_parts),
            [head_low] * 2 + outs,
            (scalars, own, got, d_own, d_got, *head_weights[level], *value_high),
            scratch=scratch,
            smem=1,
            wait=wait,
        )
        return dx_own, links.swap(dx_far, y=1), links.swap(dx_own, c=1), found

    d_normed, d_got, ffn_bias_second, hidden_bias, terms_second = ffn_back(
        1, cotan_rows, normed_second, saved_second, last_chunk.blocks(), last_chunk.blocks()
    )
    x_near = links.swap(terms_second[3], x=1)
    y_near = links.swap(terms_second[1], y=1)
    d_resid, d_own, d_mixed_got, stats_second, near_second, far_second_out = join_back(
        1, cotan_rows, d_normed, d_got, resid_second, out_second, mixed_second, mixed_got_second,
        hidden_bias, space(d_normed),
    )
    far_second_out = links.swap(far_second_out, c=1)
    dx_own, dx_got, dx_peer, found_second = synth_back(
        1, own_second, got_second, d_own, d_mixed_got, wait=[space(d_own)]
    )
    dx_peer_got = links.swap(dx_got, c=1)
    spaced = space(dx_own)
    send, b_keep = fold_first(terms_second[2], x_near, dx_got, spaced)
    y_far = links.swap(send, y=1)
    send, a_keep = fold_first(terms_second[0], y_near, dx_got, spaced)
    x_far = links.swap(send, x=1)
    grad_rows, *stats_rows_second = stage(
        1.5,
        rows_back_kernel,
        [row_high, vector, vector],
        (
            d_resid, dx_own, dx_got, dx_peer, dx_peer_got, place_cols, rows_second,
            line(ln_gain, 1, 0),
        ),
        wait=[a_keep, b_keep, space(dx_got, spaced)],
    )
    if random_parts == 2:
        x_random = links.swap(found_second[2], x=1)

    d_normed, d_got, ffn_bias_first, hidden_bias, terms_first = ffn_back(
        0, grad_rows, normed_first, saved_first, first_chunk.blocks(), second_chunk.blocks()
    )
    d_resid, d_own, d_mixed_got, stats_first, near_first, far_first_out = join_back(
        0, grad_rows, d_normed, d_got, resid_first, out_first, mixed_first, mixed_got_first,
        hidden_bias, space(d_normed),
    )
    far_first_out = links.swap(far_first_out, c=1)
    if aligned:
        terms_first = stage(
            1.5,
            misc_kernel,
            [((chips, 2 * size + 2 * lead, D), bf16)] * n,
            (near_first, far_first_out, near_second, far_second_out, *terms_first),
        )
    else:
        misc = [v.reshape(n, chips, lead, D) for v in (near_first, near_second)]
        got = [v.reshape(n, chips, lead, D) for v in (far_first_out, far_second_out)]
        misc = jnp.concatenate([a + b for a, b in zip(misc, got)], axis=2)
        terms_first = [jnp.concatenate([t, m], axis=1) for t, m in zip(terms_first, misc)]
    x_near = links.swap(terms_first[3], x=1)
    y_near = links.swap(after(terms_first[1], d_mixed_got), y=1)
    second_fold = Fold(links, [(a_keep, x_far), (b_keep, y_far)], d_own)
    second_fold.start(chain=True)
    dx_own, dx_got, dx_peer, found_first = synth_back(
        0, own_first, got_first, d_own, d_mixed_got, (found_second[0],),
        (second_fold.keep, terms_first[0], space(d_own)),
    )
    spaced = space(dx_own)
    send, b_keep = fold_first(terms_first[2], x_near, dx_own, spaced)
    y_far = links.swap(after(send, y_near), y=1)
    send, a_keep = fold_first(terms_first[0], y_near, b_keep)
    x_far = links.swap(send, x=1)
    dx_peer_got = links.swap(after(dx_got, a_keep), c=1)
    *grad_parts, gain, shift = stage(
        1.7,
        partial(rows_last_kernel, counts),
        [((k, D), f32) for k in counts] + [vector, vector],
        (
            scalars, d_resid, dx_own, dx_got, dx_peer, dx_peer_got, place_cols, token_rows,
            line(ln_gain, 0, 0),
        ),
        scratch=[pltpu.VMEM((chip_rows, D), f32)],
        smem=1,
        wait=[a_keep, space(a_keep)],
    )
    pack_own, pack_other = found_first
    x_pack = links.swap(pack_other, x=1)
    ffn, ffn_got = ffn_down(1, saved_second[0], last_chunk.blocks(), second_fold.keep)
    out_parts = stage(
        1.0,
        partial(last_kernel, counts),
        [((k, D), bf16) for k in counts],
        (scalars, resid_second, ffn, ffn_got, line(row_bias, LAYERS - 1, 1)),
        smem=1,
    )

    def stat_lines(inner, outer, ffn_bias):
        gain, shift, bias = outer
        return jnp.concatenate([inner[0], gain, inner[1], shift, bias, ffn_bias])

    summed = jnp.stack(
        [
            stat_lines((gain, shift), stats_first, ffn_bias_first),
            stat_lines(stats_rows_second, stats_second, ffn_bias_second),
        ]
    )

    if random_parts == 2:
        pairs = [(found_second[1], x_random), (pack_own, x_pack)]
    else:
        pairs = [(pack_own, x_pack)]
    head_fold = Fold(links, pairs, *second_fold.gots)
    head_fold.start()
    first_fold = Fold(links, [(a_keep, x_far), (b_keep, y_far)], head_fold.keep)
    first_fold.start()
    summed = links.total(summed, first_fold.keep, first_fold.keep)
    found = head_fold.finish(first_fold.gots[0])
    if random_parts == 2:
        random, pack = found[: heads * lines], found[heads * lines :]
    else:
        random, pack = found_second[1].reshape(heads, n_wide, lines, LC), found
        random = lax.psum_scatter(random, "wide", scatter_dimension=1, tiled=False).astype(f32)
    second, rest = (
        pack[k * lines_each :][: heads * HD // n_wide].reshape(heads, HD // n_wide, LC)
        for k in range(2)
    )
    if aligned and nz <= 4:
        weight = ((LAYERS, 2 * size, D), f32)
        down_grad, up_grad, misc = stage(
            1.0,
            partial(finish_kernel, size, lead),
            [weight, weight, ((LAYERS, 2, lead, D), f32)],
            (first_fold.keep, second_fold.keep, *first_fold.gots, *second_fold.gots),
        )
    else:
        found = [first_fold.finish().reshape(2, -1, D), second_fold.finish().reshape(2, -1, D)]
        down_grad = jnp.stack([v[:, :size].reshape(-1, D) for v in found])
        up_grad = jnp.stack([v[:, size : 2 * size].reshape(-1, D) for v in found])
        misc = found[0][:, 2 * size :].reshape(2, LAYERS, lead, D)
        misc = jnp.moveaxis(misc, 0, 1)
    out_grad = misc[:, :, :half_out].reshape(LAYERS, -1, D)[:, :out_rows]
    bias_grad = misc[:, :, half_out, :size].reshape(LAYERS, -1)
    return (
        *out_parts,
        *grad_parts,
        summed[:, 0:2],
        summed[:, 2:4],
        summed[:, 4:6],
        out_grad,
        up_grad,
        bias_grad,
        down_grad,
        rest[:, :, :HD],
        rest[:, :, 128 + HD],
        second,
        rest[:, 0, 256 : 256 + lines],
        random.reshape(heads, lines, LC),
        jnp.stack([rest[:, :, HD:128], rest[:, :, 128 : 128 + HD]]),
    )


def solution(mesh):
    placed = (
        P(("wide", "head"), None),
        P(("wide", "head"), None),
        P(("wide", "head"), None),
        P("wide"),
        P("wide"),
        P("wide"),
        P(("wide", "head"), None),
        P(("wide", "head"), None),
        P(("wide", "head"), None),
        P(),
        P(),
        P(),
        P(None, ("wide", "head"), None),
        P(None, ("wide", "head"), None),
        P(None, ("wide", "head")),
        P(None, ("wide", "head"), None),
        P("head", None, None),
        P("head", None),
        P("head", None, None),
        P("head", None),
        P("head", None, None),
        P(None, "head", None, None),
    )
    return jax.shard_map(
        partial(per_device, Links(mesh.shape["wide"], mesh.shape["head"])),
        mesh=mesh,
        in_specs=placed,
        out_specs=(
            P(("wide", "head"), None),
            P(("wide", "head"), None),
            P(("wide", "head"), None),
            P(("wide", "head"), None),
            P(("wide", "head"), None),
            P(("wide", "head"), None),
            P(),
            P(),
            P(),
            P(None, ("wide", "head"), None),
            P(None, ("wide", "head"), None),
            P(None, ("wide", "head")),
            P(None, ("wide", "head"), None),
            P("head", "wide", None),
            P("head", "wide"),
            P("head", "wide", None),
            P("head", "wide"),
            P("head", "wide", None),
            P(None, "head", "wide", None),
        ),
        check_vma=False,
    )
```

```python
import math
from functools import partial

import jax
import jax.numpy as jnp
import numpy as np
from jax import lax
from jax.experimental import pallas as pl
from jax.experimental.pallas import tpu as pltpu
from jax.sharding import PartitionSpec as P

HD = 64
LC = 512
LA = 128
LB = 256
LAYERS = 2
D = 768

EPSILON = 1e-05
MASKED_SCORE = -1e30
AXES = ("wide", "head")
ROW_TILE = 112
SCORE_TILE = 256
SPARE = 8 * 1024 * 1024
FLOPS_PER_US = 1.1e9
SPACE_US = 12.0
f32 = jnp.float32
bf16 = jnp.bfloat16


class Links:
    def __init__(self, n_wide, n_head):
        self.nx, self.nc = 2, 2
        self.nz, self.ny = n_wide // 2, n_head // 2
        self.n_wide = n_wide
        self.bits = [1 << k for k in range(self.nz.bit_length() - 1)]

    def number(self, z, x, y, c):
        return ((z * self.nx + x) * self.ny + y) * self.nc + c

    def places(self):
        wide, head = lax.axis_index("wide"), lax.axis_index("head")
        return wide // self.nx, wide % self.nx, head // self.nc, head % self.nc

    def swap(self, v, z=0, x=0, y=0, c=0):
        pairs = [
            (self.number(i ^ z, j ^ x, k ^ y, m ^ c), self.number(i, j, k, m))
            for i, j, k, m in np.ndindex(self.nz, self.nx, self.ny, self.nc)
        ]
        return lax.ppermute(v, AXES, pairs)

    def total(self, v, *waits):
        steps = [{"z": bit} for bit in self.bits] + [{"x": 1}, {"y": 1}]
        for k, step in enumerate(steps):
            got = self.swap(v, **step)
            if k + len(waits) >= len(steps):
                got = after(got, waits[k + len(waits) - len(steps)])
            v = v + got
        return v


def nothing_kernel(*refs):
    pass


def after(v, *others):
    return pl.pallas_call(
        nothing_kernel,
        out_shape=jax.ShapeDtypeStruct(v.shape, v.dtype),
        in_specs=[pl.BlockSpec(memory_space=pl.ANY)] * (1 + len(others)),
        out_specs=pl.BlockSpec(memory_space=pl.ANY),
        input_output_aliases={0: 0},
        compiler_params=pltpu.CompilerParams(vmem_limit_bytes=1 << 20),
        cost_estimate=pl.CostEstimate(flops=1, bytes_accessed=0, transcendentals=0),
    )(v, *others)


class Spread:
    def __init__(self, links, v):
        self.links, self.v = links, v

    def start_z(self, *wait):
        for bit in self.links.bits[1:-1]:
            self.v = jnp.concatenate([self.v, self.links.swap(self.v, z=bit)], axis=0)
        v = after(self.v, *wait) if wait else self.v
        self.got = self.links.swap(v, z=self.links.bits[-1])

    def end_z(self, cuts, *wait):
        n = self.v.shape[0]
        plans = []
        for a, b, rows in cuts:
            for start in (a, b):
                plans.append(((2 * n, rows), [(0, start, rows, 0, 0), (1, start, rows, n, 0)]))
        halves = assemble([self.v, self.got], plans, wait)
        return [Near(self.links, a, b) for a, b in zip(halves[::2], halves[1::2])]


class Near:
    def __init__(self, links, a, b):
        self.links, self.a, self.b = links, a, b

    def start_near(self, *wait):
        a, b = (after(v, *wait) if wait else v for v in (self.a, self.b))
        self.got_a, self.got_b = self.links.swap(a, x=1), self.links.swap(b, y=1)

    def start_far(self, *wait):
        n, rows = self.a.shape[:2]
        wait = (*wait, space(self.a))
        plan = [
            ((2 * n, rows), [(k, 0, rows, 0, 0), (k + 1, 0, rows, n, 0)]) for k in (0, 2)
        ]
        self.a, self.b = assemble([self.a, self.got_a, self.b, self.got_b], plan, wait)
        self.far_a, self.far_b = self.links.swap(self.a, y=1), self.links.swap(self.b, x=1)

    def blocks(self):
        return [self.a, self.far_a, self.b, self.far_b]


def fold_first(own, gots, *wait, rest=()):
    n, rows, width = own.shape[0] // 2, own.shape[1], own.shape[2]
    more = sum(v.shape[1] for v in rest)
    if len(gots) > 1 and gots[0].shape[1] % 16 != 0:
        gots = [jnp.concatenate(gots, axis=1)]
    return stage(
        1.0,
        partial(fold_first_kernel, len(gots)),
        [((n, rows + more, width), bf16), ((n, rows, width), bf16)],
        (own, *gots, *rest),
        wait=wait,
    )


class Fold:
    def __init__(self, links, pairs, *wait, halves=False):
        self.links = links
        starts = [pair[2] if len(pair) > 2 else 0 for pair in pairs]
        flat = [v for pair in pairs for v in pair[:2]]
        n = links.nz if links.nz <= 4 and not halves else 2
        rows = sum(pair[0].shape[1] for pair in pairs)
        shape = (links.nz // n, rows, flat[0].shape[2])
        self.keep, *self.sends = stage(
            1.0,
            partial(fold_second_kernel, n, starts),
            [(shape, f32)] + [(shape, bf16)] * (n - 1),
            flat,
            wait=wait,
        )
        self.bits = list(reversed(links.bits))[1:] if n == 2 else []

    def start(self, *wait, chain=False):
        sends = [after(v, *wait) if wait else v for v in self.sends]
        if len(sends) == 1:
            self.gots = [self.links.swap(sends[0], z=self.links.nz // 2)]
        else:
            self.gots = []
            for k, v in enumerate(sends):
                v = after(v, self.gots[0]) if chain and k > 0 else v
                self.gots.append(self.links.swap(v, z=k + 1))

    def step(self, *wait):
        bit = self.bits.pop(0)
        shape = (bit, *self.keep.shape[1:])
        send, self.keep = stage(
            1.0, fold_z_kernel, [(shape, bf16), (shape, f32)], (self.keep, *self.gots), wait=wait
        )
        self.gots = [self.links.swap(send, z=bit)]
        return self.keep

    def steps(self):
        while self.bits:
            self.step()
        return self.keep, self.gots

    def finish(self, *wait):
        keep, gots = self.steps()
        (total,) = stage(
            1.0, fold_last_kernel, [(keep.shape, f32)], (keep, *gots), wait=wait
        )
        return total[0]


def stage(us, kernel, outs, args, scratch=(), smem=0, wait=()):
    count = len(args)
    spaces = [pltpu.SMEM] * smem + [pltpu.VMEM] * (count - smem) + [pl.ANY] * len(wait)
    size = sum(a.size * a.dtype.itemsize for a in args[smem:])
    size = size + sum(math.prod(s) * jnp.dtype(d).itemsize for s, d in outs)
    held = sum(math.prod(s.shape) * jnp.dtype(s.dtype).itemsize for s in scratch)

    def body(*refs):
        kernel(*refs[:count], *refs[count + len(wait) :])

    return pl.pallas_call(
        body,
        out_shape=[jax.ShapeDtypeStruct(s, d) for s, d in outs],
        in_specs=[pl.BlockSpec(memory_space=s) for s in spaces],
        out_specs=[pl.BlockSpec(memory_space=pltpu.VMEM) for _ in outs],
        scratch_shapes=list(scratch),
        compiler_params=pltpu.CompilerParams(vmem_limit_bytes=size + held + SPARE),
        cost_estimate=pl.CostEstimate(
            flops=int(us * FLOPS_PER_US), bytes_accessed=0, transcendentals=0
        ),
    )(*args, *wait)


def space_kernel(out):
    out[...] = jnp.zeros_like(out)


def space(*deps):
    return stage(SPACE_US, space_kernel, [((8, 128), f32)], (), wait=deps)[0]


def mm(a, b):
    return lax.dot_general(a, b, (((1,), (0,)), ((), ())), preferred_element_type=f32)


def mm_nt(a, b):
    return lax.dot_general(a, b, (((1,), (1,)), ((), ())), preferred_element_type=f32)


def mm_tn(a, b):
    return lax.dot_general(a, b, (((0,), (0,)), ((), ())), preferred_element_type=f32)


def one_hot(mask):
    return mask.astype(f32).astype(bf16)


def tiles(rows):
    return [pl.ds(i, ROW_TILE) for i in range(0, rows, ROW_TILE)]


def centre(v):
    middle = jnp.mean(v, axis=-1, keepdims=True)
    centred = v - middle
    scale = lax.rsqrt(jnp.mean(centred * centred, axis=-1, keepdims=True) + EPSILON)
    return centred * scale, scale


def norm_back(v, gain, d_out):
    unit, scale = centre(v)
    inner = d_out * gain
    flat = jnp.mean(inner, axis=-1, keepdims=True)
    along = jnp.mean(inner * unit, axis=-1, keepdims=True)
    d_rows = scale * (inner - flat - unit * along)
    return d_rows, jnp.sum(d_out * unit, axis=0, keepdims=True), jnp.sum(d_out, 0, keepdims=True)


def gelu_both(v):
    k = math.sqrt(2.0 / math.pi)
    square = v * v
    t = jnp.tanh(k * v * (1.0 + 0.044715 * square))
    half = 0.5 * (1.0 + t)
    slope = half + 0.5 * v * (1.0 - t * t) * (k * (1.0 + 3 * 0.044715 * square))
    return v * half, slope


def move(moves, sems):
    copies = [pltpu.make_async_copy(a, b, sems.at[i]) for i, (a, b) in enumerate(moves)]
    for copy in copies:
        copy.start()
    for copy in copies:
        copy.wait()


def pack_rows_kernel(*refs):
    *parts, rows, sems = refs
    moves, start = [], 0
    for ref in parts:
        moves.append((ref, rows.at[pl.ds(start, ref.shape[0])]))
        start = start + ref.shape[0]
    move(moves, sems)


def pack_weights_kernel(size, misc, up, down, first, rest, sems):
    lead = misc.shape[2]
    wide, narrow = lead + size, size
    half = wide + 2 * narrow
    moves = []
    for side in range(2):
        part = pl.ds(side * size, size)
        moves.append((misc.at[0, side], first.at[pl.ds(side * wide, lead)]))
        moves.append((up.at[0, part], first.at[pl.ds(side * wide + lead, size)]))
        at = side * half
        moves.append((misc.at[1, side], rest.at[pl.ds(at, lead)]))
        moves.append((down.at[0, part], rest.at[pl.ds(at + lead, size)]))
        moves.append((up.at[1, part], rest.at[pl.ds(at + wide, size)]))
        moves.append((down.at[1, part], rest.at[pl.ds(at + wide + narrow, size)]))
    move(moves, sems)


def lay_out(kernel, outs, args, copies, wait=()):
    def body(*refs):
        kernel(*refs[: len(args)], *refs[len(args) + len(wait) :])

    return pl.pallas_call(
        body,
        out_shape=[jax.ShapeDtypeStruct((k, D), bf16) for k in outs],
        in_specs=[pl.BlockSpec(memory_space=pltpu.HBM)] * len(args)
        + [pl.BlockSpec(memory_space=pl.ANY)] * len(wait),
        out_specs=[pl.BlockSpec(memory_space=pltpu.VMEM)] * len(outs),
        scratch_shapes=[pltpu.SemaphoreType.DMA((copies,))],
        compiler_params=pltpu.CompilerParams(vmem_limit_bytes=SPARE),
    )(*args, *wait)


def assemble_kernel(plans, n, *refs):
    for out, pieces in zip(refs[n:], plans):
        for source, start, rows, place, row in pieces:
            piece = refs[source][:, start : start + rows, :]
            out[place : place + piece.shape[0], row : row + rows, :] = piece


def assemble(sources, outs, wait=()):
    whole = all(
        start % 16 == 0 and rows % 16 == 0 and row % 16 == 0
        for _, pieces in outs
        for _, start, rows, _, row in pieces
    )
    if whole:
        plans = [pieces for _, pieces in outs]
        shapes = [((*shape, D), bf16) for shape, _ in outs]
        return stage(
            0.7, partial(assemble_kernel, plans, len(sources)), shapes, sources, wait=wait
        )
    found = []
    for shape, pieces in outs:
        columns = {}
        for source, start, rows, place, row in sorted(pieces, key=lambda p: (p[4], p[3])):
            columns.setdefault(row, []).append(sources[source][:, start : start + rows])
        columns = [jnp.concatenate(v, axis=0) for _, v in sorted(columns.items())]
        found.append(jnp.concatenate(columns, axis=1))
    return found


def first_norm_kernel(scalars, mine, peer, gain, shift, pick, tokens, cotans, own, far):
    c = scalars[4]
    rows, cols = mine.shape[0] // 2, own.shape[1]
    for ref, core in ((mine, c), (peer, 1 - c)):
        for i in range(0, rows, ROW_TILE):
            t = pl.ds(pl.multiple_of(core * rows + i, 16), ROW_TILE)
            v = ref[i : i + ROW_TILE, :]
            tokens[t, :] = v
            cotans[t, :] = ref[rows + i : rows + i + ROW_TILE, :]
            unit, _ = centre(v.astype(f32))
            normed = (unit * gain[...] + shift[...]).astype(bf16)
            picked = mm(normed, pick[...]).astype(bf16)
            own[t, :] = picked[:, :cols]
            far[t, :] = picked[:, cols:]


def next_norm_kernel(resid, part, got, bias, gain, shift, pick, rows, own, far):
    for t in tiles(resid.shape[0]):
        v = resid[t, :] + (part[t, :].astype(f32) + got[t, :].astype(f32)) + bias[...]
        rows[t, :] = v
        unit, _ = centre(v)
        normed = (unit * gain[...] + shift[...]).astype(bf16)
        picked = mm(normed, pick[...]).astype(bf16)
        own[t, :] = picked[:, : own.shape[1]]
        far[t, :] = picked[:, own.shape[1] :]


def pick_kernel(at, size, mine_pick, their_pick, *refs):
    blocks, (mine, theirs) = refs[:-2], refs[-2:]
    for pick, out in ((mine_pick, mine), (their_pick, theirs)):
        total = None
        for k, ref in enumerate(blocks):
            lines = block(ref, at, size)
            n = lines.shape[0]
            term = mm(pick[:, k * n : (k + 1) * n], lines)
            total = term if total is None else total + term
        out[...] = total.astype(bf16)


def join_kernel(near, far, mine, got, part, weight):
    cols = near.shape[1]
    weight[...] = (mine[...].astype(f32) + got[...].astype(f32)).astype(bf16)
    total = mm(near[...], weight[:cols, :]) + mm(far[...], weight[cols:, :])
    part[...] = total.astype(bf16)


def block(ref, start, rows):
    if start is None:
        return ref[...]
    return ref[:, start : start + rows, :].reshape(-1, D)


def line_mask(shape, lead, line, size):
    row = lax.broadcasted_iota(jnp.int32, shape, 0)
    unit = lax.broadcasted_iota(jnp.int32, shape, 1)
    return (row % lead == line) & (row // lead == unit // size)


def ffn_up_kernel(n, at, misc_at, size, lead, line, rows, part, got, bias, gain, shift, *refs):
    ups, miscs = refs[:n], refs[n : 2 * n]
    resid, normed, hidden, slope = refs[2 * n :]
    for t in tiles(rows.shape[0]):
        v = rows[t, :].astype(f32) + (part[t, :].astype(f32) + got[t, :].astype(f32)) + bias[...]
        resid[t, :] = v
        unit, _ = centre(v)
        normed[t, :] = (unit * gain[...] + shift[...]).astype(bf16)
    units = hidden.shape[2]
    lane = lax.broadcasted_iota(jnp.int32, (128, units), 0)
    column = lax.broadcasted_iota(jnp.int32, (128, units), 1)
    place = ((lane % size == column % size) & (lane < 2 * size)).astype(f32).astype(bf16)
    for k in range(n):
        lines = mm(block(miscs[k], misc_at, lead)[:, :128], place)
        lines = jnp.where(line_mask(lines.shape, lead, line, size), lines, 0.0)
        lines = jnp.sum(lines, axis=0, keepdims=True)
        value, grad = gelu_both(mm_nt(normed[...], block(ups[k], at, size)) + lines)
        hidden[k] = value.astype(bf16)
        slope[k] = grad.astype(bf16)


def ffn_down_kernel(n, at, size, hidden, *refs):
    downs, ffn = refs[:n], refs[n]
    total = None
    for k in range(n):
        term = mm(hidden[k], block(downs[k], at, size))
        total = term if total is None else total + term
    ffn[...] = total.astype(bf16)


def ffn_back_kernel(n, up_at, down_at, size, grad_rows, normed, hidden, slope, *refs):
    ups, downs = refs[:n], refs[n : 2 * n]
    d_normed, bias_grad, hidden_bias = refs[2 * n : 2 * n + 3]
    grads = refs[2 * n + 3 :]
    d_ffn = grad_rows[...].astype(bf16)
    bias_grad[...] = jnp.sum(d_ffn.astype(f32), axis=0, keepdims=True)
    total = None
    for k in range(n):
        d_hidden = mm_nt(d_ffn, block(downs[k], down_at, size))
        d_pre = (d_hidden * slope[k].astype(f32)).astype(bf16)
        hidden_bias[k : k + 1, :] = jnp.sum(d_pre.astype(f32), axis=0, keepdims=True)
        down_grad = mm_tn(hidden[k], d_ffn).astype(bf16)
        up_grad = mm_tn(d_pre, normed[...]).astype(bf16)
        if up_at is None:
            grads[k][0] = down_grad
            grads[k][1] = up_grad
        elif k == 1 and len(grads) > n:
            grads[1][...] = down_grad.reshape(-1, size, D)
            grads[n][...] = up_grad.reshape(-1, size, D)
        else:
            grads[k][:, :size, :] = down_grad.reshape(-1, size, D)
            grads[k][:, size:, :] = up_grad.reshape(-1, size, D)
        term = mm(d_pre, block(ups[k], up_at, size))
        total = term if total is None else total + term
    d_normed[...] = total.astype(bf16)


def fold_first_kernel(count, own, *refs):
    gots, rest, (send, keep) = refs[:count], refs[count:-2], refs[-2:]
    n, start = send.shape[0], 0
    for got in gots:
        part = slice(start, start + got.shape[1])
        start = start + got.shape[1]
        for out, half in ((keep, slice(0, n)), (send, slice(n, 2 * n))):
            total = own[half, part, :].astype(f32) + got[half].astype(f32)
            out[:, part, :] = total.astype(bf16)
    for other in rest:
        send[:, start:, :] = other[...]


def misc_kernel(first, second, got, *refs):
    n = len(refs) // 2
    half = first.shape[0]
    for k, (source, out) in enumerate(zip(refs[:n], refs[n:])):
        chips, start = source.shape[:2]
        lead = (out.shape[1] - start) // 2
        out[:, :start, :] = source[...]
        part = slice(k * chips * lead, (k + 1) * chips * lead)
        for i, own in enumerate((first, second)):
            at = start + i * lead
            theirs = got[i * half + part.start : i * half + part.stop, :]
            total = own[part, :].astype(f32) + theirs.astype(f32)
            out[:, at : at + lead, :] = total.astype(bf16).reshape(chips, lead, D)


def fold_second_kernel(n, starts, *refs):
    count = len(refs) - n
    keep, sends = refs[count], refs[count + 1 :]
    at = 0
    for i, start in enumerate(starts):
        own, got = refs[2 * i], refs[2 * i + 1]
        lines, length = own.shape[0] // n, own.shape[1]
        rows, source = slice(at, at + length), slice(start, start + length)
        at = at + length
        for k in range(n):
            part = slice(k * lines, (k + 1) * lines)
            total = own[part].astype(f32) + got[part, source, :].astype(f32)
            if k == 0:
                keep[:, rows, :] = total
            else:
                sends[k - 1][:, rows, :] = total.astype(bf16)


def fold_z_kernel(own, got, send, keep):
    n = send.shape[0]
    keep[...] = own[:n] + got[:n].astype(f32)
    send[...] = (own[n:] + got[n:].astype(f32)).astype(bf16)


def fold_last_kernel(own, *refs):
    *gots, out = refs
    total = own[...]
    for got in gots:
        total = total + got[...].astype(f32)
    out[...] = total


def finish_kernel(size, lead, n, first, second, *refs):
    gots, (down, up, misc, pack) = (refs[:n], refs[n:-4]), refs[-4:]

    def total(own, gots):
        found = own[0]
        for got in gots:
            found = found + got[0].astype(f32)
        return found

    for level, own in enumerate((first, second)):
        found = total(own, gots[level])
        each = 2 * size + (2 * lead if level == 0 else 0)
        for side in range(2):
            at, part = side * each, slice(side * size, (side + 1) * size)
            down[level, part, :] = found[at : at + size]
            up[level, part, :] = found[at + size : at + 2 * size]
            if level == 0:
                for i in range(2):
                    start = at + 2 * size + i * lead
                    misc[i, side] = found[start : start + lead]
        if level == 0:
            pack[...] = found[2 * each :]


def stats_kernel(*refs):
    *rows, out = refs
    for k, row in enumerate(rows):
        out[k : k + 1, :] = row[...]


def last_kernel(counts, scalars, resid, part, got, bias, *outs):
    start = scalars[4] * sum(counts)
    for out, n in zip(outs, counts):
        t = pl.ds(pl.multiple_of(start, 16), n)
        v = resid[t, :] + (part[t, :].astype(f32) + got[t, :].astype(f32)) + bias[...]
        out[...] = v.astype(bf16)
        start = start + n


def rows_last_kernel(counts, scalars, *refs):
    *given, grad_a, grad_b, grad_c, gain_grad, shift_grad, rows = refs
    rows_back_kernel(*given, rows, gain_grad, shift_grad)
    start = scalars[4] * sum(counts)
    for out, n in zip((grad_a, grad_b, grad_c), counts):
        out[...] = rows[pl.ds(pl.multiple_of(start, 16), n), :]
        start = start + n


def join_back_kernel(
    lead, line, size, given, grad_rows, part, got, resid, gain, weight, near, far, near_pick,
    far_pick, hidden_bias, *refs,
):
    earlier, refs = refs[:given], refs[given:]
    (
        d_resid, d_near, d_far, gain_grad, shift_grad, bias_grad, out_near, out_far, d_join,
    ) = refs
    gain_grad[...] = jnp.zeros_like(gain_grad)
    shift_grad[...] = jnp.zeros_like(shift_grad)
    bias_grad[...] = jnp.zeros_like(bias_grad)
    for t in tiles(resid.shape[0]):
        d_out = part[t, :].astype(f32) + got[t, :].astype(f32)
        d_rows, d_gain, d_shift = norm_back(resid[t, :], gain[...], d_out)
        gain_grad[...] += d_gain
        shift_grad[...] += d_shift
        d_rows = d_rows + grad_rows[t, :].astype(f32)
        d_resid[t, :] = d_rows
        low = d_rows.astype(bf16)
        d_join[t, :] = low
        bias_grad[...] += jnp.sum(low.astype(f32), axis=0, keepdims=True)
    cols = near.shape[1]
    d_near[...] = mm_nt(d_join[...], weight[:cols, :]).astype(bf16)
    d_far[...] = mm_nt(d_join[...], weight[cols:, :]).astype(bf16)
    grad_near = mm_tn(near[...], d_join[...]).astype(bf16)
    grad_far = mm_tn(far[...], d_join[...]).astype(bf16)
    lines = out_near.shape[0]
    for pick, out in ((near_pick, out_near), (far_pick, out_far)):
        total = mm_tn(pick[:cols, :], grad_near) + mm_tn(pick[cols:, :], grad_far)
        out[:lines, :] = total.astype(bf16)
    for other in earlier:
        out_far[lines:, :] = other[...]
    n, units = hidden_bias.shape
    rows = out_near.shape[0] // n
    unit = lax.broadcasted_iota(jnp.int32, (units, 128), 0)
    lane = lax.broadcasted_iota(jnp.int32, (units, 128), 1)
    place = (unit % size == lane).astype(f32).astype(bf16)
    mask = line_mask((rows, units), lead, line, size)
    for k in range(n):
        lines = jnp.where(mask, hidden_bias[k : k + 1, :], 0.0).astype(bf16)
        part_rows = slice(k * rows, (k + 1) * rows)
        lines = mm(lines, place) + out_near[part_rows, :128].astype(f32)
        out_near[part_rows, :128] = lines.astype(bf16)


def rows_back_kernel(
    d_resid, near, far, peer_near, peer_far, place, rows, gain, grad_rows, gain_grad, shift_grad
):
    cols = near.shape[1]
    gain_grad[...] = jnp.zeros_like(gain_grad)
    shift_grad[...] = jnp.zeros_like(shift_grad)
    for t in tiles(rows.shape[0]):
        d_out = mm(near[t, :], place[:cols, :]) + mm(far[t, :], place[cols : 2 * cols, :])
        d_out = d_out + mm(peer_near[t, :], place[2 * cols : 3 * cols, :])
        d_out = d_out + mm(peer_far[t, :], place[3 * cols :, :])
        d_rows, d_gain, d_shift = norm_back(rows[t, :].astype(f32), gain[...], d_out)
        gain_grad[...] += d_gain
        shift_grad[...] += d_shift
        grad_rows[t, :] = d_resid[t, :] + d_rows


def group_pieces(counts):
    total = sum(counts)
    start = 0
    found = []
    for bucket, n in enumerate(counts):
        for chip in range(2):
            for core in range(2):
                found.append((bucket, chip, core * total + start, (2 * chip + core) * n, n))
        start = start + n
    return found


def load_groups(counts, y, near, far, whole, buckets):
    whole[y] = near[...]
    whole[1 - y] = far[...]
    for bucket, chip, source, target, n in group_pieces(counts):
        buckets[bucket][target : target + n, :] = whole[chip, source : source + n, :]


def store_groups(counts, y, buckets, whole, near, far):
    for bucket, chip, source, target, n in group_pieces(counts):
        whole[chip, source : source + n, :] = buckets[bucket][target : target + n, :]
    near[...] = whole[y]
    far[...] = whole[1 - y]


def head_lanes(shape, h):
    return lax.broadcasted_iota(jnp.int32, shape, 1) // HD == h


def only_head(v, h):
    return jnp.where(head_lanes(v.shape, h), v, jnp.zeros_like(v))


def soft(level, h, act, length, span, second, second_bias, random, tile):
    if level == 0:
        scores = mm(only_head(act, h), second[:, :span]) + second_bias[h : h + 1, :span]
    else:
        scores = random[h, tile, :span].astype(f32)
    keys = lax.broadcasted_iota(jnp.int32, scores.shape, 1) < length
    scores = jnp.where(keys, scores, MASKED_SCORE)
    e = jnp.exp(scores - jnp.max(scores, axis=-1, keepdims=True))
    return e * (1.0 / jnp.sum(e, axis=-1, keepdims=True))


def score_tiles(span):
    size = min(span, SCORE_TILE)
    return [pl.ds(i, size) for i in range(0, span, size)]


def diagonal(ref):
    cols = ref.shape[0]
    row = lax.broadcasted_iota(jnp.int32, (HD, cols), 0)
    col = lax.broadcasted_iota(jnp.int32, (HD, cols), 1)
    wide = mm(ref[...], one_hot(col % HD == row))
    row = lax.broadcasted_iota(jnp.int32, (cols, cols), 0)
    col = lax.broadcasted_iota(jnp.int32, (cols, cols), 1)
    return jnp.where(row // HD == col // HD, wide, 0.0).astype(bf16)


def synth_kernel(level, counts, scalars, near, far, first, first_bias, second, second_bias,
                 random, value, mixed_near, mixed_far, whole, rows_a, rows_b, rows_c,
                 mixed_a, mixed_b, mixed_c):
    y = scalars[0]
    rows, mixed = (rows_a, rows_b, rows_c), (mixed_a, mixed_b, mixed_c)
    heads = near.shape[1] // HD
    value = diagonal(value)
    if level == 0:
        first = diagonal(first)
    load_groups(counts, y, near, far, whole, rows)
    for k, span in enumerate((LA, LB, LC)):
        values = mm(rows[k][...], value).astype(bf16)
        by_head = [only_head(values, h) for h in range(heads)]
        for t in score_tiles(span):
            act = None
            if level == 0:
                act = gelu_both(mm(rows[k][t, :], first) + first_bias[...])[0].astype(bf16)
            total = None
            for h in range(heads):
                p = soft(level, h, act, scalars[1 + k], span, second, second_bias, random, t)
                term = mm(p.astype(bf16), by_head[h])
                total = term if total is None else total + term
            mixed[k][t, :] = total.astype(bf16)
    store_groups(counts, y, mixed, whole, mixed_near, mixed_far)


def pack_grads(heads, n_wide, value_high, value_low, second, second_bias, first, first_bias):
    cols = heads * HD

    def grid(shape):
        return [lax.broadcasted_iota(jnp.int32, shape, k) for k in range(2)]

    row, col = grid((cols, cols))
    same = row // HD == col // HD
    source, lane = grid((cols, 128))
    left = one_hot((source % HD == lane) & (lane < HD))
    right = one_hot((source % HD == lane - HD) & (lane >= HD))

    def blocks(v, place):
        return mm(jnp.where(same, v[...], 0.0).astype(bf16), place)

    column = jnp.sum(jnp.where(row == col, first_bias[...], 0.0), axis=1, keepdims=True)
    tail = blocks(value_high, left) + jnp.where(lane == HD, column, 0.0)
    row, col = grid((cols, second_bias.shape[0]))
    lines = mm(one_hot(row // HD == col), second_bias[...].astype(bf16))
    wide = LC // n_wide
    row, col = grid((cols, LC))
    lines = jnp.where(col // wide == (row % HD) // (HD // n_wide), lines, 0.0).astype(bf16)
    source, lane = grid((LC, 128))
    lines = mm(lines, one_hot((source % wide == lane) & (lane < wide)))
    rest = jnp.concatenate(
        [
            second[...].astype(bf16),
            (blocks(first, left) + blocks(value_low, right)).astype(bf16),
            tail.astype(bf16),
        ],
        axis=1,
    )
    return rest, lines.astype(bf16)


def wide_rows(shape, heads, z, x):
    n, lines = shape[0], shape[1]
    row = lax.broadcasted_iota(jnp.int32, (n * lines, heads * HD), 0)
    col = lax.broadcasted_iota(jnp.int32, (n * lines, heads * HD), 1)
    per = HD // (2 * n)
    wide = 2 * (z ^ (row // lines)) + x
    i = row % lines
    source = (i // per) * HD + wide * per + i % per
    return one_hot((source == col) & (i < heads * per))


def synth_back_kernel(level, counts, random_parts, scalars, near, far, d_near, d_far, first, first_bias, second,
                      second_bias, random, value, *refs):
    y = scalars[0]
    if level == 0:
        (value_high, dx_near, dx_far, pack_own, pack_other, *scratch) = refs
        *scratch, value_grad, second_grad, second_bias_grad, first_grad, first_bias_grad = scratch
        sums = (value_grad, second_grad, second_bias_grad, first_grad, first_bias_grad)
    else:
        dx_near, dx_far, value_grad, random_outs = *refs[:3], refs[3 : 3 + random_parts]
        *scratch, random_grad = refs[3 + random_parts :]
        sums = (value_grad, random_grad)
    whole, dx, *rest = scratch
    rows, d_mixed = rest[:3], rest[3:6]
    d_values = rest[6]
    heads = near.shape[1] // HD
    value = diagonal(value)
    if level == 0:
        first = diagonal(first)
    load_groups(counts, y, near, far, whole, rows)
    load_groups(counts, y, d_near, d_far, whole, d_mixed)
    for s in sums:
        s[...] = jnp.zeros_like(s)
    for k, span in enumerate((LA, LB, LC)):
        values = mm(rows[k][...], value).astype(bf16)
        d_values[:span, :] = jnp.zeros((span, heads * HD), f32)
        for t in score_tiles(span):
            x = rows[k][t, :]
            act = None
            if level == 0:
                act, slope = gelu_both(mm(x, first) + first_bias[...])
                act = act.astype(bf16)
                d_act = None
            dm = d_mixed[k][t, :]
            for h in range(heads):
                p = soft(level, h, act, scalars[1 + k], span, second, second_bias, random, t)
                dm_h = only_head(dm, h)
                dp = mm_nt(dm_h, values)
                d_values[:span, :] += mm_tn(p.astype(bf16), dm_h)
                ds = p * (dp - jnp.sum(p * dp, axis=-1, keepdims=True))
                if level == 0:
                    low = ds.astype(bf16)
                    second_bias_grad[h : h + 1, :span] += jnp.sum(
                        low.astype(f32), axis=0, keepdims=True
                    )
                    second_grad[:, :span] += mm_tn(only_head(act, h), low)
                    term = only_head(mm_nt(low, second[:, :span]), h)
                    d_act = term if d_act is None else d_act + term
                else:
                    random_grad[h, t, :span] += ds
            if level == 0:
                d_pre = (d_act * slope).astype(bf16)
                first_bias_grad[...] += jnp.sum(d_pre.astype(f32), axis=0, keepdims=True)
                first_grad[...] += mm_tn(x, d_pre)
                dx[t, :] = mm_nt(d_pre, first)
        d_low = d_values[:span, :].astype(bf16)
        value_grad[...] += mm_tn(rows[k][...], d_low)
        back = mm_nt(d_low, value)
        if level == 0:
            back = back + dx[:span, :]
        d_mixed[k][...] = back.astype(bf16)
    store_groups(counts, y, d_mixed, whole, dx_near, dx_far)
    if level == 0:
        packed = pack_grads(
            heads, 2 * pack_own.shape[0], value_high, value_grad, second_grad, second_bias_grad, first_grad,
            first_bias_grad,
        )
        for side, out in enumerate((pack_own, pack_other)):
            half = out.shape[1] - 16
            pick = wide_rows((out.shape[0], half), heads, scalars[6], scalars[5] ^ side)
            rest, last = (
                mm(pick, part).astype(bf16).reshape(out.shape[0], half, -1) for part in packed
            )
            out[:, :half, :] = rest
            out[:, half:, :] = jnp.zeros((out.shape[0], 16, D), bf16)
            for i in range(half // 16):
                part = slice(i * 128, (i + 1) * 128)
                out[:, half:, part] = last[:, i * 16 : (i + 1) * 16, :]
    if level == 1 and random_parts == 1:
        random_outs[0][...] = random_grad[...].astype(bf16)
    elif level == 1:
        n, lines = random_outs[0].shape[0], random_outs[0].shape[1] // heads
        for side, out in enumerate(random_outs):
            for i in range(n):
                wide = 2 * (scalars[6] ^ i) + (scalars[5] ^ side)
                at = pl.ds(pl.multiple_of(wide * lines, 16), lines)
                for h in range(heads):
                    out[i, h * lines : (h + 1) * lines, :] = random_grad[h, at, :].astype(bf16)


def per_device(
    links,
    tokens_a,
    tokens_b,
    tokens_c,
    lengths_a,
    lengths_b,
    lengths_c,
    cotan_a,
    cotan_b,
    cotan_c,
    ln_gain,
    ln_bias,
    row_bias,
    out_weight,
    up_weight,
    up_bias,
    down_weight,
    synth_first,
    synth_first_bias,
    synth_second,
    synth_second_bias,
    random_scores,
    value_weight,
):
    counts = (tokens_a.shape[0], tokens_b.shape[0], tokens_c.shape[0])
    starts = (0, counts[0], counts[0] + counts[1])
    rows = sum(counts)
    heads = synth_first.shape[0]
    z, x, y, c = links.places()
    nz, n_wide = links.nz, links.n_wide
    chips = 2 * nz
    cols = heads * HD
    out_rows, ff_rows = out_weight.shape[1], up_weight.shape[1]
    size = ff_rows // 2
    units = chips * size
    lead = 16
    half_out = -(-out_rows // 2)
    aligned = size % 16 == 0
    n = 4
    scalars = jnp.stack([y, lengths_a[0], lengths_b[0], lengths_c[0], c, x, z]).astype(jnp.int32)

    def misc_halves(level):
        high = up_bias[level].astype(bf16)
        low = (up_bias[level] - high.astype(f32)).astype(bf16)
        found = []
        for side in range(2):
            w = out_weight[level, side * half_out : (side + 1) * half_out]
            part = slice(side * size, (side + 1) * size)
            line = jnp.pad(jnp.concatenate([high[part], low[part]])[None], ((0, 0), (0, D - ff_rows)))
            w = jnp.pad(w, ((0, half_out - w.shape[0]), (0, 0)))
            found.append(
                jnp.pad(jnp.concatenate([w, line], axis=0), ((0, lead - half_out - 1), (0, 0)))
            )
        return jnp.stack(found)

    misc = jnp.stack([misc_halves(level) for level in range(LAYERS)])
    tokens = (tokens_a, tokens_b, tokens_c, cotan_a, cotan_b, cotan_c)
    wide, half = lead + size, lead + 3 * size
    if aligned:
        (mine,) = lay_out(pack_rows_kernel, [2 * rows], tokens, len(tokens))
        first_rows, rest_rows = lay_out(
            partial(pack_weights_kernel, size),
            [2 * wide, 2 * half],
            (misc, up_weight, down_weight),
            12,
        )
    else:
        mine = jnp.concatenate(tokens, axis=0)
        parts = [slice(0, size), slice(size, 2 * size)]
        first_rows = jnp.concatenate(
            [v for k, p in enumerate(parts) for v in (misc[0, k], up_weight[0, p])]
        )
        rest_rows = jnp.concatenate(
            [
                v
                for k, p in enumerate(parts)
                for v in (misc[1, k], down_weight[0, p], up_weight[1, p], down_weight[1, p])
            ]
        )
    peer = links.swap(mine, c=1)
    first_rows, rest_rows = first_rows[None], rest_rows[None]
    first_got = links.swap(first_rows, z=1)
    rest_got = links.swap(rest_rows, z=1)

    def block_lines(block):
        return block * cols + jnp.arange(cols)

    wanted = jnp.concatenate([block_lines(links.nc * y + c), block_lines(links.nc * (1 - y) + c)])
    their_wanted = jnp.concatenate(
        [block_lines(links.nc * y + 1 - c), block_lines(links.nc * (1 - y) + 1 - c)]
    )

    def misc_numbers(core):
        iz, ix, iy = z ^ jnp.arange(nz), x ^ jnp.arange(2), y ^ jnp.arange(2)
        device = links.number(iz[:, None, None], ix[None, :, None], iy[None, None, :], core)
        i = jnp.arange(lead)
        a_rows = jnp.where(i < half_out, i, -1)
        b_rows = jnp.where(i < out_rows - half_out, half_out + i, -1)
        found = []
        for side, lines in ((0, a_rows), (1, a_rows), (2, b_rows), (3, b_rows)):
            at = device[:, :, side].T if side < 2 else device[:, side - 2, :].T
            found.append(jnp.where(lines < 0, -1, at[..., None] * out_rows + lines).reshape(-1))
        return jnp.concatenate(found)

    own_numbers, peer_numbers = misc_numbers(c), misc_numbers(1 - c)
    near_pick = (wanted[:, None] == own_numbers[None, :]).astype(bf16)
    far_pick = (wanted[:, None] == peer_numbers[None, :]).astype(bf16)
    their_pick = (their_wanted[:, None] == own_numbers[None, :]).astype(bf16)
    pick_cols = (jnp.arange(D)[:, None] == wanted[None, :]).astype(bf16)
    places = jnp.concatenate([wanted, their_wanted])
    place_cols = (places[:, None] == jnp.arange(D)[None, :]).astype(bf16)

    first_bias = synth_first_bias.reshape(1, cols)
    second = synth_second.reshape(cols, LC)
    values = [value_weight[level].reshape(cols, HD) for level in range(LAYERS)]
    first = synth_first.reshape(cols, HD)
    head_weights = [
        (first, first_bias, second, synth_second_bias, first_bias, values[0]),
        (first_bias, first_bias, first_bias, first_bias, random_scores, values[1]),
    ]

    def line(v, level, which):
        return v[level, which][None]

    chip_rows = 2 * rows
    row_low, row_high = ((chip_rows, D), bf16), ((chip_rows, D), f32)
    head_low, vector = ((chip_rows, cols), bf16), ((1, D), f32)
    hidden_low = ((n, chip_rows, units), bf16)
    groups = [pltpu.VMEM((4 * k, cols), bf16) for k in counts]
    group_pair = pltpu.VMEM((2, chip_rows, cols), bf16)

    def refs(blocks, at, length):
        if aligned:
            return list(blocks), at
        return [b[:, at : at + length].reshape(-1, D) for b in blocks], None

    def synthesis(level, own, got, *wait):
        return stage(
            4.5 if level == 0 else 2.3,
            partial(synth_kernel, level, counts),
            [head_low] * 2,
            (scalars, own, got, *head_weights[level]),
            scratch=[group_pair, *groups, *groups],
            smem=1,
            wait=wait,
        )

    def pick(blocks, *wait):
        blocks, at = refs(blocks, 0, lead)
        out = ((2 * cols, D), bf16)
        mine, theirs = stage(
            1.4,
            partial(pick_kernel, at, lead),
            [out, out],
            (near_pick, their_pick, *blocks),
            wait=wait,
        )
        return mine, links.swap(theirs, c=1)

    def join(near, far, mine, got):
        part, weight = stage(
            0.6,
            join_kernel,
            [row_low, ((2 * cols, D), bf16)],
            (near, far, mine, got),
            wait=[space(mine)],
        )
        return part, links.swap(part, c=1), weight

    def ffn_up(level, rows_in, part, got, ups, miscs, *wait):
        ups, at = refs(ups, lead if level == 0 else 0, size)
        miscs, misc_at = refs(miscs, 0, lead)
        return stage(
            3.6,
            partial(ffn_up_kernel, n, at, misc_at, size, lead, half_out),
            [row_high, row_low, hidden_low, hidden_low],
            (
                rows_in,
                part,
                got,
                line(row_bias, level, 0),
                line(ln_gain, level, 1),
                line(ln_bias, level, 1),
                *ups,
                *miscs,
            ),
            wait=[space(part), *wait],
        )

    def ffn_down(level, hidden, downs, *wait):
        downs, at = refs(downs, lead if level == 0 else size, size)
        (ffn,) = stage(1.6, partial(ffn_down_kernel, n, at, size), [row_low], (hidden, *downs), wait=wait)
        return ffn, links.swap(ffn, c=1)

    gain, shift = line(ln_gain, 0, 0), line(ln_bias, 0, 0)
    token_rows, cotan_rows, own_first, far_first = stage(
        1.6,
        first_norm_kernel,
        [row_low, row_low, head_low, head_low],
        (scalars, mine, peer, gain, shift, pick_cols),
        smem=1,
    )
    got_first = links.swap(far_first, y=1)
    def whole(length):
        return [(0, 0, length, 0, 0), (1, 0, length, 1, 0)]

    (first_rows,) = assemble(
        [first_rows, first_got], [((2, 2 * wide), whole(2 * wide))]
    )
    first_z = Spread(links, first_rows)
    first_z.start_z()
    mixed_first, mixed_far = synthesis(0, own_first, got_first, space(own_first))
    mixed_got_first = links.swap(mixed_far, y=1)

    def pieces(start, length):
        return [
            (source, start + side * half, length, source, side * length)
            for source in range(2)
            for side in range(2)
        ]

    second_rows, last_rows = assemble(
        [rest_rows, rest_got],
        [((2, 2 * wide), pieces(0, wide)), ((2, 4 * size), pieces(wide, 2 * size))],
        [mixed_first],
    )
    second_z, last_z = Spread(links, second_rows), Spread(links, last_rows)
    second_z.start_z()
    (first_chunk,) = first_z.end_z([(0, wide, wide)], mixed_first)
    first_chunk.start_near()
    first_chunk.start_far()
    last_z.start_z(mixed_got_first)
    mine_first, got_weight = pick(first_chunk.blocks())
    (second_chunk,) = second_z.end_z([(0, wide, wide)], first_chunk.a, mixed_got_first)
    second_chunk.start_near()
    part, part_got, out_first = join(mixed_first, mixed_got_first, mine_first, got_weight)
    (last_chunk,) = last_z.end_z([(0, 2 * size, 2 * size)], part)
    second_chunk.start_far()
    last_chunk.start_near()
    resid_first, normed_first, *saved_first = ffn_up(
        0, token_rows, part, part_got, first_chunk.blocks(), first_chunk.blocks()
    )
    ffn, ffn_got = ffn_down(0, saved_first[0], second_chunk.blocks())

    rows_second, own_second, far_second = stage(
        1.1,
        next_norm_kernel,
        [row_high, head_low, head_low],
        (
            resid_first,
            ffn,
            ffn_got,
            line(row_bias, 0, 1),
            line(ln_gain, 1, 0),
            line(ln_bias, 1, 0),
            pick_cols,
        ),
        wait=[space(ffn)],
    )
    got_second = links.swap(far_second, y=1)
    mine_second, got_weight = pick(second_chunk.blocks(), rows_second)
    mixed_second, mixed_far = synthesis(1, own_second, got_second, space(own_second))
    mixed_got_second = links.swap(mixed_far, y=1)
    last_chunk.start_far(mixed_got_second)
    part, part_got, out_second = join(mixed_second, mixed_got_second, mine_second, got_weight)
    resid_second, normed_second, *saved_second = ffn_up(
        1, rows_second, part, part_got, last_chunk.blocks(), second_chunk.blocks()
    )

    def ffn_back(level, grad_rows, normed, saved, ups, downs, *wait):
        ups, up_at = refs(ups, lead if level == 0 else 0, size)
        downs, down_at = refs(downs, lead if level == 0 else size, size)
        out = ((chips, 2 * size, D) if aligned else (2, units, D), bf16)
        outs = [out] * n
        if aligned and level == 1:
            part = ((chips, size, D), bf16)
            outs = [out, part, out, out, part]
        d_normed, bias_grad, hidden_bias, *terms = stage(
            6.5,
            partial(ffn_back_kernel, n, up_at, down_at, size),
            [row_low, vector, ((n, units), f32)] + outs,
            (grad_rows, normed, *saved, *ups, *downs),
            wait=wait,
        )
        if not aligned:
            terms = [t.reshape(2, chips, size, D) for t in terms]
            parts = list(terms[1])
            terms = [jnp.concatenate(list(t), axis=1) for t in terms]
            if level == 1:
                terms = [terms[0], parts[0], *terms[2:], parts[1]]
        return d_normed, links.swap(d_normed, c=1), bias_grad, hidden_bias, terms

    def join_back(
        level, grad_rows, part, got, resid, weight, near, far, hidden_bias, *wait, earlier=()
    ):
        misc_out = ((n * chips * lead, D), bf16)
        far_out = (((1 + len(earlier)) * n * chips * lead, D), bf16)
        d_resid, d_own, d_far, gain, shift, bias, out_near, out_far = stage(
            3.2,
            partial(join_back_kernel, lead, half_out, size, len(earlier)),
            [row_high, head_low, head_low, vector, vector, vector, misc_out, far_out],
            (
                grad_rows,
                part,
                got,
                resid,
                line(ln_gain, level, 1),
                weight,
                near,
                far,
                near_pick,
                far_pick,
                hidden_bias,
                *earlier,
            ),
            scratch=[pltpu.VMEM((chip_rows, D), bf16)],
            wait=wait,
        )
        return d_resid, d_own, links.swap(d_far, y=1), (gain, shift, bias), out_near, out_far

    lines = LC // n_wide
    random_parts = 2 if lines % 16 == 0 else 1
    lines_each = -(-heads * HD // n_wide // 16) * 16

    def synth_back(level, own, got, d_own, d_got, value_high=(), wait=()):
        square = pltpu.VMEM((cols, cols), f32)
        scratch = [group_pair, pltpu.VMEM((LC, cols), f32), *groups, *groups]
        scratch = scratch + [pltpu.VMEM((LC, cols), f32)]
        if level == 0:
            outs = [((nz, lines_each + 16, D), bf16)] * 2
            scratch = scratch + [
                square,
                pltpu.VMEM((cols, LC), f32),
                pltpu.VMEM((8, LC), f32),
                square,
                pltpu.VMEM((1, cols), f32),
            ]
        else:
            random_out = (nz, heads * lines, LC) if random_parts == 2 else (heads, LC, LC)
            outs = [((cols, cols), f32)] + [(random_out, bf16)] * random_parts
            scratch = scratch + [pltpu.VMEM((heads, LC, LC), f32)]
        dx_own, dx_far, *found = stage(
            10.4 if level == 0 else 4.6,
            partial(synth_back_kernel, level, counts, random_parts),
            [head_low] * 2 + outs,
            (scalars, own, got, d_own, d_got, *head_weights[level], *value_high),
            scratch=scratch,
            smem=1,
            wait=wait,
        )
        return dx_own, links.swap(dx_far, y=1), links.swap(dx_own, c=1), found

    d_normed, d_got, ffn_bias_second, hidden_bias, terms_second = ffn_back(
        1, cotan_rows, normed_second, saved_second, last_chunk.blocks(), last_chunk.blocks()
    )
    x_near = links.swap(terms_second[3], x=1)
    y_down = links.swap(terms_second[1], y=1)
    d_resid, d_own, d_mixed_got, stats_second, near_second, far_second_out = join_back(
        1, cotan_rows, d_normed, d_got, resid_second, out_second, mixed_second, mixed_got_second,
        hidden_bias, space(d_normed),
    )
    y_up = links.swap(after(terms_second[4], d_mixed_got), y=1)
    dx_own, dx_got, dx_peer, found_second = synth_back(
        1, own_second, got_second, d_own, d_mixed_got, wait=[space(d_own)]
    )
    dx_peer_got = links.swap(dx_got, c=1)
    spaced = space(dx_own)
    send, b_keep = fold_first(terms_second[2], [x_near], dx_got, spaced)
    y_far = links.swap(send, y=1)
    send, a_keep = fold_first(terms_second[0], [y_down, y_up], dx_got, spaced)
    x_far = links.swap(send, x=1)
    grad_rows, *stats_rows_second = stage(
        1.5,
        rows_back_kernel,
        [row_high, vector, vector],
        (
            d_resid, dx_own, dx_got, dx_peer, dx_peer_got, place_cols, rows_second,
            line(ln_gain, 1, 0),
        ),
        wait=[a_keep, b_keep, space(dx_got, spaced)],
    )
    if random_parts == 2:
        x_random = links.swap(found_second[2], x=1)

    wait = []
    if random_parts == 2:
        x_random = after(x_random, grad_rows)
        wait.append(x_random)

    d_normed, d_got, ffn_bias_first, hidden_bias, terms_first = ffn_back(
        0, grad_rows, normed_first, saved_first, first_chunk.blocks(), second_chunk.blocks(),
        *wait,
    )
    d_resid, d_own, d_mixed_got, stats_first, near_first, far_out = join_back(
        0, grad_rows, d_normed, d_got, resid_first, out_first, mixed_first, mixed_got_first,
        hidden_bias, space(d_normed), earlier=[far_second_out],
    )
    far_out = links.swap(far_out, c=1)
    second_fold = Fold(links, [(a_keep, x_far), (b_keep, y_far)], d_own, halves=True)
    second_fold.start()
    if aligned:
        terms_first = stage(
            1.5,
            misc_kernel,
            [((chips, 2 * size + 2 * lead, D), bf16)] * n,
            (near_first, near_second, far_out, *terms_first),
        )
    else:
        misc = [v.reshape(n, chips, lead, D) for v in (near_first, near_second)]
        got = list(far_out.reshape(2, n, chips, lead, D))
        misc = jnp.concatenate([a + b for a, b in zip(misc, got)], axis=2)
        terms_first = [jnp.concatenate([t, m], axis=1) for t, m in zip(terms_first, misc)]
    x_near = links.swap(terms_first[3], x=1)
    y_near = links.swap(after(terms_first[1], d_mixed_got), y=1)
    wait = []
    if random_parts == 2:
        random_fold = Fold(
            links, [(found_second[1], x_random)], second_fold.keep, halves=True
        )
        wait.append(random_fold.keep)
    dx_own, dx_got, dx_peer, found_first = synth_back(
        0, own_first, got_first, d_own, d_mixed_got, (found_second[0],),
        (second_fold.keep, terms_first[0], space(d_own), *wait),
    )
    spaced = space(dx_own)
    pack_own, pack_other = found_first
    second_last = second_fold.step(dx_own)
    if random_parts == 2:
        random_fold.start(second_last)
    send, b_keep = fold_first(terms_first[2], [x_near], dx_own, spaced, second_last)
    y_far = links.swap(after(send, y_near), y=1)
    send, a_keep = fold_first(terms_first[0], [y_near], b_keep, rest=[pack_other])
    x_far = links.swap(send, x=1)
    dx_peer_got = links.swap(after(dx_got, a_keep), c=1)
    *grad_parts, gain, shift = stage(
        1.7,
        partial(rows_last_kernel, counts),
        [((k, D), f32) for k in counts] + [vector, vector],
        (
            scalars, d_resid, dx_own, dx_got, dx_peer, dx_peer_got, place_cols, token_rows,
            line(ln_gain, 0, 0),
        ),
        scratch=[pltpu.VMEM((chip_rows, D), f32)],
        smem=1,
        wait=[a_keep, b_keep, space(a_keep)],
    )
    ffn, ffn_got = ffn_down(1, saved_second[0], last_chunk.blocks(), a_keep)
    out_parts = stage(
        1.0,
        partial(last_kernel, counts),
        [((k, D), bf16) for k in counts],
        (scalars, resid_second, ffn, ffn_got, line(row_bias, LAYERS - 1, 1)),
        smem=1,
    )

    (summed,) = stage(
        1.0,
        stats_kernel,
        [((LAYERS * 6, D), f32)],
        [
            row
            for inner, (gain_second, shift_second, bias), ffn_bias in (
                ((gain, shift), stats_first, ffn_bias_first),
                (stats_rows_second, stats_second, ffn_bias_second),
            )
            for row in (inner[0], gain_second, inner[1], shift_second, bias, ffn_bias)
        ],
    )

    pack_at = a_keep.shape[1]
    first_fold = Fold(
        links, [(a_keep, x_far), (b_keep, y_far), (pack_own, x_far, pack_at)]
    )
    first_fold.start()
    summed = links.total(summed, first_fold.keep, first_fold.keep)
    summed = summed.reshape(LAYERS, 6, D)
    if random_parts == 2:
        random_fold.step(a_keep)
        random = random_fold.finish(first_fold.keep)
    else:
        random = found_second[1].reshape(heads, n_wide, lines, LC)
        random = lax.psum_scatter(random, "wide", scatter_dimension=1, tiled=False).astype(f32)
    if aligned and nz <= 4:
        weight = ((LAYERS, 2 * size, D), f32)
        folds = (first_fold, second_fold)
        down_grad, up_grad, misc, pack = stage(
            1.0,
            partial(finish_kernel, size, lead, len(first_fold.gots)),
            [weight, weight, ((LAYERS, 2, lead, D), f32), (pack_own.shape[1:], f32)],
            [f.keep for f in folds] + first_fold.gots + second_fold.gots,
        )
    else:
        found, layer = first_fold.finish(), second_fold.finish().reshape(2, -1, D)
        found, pack = found[: 2 * pack_at].reshape(2, -1, D), found[2 * pack_at :]
        found = [found, layer]
        down_grad = jnp.stack([v[:, :size].reshape(-1, D) for v in found])
        up_grad = jnp.stack([v[:, size : 2 * size].reshape(-1, D) for v in found])
        misc = found[0][:, 2 * size :].reshape(2, LAYERS, lead, D)
        misc = jnp.moveaxis(misc, 0, 1)
    pack_rows = heads * HD // n_wide
    rest = pack[:pack_rows].reshape(heads, HD // n_wide, D)
    first_rows = HD // n_wide
    bias_lines = [
        pack[lines_each + k % 16, 128 * (k // 16) : 128 * (k // 16) + lines]
        for k in range(0, pack_rows, first_rows)
    ]
    out_grad = misc[:, :, :half_out].reshape(LAYERS, -1, D)[:, :out_rows]
    bias_grad = misc[:, :, half_out, :size].reshape(LAYERS, -1)
    return (
        *out_parts,
        *grad_parts,
        summed[:, 0:2],
        summed[:, 2:4],
        summed[:, 4:6],
        out_grad,
        up_grad,
        bias_grad,
        down_grad,
        rest[:, :, LC : LC + HD],
        rest[:, :, LC + 128 + HD],
        rest[:, :, :LC],
        jnp.stack(bias_lines),
        random.reshape(heads, lines, LC),
        jnp.stack([rest[:, :, LC + HD : LC + 128], rest[:, :, LC + 128 : LC + 128 + HD]]),
    )


def solution(mesh):
    placed = (
        P(("wide", "head"), None),
        P(("wide", "head"), None),
        P(("wide", "head"), None),
        P("wide"),
        P("wide"),
        P("wide"),
        P(("wide", "head"), None),
        P(("wide", "head"), None),
        P(("wide", "head"), None),
        P(),
        P(),
        P(),
        P(None, ("wide", "head"), None),
        P(None, ("wide", "head"), None),
        P(None, ("wide", "head")),
        P(None, ("wide", "head"), None),
        P("head", None, None),
        P("head", None),
        P("head", None, None),
        P("head", None),
        P("head", None, None),
        P(None, "head", None, None),
    )
    return jax.shard_map(
        partial(per_device, Links(mesh.shape["wide"], mesh.shape["head"])),
        mesh=mesh,
        in_specs=placed,
        out_specs=(
            P(("wide", "head"), None),
            P(("wide", "head"), None),
            P(("wide", "head"), None),
            P(("wide", "head"), None),
            P(("wide", "head"), None),
            P(("wide", "head"), None),
            P(),
            P(),
            P(),
            P(None, ("wide", "head"), None),
            P(None, ("wide", "head"), None),
            P(None, ("wide", "head")),
            P(None, ("wide", "head"), None),
            P("head", "wide", None),
            P("head", "wide"),
            P("head", "wide", None),
            P("head", "wide"),
            P("head", "wide", None),
            P(None, "head", "wide", None),
        ),
        check_vma=False,
    )
```

```python
import math
from functools import partial

import jax
import jax.numpy as jnp
import numpy as np
from jax import lax
from jax.experimental import pallas as pl
from jax.experimental.pallas import tpu as pltpu
from jax.sharding import PartitionSpec as P

HD = 64
LC = 512
LA = 128
LB = 256
LAYERS = 2
D = 768

EPSILON = 1e-05
MASKED_SCORE = -1e30
AXES = ("wide", "head")
ROW_TILE = 112
SCORE_TILE = 256
SPARE = 8 * 1024 * 1024
FLOPS_PER_US = 1.1e9
SPACE_US = 12.0
f32 = jnp.float32
bf16 = jnp.bfloat16


class Links:
    def __init__(self, n_wide, n_head):
        self.nx, self.nc = 2, 2
        self.nz, self.ny = n_wide // 2, n_head // 2
        self.n_wide = n_wide
        self.bits = [1 << k for k in range(self.nz.bit_length() - 1)]

    def number(self, z, x, y, c):
        return ((z * self.nx + x) * self.ny + y) * self.nc + c

    def places(self):
        wide, head = lax.axis_index("wide"), lax.axis_index("head")
        return wide // self.nx, wide % self.nx, head // self.nc, head % self.nc

    def swap(self, v, z=0, x=0, y=0, c=0):
        pairs = [
            (self.number(i ^ z, j ^ x, k ^ y, m ^ c), self.number(i, j, k, m))
            for i, j, k, m in np.ndindex(self.nz, self.nx, self.ny, self.nc)
        ]
        return lax.ppermute(v, AXES, pairs)

    def total(self, v, *waits):
        steps = [{"z": bit} for bit in self.bits] + [{"x": 1}, {"y": 1}]
        for k, step in enumerate(steps):
            got = self.swap(v, **step)
            if k + len(waits) >= len(steps):
                got = after(got, waits[k + len(waits) - len(steps)])
            v = v + got
        return v


def nothing_kernel(*refs):
    pass


def after(v, *others):
    return pl.pallas_call(
        nothing_kernel,
        out_shape=jax.ShapeDtypeStruct(v.shape, v.dtype),
        in_specs=[pl.BlockSpec(memory_space=pl.ANY)] * (1 + len(others)),
        out_specs=pl.BlockSpec(memory_space=pl.ANY),
        input_output_aliases={0: 0},
        compiler_params=pltpu.CompilerParams(vmem_limit_bytes=1 << 20),
        cost_estimate=pl.CostEstimate(flops=1, bytes_accessed=0, transcendentals=0),
    )(v, *others)


class Spread:
    def __init__(self, links, v):
        self.links, self.v = links, v

    def start_z(self, *wait):
        for bit in self.links.bits[1:-1]:
            self.v = jnp.concatenate([self.v, self.links.swap(self.v, z=bit)], axis=0)
        v = after(self.v, *wait) if wait else self.v
        self.got = self.links.swap(v, z=self.links.bits[-1])

    def end_z(self, cuts, *wait):
        n = self.v.shape[0]
        plans = []
        for a, b, rows in cuts:
            for start in (a, b):
                plans.append(((2 * n, rows), [(0, start, rows, 0, 0), (1, start, rows, n, 0)]))
        halves = assemble([self.v, self.got], plans, wait)
        return [Near(self.links, a, b) for a, b in zip(halves[::2], halves[1::2])]


class Near:
    def __init__(self, links, a, b):
        self.links, self.a, self.b = links, a, b

    def start_near(self, *wait):
        a, b = (after(v, *wait) if wait else v for v in (self.a, self.b))
        self.got_a, self.got_b = self.links.swap(a, x=1), self.links.swap(b, y=1)

    def start_far(self, *wait):
        n, rows = self.a.shape[:2]
        wait = (*wait, space(self.a))
        plan = [
            ((2 * n, rows), [(k, 0, rows, 0, 0), (k + 1, 0, rows, n, 0)]) for k in (0, 2)
        ]
        self.a, self.b = assemble([self.a, self.got_a, self.b, self.got_b], plan, wait)
        self.far_a, self.far_b = self.links.swap(self.a, y=1), self.links.swap(self.b, x=1)

    def blocks(self):
        return [self.a, self.far_a, self.b, self.far_b]


def fold_first(own, gots, *wait, rest=()):
    n, rows, width = own.shape[0] // 2, own.shape[1], own.shape[2]
    more = sum(v.shape[1] for v in rest)
    if len(gots) > 1 and gots[0].shape[1] % 16 != 0:
        gots = [jnp.concatenate(gots, axis=1)]
    return stage(
        1.0,
        partial(fold_first_kernel, len(gots)),
        [((n, rows + more, width), bf16), ((n, rows, width), bf16)],
        (own, *gots, *rest),
        wait=wait,
    )


class Fold:
    def __init__(self, links, pairs, *wait, halves=False):
        self.links = links
        starts = [pair[2] if len(pair) > 2 else 0 for pair in pairs]
        flat = [v for pair in pairs for v in pair[:2]]
        n = links.nz if links.nz <= 4 and not halves else 2
        rows = sum(pair[0].shape[1] for pair in pairs)
        shape = (links.nz // n, rows, flat[0].shape[2])
        self.keep, *self.sends = stage(
            1.0,
            partial(fold_second_kernel, n, starts),
            [(shape, f32)] + [(shape, bf16)] * (n - 1),
            flat,
            wait=wait,
        )
        self.bits = list(reversed(links.bits))[1:] if n == 2 else []

    def start(self, *wait, chain=False):
        sends = [after(v, *wait) if wait else v for v in self.sends]
        if len(sends) == 1:
            self.gots = [self.links.swap(sends[0], z=self.links.nz // 2)]
        else:
            self.gots = []
            for k, v in enumerate(sends):
                v = after(v, self.gots[0]) if chain and k > 0 else v
                self.gots.append(self.links.swap(v, z=k + 1))

    def step(self, *wait):
        bit = self.bits.pop(0)
        shape = (bit, *self.keep.shape[1:])
        send, self.keep = stage(
            1.0, fold_z_kernel, [(shape, bf16), (shape, f32)], (self.keep, *self.gots), wait=wait
        )
        self.gots = [self.links.swap(send, z=bit)]
        return self.keep

    def steps(self):
        while self.bits:
            self.step()
        return self.keep, self.gots

    def finish(self, *wait):
        keep, gots = self.steps()
        (total,) = stage(
            1.0, fold_last_kernel, [(keep.shape, f32)], (keep, *gots), wait=wait
        )
        return total[0]


def stage(us, kernel, outs, args, scratch=(), smem=0, wait=()):
    count = len(args)
    spaces = [pltpu.SMEM] * smem + [pltpu.VMEM] * (count - smem) + [pl.ANY] * len(wait)
    size = sum(a.size * a.dtype.itemsize for a in args[smem:])
    size = size + sum(math.prod(s) * jnp.dtype(d).itemsize for s, d in outs)
    held = sum(math.prod(s.shape) * jnp.dtype(s.dtype).itemsize for s in scratch)

    def body(*refs):
        kernel(*refs[:count], *refs[count + len(wait) :])

    return pl.pallas_call(
        body,
        out_shape=[jax.ShapeDtypeStruct(s, d) for s, d in outs],
        in_specs=[pl.BlockSpec(memory_space=s) for s in spaces],
        out_specs=[pl.BlockSpec(memory_space=pltpu.VMEM) for _ in outs],
        scratch_shapes=list(scratch),
        compiler_params=pltpu.CompilerParams(vmem_limit_bytes=size + held + SPARE),
        cost_estimate=pl.CostEstimate(
            flops=int(us * FLOPS_PER_US), bytes_accessed=0, transcendentals=0
        ),
    )(*args, *wait)


def space_kernel(out):
    out[...] = jnp.zeros_like(out)


def space(*deps):
    return stage(SPACE_US, space_kernel, [((8, 128), f32)], (), wait=deps)[0]


def mm(a, b):
    return lax.dot_general(a, b, (((1,), (0,)), ((), ())), preferred_element_type=f32)


def mm_nt(a, b):
    return lax.dot_general(a, b, (((1,), (1,)), ((), ())), preferred_element_type=f32)


def mm_tn(a, b):
    return lax.dot_general(a, b, (((0,), (0,)), ((), ())), preferred_element_type=f32)


def one_hot(mask):
    return mask.astype(f32).astype(bf16)


def tiles(rows):
    return [pl.ds(i, ROW_TILE) for i in range(0, rows, ROW_TILE)]


def centre(v):
    middle = jnp.mean(v, axis=-1, keepdims=True)
    centred = v - middle
    scale = lax.rsqrt(jnp.mean(centred * centred, axis=-1, keepdims=True) + EPSILON)
    return centred * scale, scale


def norm_back(v, gain, d_out):
    unit, scale = centre(v)
    inner = d_out * gain
    flat = jnp.mean(inner, axis=-1, keepdims=True)
    along = jnp.mean(inner * unit, axis=-1, keepdims=True)
    d_rows = scale * (inner - flat - unit * along)
    return d_rows, jnp.sum(d_out * unit, axis=0, keepdims=True), jnp.sum(d_out, 0, keepdims=True)


def gelu_both(v):
    k = math.sqrt(2.0 / math.pi)
    square = v * v
    t = jnp.tanh(k * v * (1.0 + 0.044715 * square))
    half = 0.5 * (1.0 + t)
    slope = half + 0.5 * v * (1.0 - t * t) * (k * (1.0 + 3 * 0.044715 * square))
    return v * half, slope


def move(moves, sems):
    copies = [pltpu.make_async_copy(a, b, sems.at[i]) for i, (a, b) in enumerate(moves)]
    for copy in copies:
        copy.start()
    for copy in copies:
        copy.wait()


def pack_rows_kernel(*refs):
    *parts, rows, sems = refs
    moves, start = [], 0
    for ref in parts:
        moves.append((ref, rows.at[pl.ds(start, ref.shape[0])]))
        start = start + ref.shape[0]
    move(moves, sems)


def pack_weights_kernel(size, misc, up, down, first, rest, sems):
    lead = misc.shape[2]
    wide, narrow = lead + size, size
    half = wide + 2 * narrow
    moves = []
    for side in range(2):
        part = pl.ds(side * size, size)
        moves.append((misc.at[0, side], first.at[pl.ds(side * wide, lead)]))
        moves.append((up.at[0, part], first.at[pl.ds(side * wide + lead, size)]))
        at = side * half
        moves.append((misc.at[1, side], rest.at[pl.ds(at, lead)]))
        moves.append((down.at[0, part], rest.at[pl.ds(at + lead, size)]))
        moves.append((up.at[1, part], rest.at[pl.ds(at + wide, size)]))
        moves.append((down.at[1, part], rest.at[pl.ds(at + wide + narrow, size)]))
    move(moves, sems)


def lay_out(kernel, outs, args, copies, wait=()):
    def body(*refs):
        kernel(*refs[: len(args)], *refs[len(args) + len(wait) :])

    return pl.pallas_call(
        body,
        out_shape=[jax.ShapeDtypeStruct((k, D), bf16) for k in outs],
        in_specs=[pl.BlockSpec(memory_space=pltpu.HBM)] * len(args)
        + [pl.BlockSpec(memory_space=pl.ANY)] * len(wait),
        out_specs=[pl.BlockSpec(memory_space=pltpu.VMEM)] * len(outs),
        scratch_shapes=[pltpu.SemaphoreType.DMA((copies,))],
        compiler_params=pltpu.CompilerParams(vmem_limit_bytes=SPARE),
    )(*args, *wait)


def assemble_kernel(plans, n, *refs):
    for out, pieces in zip(refs[n:], plans):
        for source, start, rows, place, row in pieces:
            piece = refs[source][:, start : start + rows, :]
            out[place : place + piece.shape[0], row : row + rows, :] = piece


def assemble(sources, outs, wait=()):
    whole = all(
        start % 16 == 0 and rows % 16 == 0 and row % 16 == 0
        for _, pieces in outs
        for _, start, rows, _, row in pieces
    )
    if whole:
        plans = [pieces for _, pieces in outs]
        shapes = [((*shape, D), bf16) for shape, _ in outs]
        return stage(
            0.7, partial(assemble_kernel, plans, len(sources)), shapes, sources, wait=wait
        )
    found = []
    for shape, pieces in outs:
        columns = {}
        for source, start, rows, place, row in sorted(pieces, key=lambda p: (p[4], p[3])):
            columns.setdefault(row, []).append(sources[source][:, start : start + rows])
        columns = [jnp.concatenate(v, axis=0) for _, v in sorted(columns.items())]
        found.append(jnp.concatenate(columns, axis=1))
    return found


def first_norm_kernel(scalars, mine, peer, gain, shift, pick, tokens, cotans, own, far):
    c = scalars[4]
    rows, cols = mine.shape[0] // 2, own.shape[1]
    for ref, core in ((mine, c), (peer, 1 - c)):
        for i in range(0, rows, ROW_TILE):
            t = pl.ds(pl.multiple_of(core * rows + i, 16), ROW_TILE)
            v = ref[i : i + ROW_TILE, :]
            tokens[t, :] = v
            cotans[t, :] = ref[rows + i : rows + i + ROW_TILE, :]
            unit, _ = centre(v.astype(f32))
            normed = (unit * gain[...] + shift[...]).astype(bf16)
            picked = mm(normed, pick[...]).astype(bf16)
            own[t, :] = picked[:, :cols]
            far[t, :] = picked[:, cols:]


def next_norm_kernel(resid, part, got, bias, gain, shift, pick, rows, own, far):
    for t in tiles(resid.shape[0]):
        v = resid[t, :] + (part[t, :].astype(f32) + got[t, :].astype(f32)) + bias[...]
        rows[t, :] = v
        unit, _ = centre(v)
        normed = (unit * gain[...] + shift[...]).astype(bf16)
        picked = mm(normed, pick[...]).astype(bf16)
        own[t, :] = picked[:, : own.shape[1]]
        far[t, :] = picked[:, own.shape[1] :]


def pick_kernel(at, size, mine_pick, their_pick, *refs):
    blocks, (mine, theirs) = refs[:-2], refs[-2:]
    for pick, out in ((mine_pick, mine), (their_pick, theirs)):
        total = None
        for k, ref in enumerate(blocks):
            lines = block(ref, at, size)
            n = lines.shape[0]
            term = mm(pick[:, k * n : (k + 1) * n], lines)
            total = term if total is None else total + term
        out[...] = total.astype(bf16)


def join_kernel(near, far, mine, got, part, weight):
    cols = near.shape[1]
    weight[...] = (mine[...].astype(f32) + got[...].astype(f32)).astype(bf16)
    total = mm(near[...], weight[:cols, :]) + mm(far[...], weight[cols:, :])
    part[...] = total.astype(bf16)


def block(ref, start, rows):
    if start is None:
        return ref[...]
    return ref[:, start : start + rows, :].reshape(-1, D)


def line_mask(shape, lead, line, size):
    row = lax.broadcasted_iota(jnp.int32, shape, 0)
    unit = lax.broadcasted_iota(jnp.int32, shape, 1)
    return (row % lead == line) & (row // lead == unit // size)


def ffn_up_kernel(n, at, misc_at, size, lead, line, rows, part, got, bias, gain, shift, *refs):
    ups, miscs = refs[:n], refs[n : 2 * n]
    resid, normed, hidden, slope = refs[2 * n :]
    for t in tiles(rows.shape[0]):
        v = rows[t, :].astype(f32) + (part[t, :].astype(f32) + got[t, :].astype(f32)) + bias[...]
        resid[t, :] = v
        unit, _ = centre(v)
        normed[t, :] = (unit * gain[...] + shift[...]).astype(bf16)
    units = hidden.shape[2]
    lane = lax.broadcasted_iota(jnp.int32, (128, units), 0)
    column = lax.broadcasted_iota(jnp.int32, (128, units), 1)
    place = ((lane % size == column % size) & (lane < 2 * size)).astype(f32).astype(bf16)
    for k in range(n):
        lines = mm(block(miscs[k], misc_at, lead)[:, :128], place)
        lines = jnp.where(line_mask(lines.shape, lead, line, size), lines, 0.0)
        lines = jnp.sum(lines, axis=0, keepdims=True)
        value, grad = gelu_both(mm_nt(normed[...], block(ups[k], at, size)) + lines)
        hidden[k] = value.astype(bf16)
        slope[k] = grad.astype(bf16)


def ffn_down_kernel(n, at, size, hidden, *refs):
    downs, ffn = refs[:n], refs[n]
    total = None
    for k in range(n):
        term = mm(hidden[k], block(downs[k], at, size))
        total = term if total is None else total + term
    ffn[...] = total.astype(bf16)


def ffn_back_kernel(n, up_at, down_at, size, grad_rows, slope, *refs):
    ups, downs = refs[:n], refs[n : 2 * n]
    d_normed, bias_grad, hidden_bias, d_pre = refs[2 * n :]
    d_ffn = grad_rows[...].astype(bf16)
    total = None
    for k in range(n):
        d_hidden = mm_nt(d_ffn, block(downs[k], down_at, size))
        d_pre[k] = (d_hidden * slope[k].astype(f32)).astype(bf16)
        term = mm(d_pre[k], block(ups[k], up_at, size))
        total = term if total is None else total + term
    d_normed[...] = total.astype(bf16)
    bias_grad[...] = jnp.sum(d_ffn.astype(f32), axis=0, keepdims=True)
    for k in range(n):
        hidden_bias[k : k + 1, :] = jnp.sum(d_pre[k].astype(f32), axis=0, keepdims=True)


def ffn_terms_kernel(n, whole, size, grad_rows, normed, hidden, d_pre, *grads):
    d_ffn = grad_rows[...].astype(bf16)
    for k in range(n):
        down_grad = mm_tn(hidden[k], d_ffn).astype(bf16)
        up_grad = mm_tn(d_pre[k], normed[...]).astype(bf16)
        if whole:
            grads[k][0] = down_grad
            grads[k][1] = up_grad
        elif k == 1 and len(grads) > n:
            grads[1][...] = down_grad.reshape(-1, size, D)
            grads[n][...] = up_grad.reshape(-1, size, D)
        else:
            grads[k][:, :size, :] = down_grad.reshape(-1, size, D)
            grads[k][:, size:, :] = up_grad.reshape(-1, size, D)


def fold_first_kernel(count, own, *refs):
    gots, rest, (send, keep) = refs[:count], refs[count:-2], refs[-2:]
    n, start = send.shape[0], 0
    for got in gots:
        part = slice(start, start + got.shape[1])
        start = start + got.shape[1]
        for out, half in ((keep, slice(0, n)), (send, slice(n, 2 * n))):
            total = own[half, part, :].astype(f32) + got[half].astype(f32)
            out[:, part, :] = total.astype(bf16)
    for other in rest:
        send[:, start:, :] = other[...]


def misc_kernel(first, second, got, *refs):
    n = len(refs) // 2
    half = first.shape[0]
    for k, (source, out) in enumerate(zip(refs[:n], refs[n:])):
        chips, start = source.shape[:2]
        lead = (out.shape[1] - start) // 2
        out[:, :start, :] = source[...]
        part = slice(k * chips * lead, (k + 1) * chips * lead)
        for i, own in enumerate((first, second)):
            at = start + i * lead
            theirs = got[i * half + part.start : i * half + part.stop, :]
            total = own[part, :].astype(f32) + theirs.astype(f32)
            out[:, at : at + lead, :] = total.astype(bf16).reshape(chips, lead, D)


def fold_second_kernel(n, starts, *refs):
    count = len(refs) - n
    keep, sends = refs[count], refs[count + 1 :]
    at = 0
    for i, start in enumerate(starts):
        own, got = refs[2 * i], refs[2 * i + 1]
        lines, length = own.shape[0] // n, own.shape[1]
        rows, source = slice(at, at + length), slice(start, start + length)
        at = at + length
        for k in range(n):
            part = slice(k * lines, (k + 1) * lines)
            total = own[part].astype(f32) + got[part, source, :].astype(f32)
            if k == 0:
                keep[:, rows, :] = total
            else:
                sends[k - 1][:, rows, :] = total.astype(bf16)


def fold_z_kernel(own, got, send, keep):
    n = send.shape[0]
    keep[...] = own[:n] + got[:n].astype(f32)
    send[...] = (own[n:] + got[n:].astype(f32)).astype(bf16)


def fold_last_kernel(own, *refs):
    *gots, out = refs
    total = own[...]
    for got in gots:
        total = total + got[...].astype(f32)
    out[...] = total


def finish_kernel(size, lead, n, first, second, *refs):
    gots, (down, up, misc, pack) = (refs[:n], refs[n:-4]), refs[-4:]

    def total(own, gots):
        found = own[0]
        for got in gots:
            found = found + got[0].astype(f32)
        return found

    for level, own in enumerate((first, second)):
        found = total(own, gots[level])
        each = 2 * size + (2 * lead if level == 0 else 0)
        for side in range(2):
            at, part = side * each, slice(side * size, (side + 1) * size)
            down[level, part, :] = found[at : at + size]
            up[level, part, :] = found[at + size : at + 2 * size]
            if level == 0:
                for i in range(2):
                    start = at + 2 * size + i * lead
                    misc[i, side] = found[start : start + lead]
        if level == 0:
            pack[...] = found[2 * each :]


def stats_kernel(*refs):
    *rows, out = refs
    for k, row in enumerate(rows):
        out[k : k + 1, :] = row[...]


def last_kernel(counts, scalars, resid, part, got, bias, *outs):
    start = scalars[4] * sum(counts)
    for out, n in zip(outs, counts):
        t = pl.ds(pl.multiple_of(start, 16), n)
        v = resid[t, :] + (part[t, :].astype(f32) + got[t, :].astype(f32)) + bias[...]
        out[...] = v.astype(bf16)
        start = start + n


def rows_last_kernel(counts, scalars, *refs):
    *given, grad_a, grad_b, grad_c, gain_grad, shift_grad, rows = refs
    rows_back_kernel(*given, rows, gain_grad, shift_grad)
    start = scalars[4] * sum(counts)
    for out, n in zip((grad_a, grad_b, grad_c), counts):
        out[...] = rows[pl.ds(pl.multiple_of(start, 16), n), :]
        start = start + n


def join_back_kernel(
    lead, line, size, given, grad_rows, part, got, resid, gain, weight, near, far, near_pick,
    far_pick, hidden_bias, *refs,
):
    earlier, refs = refs[:given], refs[given:]
    (
        d_resid, d_near, d_far, gain_grad, shift_grad, bias_grad, out_near, out_far, d_join,
    ) = refs
    gain_grad[...] = jnp.zeros_like(gain_grad)
    shift_grad[...] = jnp.zeros_like(shift_grad)
    bias_grad[...] = jnp.zeros_like(bias_grad)
    for t in tiles(resid.shape[0]):
        d_out = part[t, :].astype(f32) + got[t, :].astype(f32)
        d_rows, d_gain, d_shift = norm_back(resid[t, :], gain[...], d_out)
        gain_grad[...] += d_gain
        shift_grad[...] += d_shift
        d_rows = d_rows + grad_rows[t, :].astype(f32)
        d_resid[t, :] = d_rows
        low = d_rows.astype(bf16)
        d_join[t, :] = low
        bias_grad[...] += jnp.sum(low.astype(f32), axis=0, keepdims=True)
    cols = near.shape[1]
    d_near[...] = mm_nt(d_join[...], weight[:cols, :]).astype(bf16)
    d_far[...] = mm_nt(d_join[...], weight[cols:, :]).astype(bf16)
    grad_near = mm_tn(near[...], d_join[...]).astype(bf16)
    grad_far = mm_tn(far[...], d_join[...]).astype(bf16)
    lines = out_near.shape[0]
    for pick, out in ((near_pick, out_near), (far_pick, out_far)):
        total = mm_tn(pick[:cols, :], grad_near) + mm_tn(pick[cols:, :], grad_far)
        out[:lines, :] = total.astype(bf16)
    for other in earlier:
        out_far[lines:, :] = other[...]
    n, units = hidden_bias.shape
    rows = out_near.shape[0] // n
    unit = lax.broadcasted_iota(jnp.int32, (units, 128), 0)
    lane = lax.broadcasted_iota(jnp.int32, (units, 128), 1)
    place = (unit % size == lane).astype(f32).astype(bf16)
    mask = line_mask((rows, units), lead, line, size)
    for k in range(n):
        lines = jnp.where(mask, hidden_bias[k : k + 1, :], 0.0).astype(bf16)
        part_rows = slice(k * rows, (k + 1) * rows)
        lines = mm(lines, place) + out_near[part_rows, :128].astype(f32)
        out_near[part_rows, :128] = lines.astype(bf16)


def rows_back_kernel(
    d_resid, near, far, peer_near, peer_far, place, rows, gain, grad_rows, gain_grad, shift_grad
):
    cols = near.shape[1]
    gain_grad[...] = jnp.zeros_like(gain_grad)
    shift_grad[...] = jnp.zeros_like(shift_grad)
    for t in tiles(rows.shape[0]):
        d_out = mm(near[t, :], place[:cols, :]) + mm(far[t, :], place[cols : 2 * cols, :])
        d_out = d_out + mm(peer_near[t, :], place[2 * cols : 3 * cols, :])
        d_out = d_out + mm(peer_far[t, :], place[3 * cols :, :])
        d_rows, d_gain, d_shift = norm_back(rows[t, :].astype(f32), gain[...], d_out)
        gain_grad[...] += d_gain
        shift_grad[...] += d_shift
        grad_rows[t, :] = d_resid[t, :] + d_rows


def group_pieces(counts):
    total = sum(counts)
    start = 0
    found = []
    for bucket, n in enumerate(counts):
        for chip in range(2):
            for core in range(2):
                found.append((bucket, chip, core * total + start, (2 * chip + core) * n, n))
        start = start + n
    return found


def load_groups(counts, y, near, far, whole, buckets):
    whole[y] = near[...]
    whole[1 - y] = far[...]
    for bucket, chip, source, target, n in group_pieces(counts):
        buckets[bucket][target : target + n, :] = whole[chip, source : source + n, :]


def store_groups(counts, y, buckets, whole, near, far):
    for bucket, chip, source, target, n in group_pieces(counts):
        whole[chip, source : source + n, :] = buckets[bucket][target : target + n, :]
    near[...] = whole[y]
    far[...] = whole[1 - y]


def head_lanes(shape, h):
    return lax.broadcasted_iota(jnp.int32, shape, 1) // HD == h


def only_head(v, h):
    return jnp.where(head_lanes(v.shape, h), v, jnp.zeros_like(v))


def soft(level, h, act, length, span, second, second_bias, random, tile):
    if level == 0:
        scores = mm(only_head(act, h), second[:, :span]) + second_bias[h : h + 1, :span]
    else:
        scores = random[h, tile, :span].astype(f32)
    keys = lax.broadcasted_iota(jnp.int32, scores.shape, 1) < length
    scores = jnp.where(keys, scores, MASKED_SCORE)
    e = jnp.exp(scores - jnp.max(scores, axis=-1, keepdims=True))
    return e * (1.0 / jnp.sum(e, axis=-1, keepdims=True))


def score_tiles(span):
    size = min(span, SCORE_TILE)
    return [pl.ds(i, size) for i in range(0, span, size)]


def diagonal(ref):
    cols = ref.shape[0]
    row = lax.broadcasted_iota(jnp.int32, (HD, cols), 0)
    col = lax.broadcasted_iota(jnp.int32, (HD, cols), 1)
    wide = mm(ref[...], one_hot(col % HD == row))
    row = lax.broadcasted_iota(jnp.int32, (cols, cols), 0)
    col = lax.broadcasted_iota(jnp.int32, (cols, cols), 1)
    return jnp.where(row // HD == col // HD, wide, 0.0).astype(bf16)


def synth_kernel(level, counts, scalars, near, far, first, first_bias, second, second_bias,
                 random, value, mixed_near, mixed_far, whole, rows_a, rows_b, rows_c,
                 mixed_a, mixed_b, mixed_c):
    y = scalars[0]
    rows, mixed = (rows_a, rows_b, rows_c), (mixed_a, mixed_b, mixed_c)
    heads = near.shape[1] // HD
    value = diagonal(value)
    if level == 0:
        first = diagonal(first)
    load_groups(counts, y, near, far, whole, rows)
    for k, span in enumerate((LA, LB, LC)):
        values = mm(rows[k][...], value).astype(bf16)
        by_head = [only_head(values, h) for h in range(heads)]
        for t in score_tiles(span):
            act = None
            if level == 0:
                act = gelu_both(mm(rows[k][t, :], first) + first_bias[...])[0].astype(bf16)
            total = None
            for h in range(heads):
                p = soft(level, h, act, scalars[1 + k], span, second, second_bias, random, t)
                term = mm(p.astype(bf16), by_head[h])
                total = term if total is None else total + term
            mixed[k][t, :] = total.astype(bf16)
    store_groups(counts, y, mixed, whole, mixed_near, mixed_far)


def pack_grads(heads, n_wide, value_high, value_low, second, second_bias, first, first_bias):
    cols = heads * HD

    def grid(shape):
        return [lax.broadcasted_iota(jnp.int32, shape, k) for k in range(2)]

    row, col = grid((cols, cols))
    same = row // HD == col // HD
    source, lane = grid((cols, 128))
    left = one_hot((source % HD == lane) & (lane < HD))
    right = one_hot((source % HD == lane - HD) & (lane >= HD))

    def blocks(v, place):
        return mm(jnp.where(same, v[...], 0.0).astype(bf16), place)

    column = jnp.sum(jnp.where(row == col, first_bias[...], 0.0), axis=1, keepdims=True)
    tail = blocks(value_high, left) + jnp.where(lane == HD, column, 0.0)
    row, col = grid((cols, second_bias.shape[0]))
    lines = mm(one_hot(row // HD == col), second_bias[...].astype(bf16))
    wide = LC // n_wide
    row, col = grid((cols, LC))
    lines = jnp.where(col // wide == (row % HD) // (HD // n_wide), lines, 0.0).astype(bf16)
    source, lane = grid((LC, 128))
    lines = mm(lines, one_hot((source % wide == lane) & (lane < wide)))
    rest = jnp.concatenate(
        [
            second[...].astype(bf16),
            (blocks(first, left) + blocks(value_low, right)).astype(bf16),
            tail.astype(bf16),
        ],
        axis=1,
    )
    return rest, lines.astype(bf16)


def wide_rows(shape, heads, z, x):
    n, lines = shape[0], shape[1]
    row = lax.broadcasted_iota(jnp.int32, (n * lines, heads * HD), 0)
    col = lax.broadcasted_iota(jnp.int32, (n * lines, heads * HD), 1)
    per = HD // (2 * n)
    wide = 2 * (z ^ (row // lines)) + x
    i = row % lines
    source = (i // per) * HD + wide * per + i % per
    return one_hot((source == col) & (i < heads * per))


def synth_back_kernel(level, counts, random_parts, scalars, near, far, d_near, d_far, first, first_bias, second,
                      second_bias, random, value, *refs):
    y = scalars[0]
    if level == 0:
        (value_high, dx_near, dx_far, pack_own, pack_other, *scratch) = refs
        *scratch, value_grad, second_grad, second_bias_grad, first_grad, first_bias_grad = scratch
        sums = (value_grad, second_grad, second_bias_grad, first_grad, first_bias_grad)
    else:
        dx_near, dx_far, value_grad, random_outs = *refs[:3], refs[3 : 3 + random_parts]
        *scratch, random_grad = refs[3 + random_parts :]
        sums = (value_grad, random_grad)
    whole, dx, *rest = scratch
    rows, d_mixed = rest[:3], rest[3:6]
    d_values = rest[6]
    heads = near.shape[1] // HD
    value = diagonal(value)
    if level == 0:
        first = diagonal(first)
    load_groups(counts, y, near, far, whole, rows)
    load_groups(counts, y, d_near, d_far, whole, d_mixed)
    for s in sums:
        s[...] = jnp.zeros_like(s)
    for k, span in enumerate((LA, LB, LC)):
        values = mm(rows[k][...], value).astype(bf16)
        d_values[:span, :] = jnp.zeros((span, heads * HD), f32)
        for t in score_tiles(span):
            x = rows[k][t, :]
            act = None
            if level == 0:
                act, slope = gelu_both(mm(x, first) + first_bias[...])
                act = act.astype(bf16)
                d_act = None
            dm = d_mixed[k][t, :]
            for h in range(heads):
                p = soft(level, h, act, scalars[1 + k], span, second, second_bias, random, t)
                dm_h = only_head(dm, h)
                dp = mm_nt(dm_h, values)
                d_values[:span, :] += mm_tn(p.astype(bf16), dm_h)
                ds = p * (dp - jnp.sum(p * dp, axis=-1, keepdims=True))
                if level == 0:
                    low = ds.astype(bf16)
                    second_bias_grad[h : h + 1, :span] += jnp.sum(
                        low.astype(f32), axis=0, keepdims=True
                    )
                    second_grad[:, :span] += mm_tn(only_head(act, h), low)
                    term = only_head(mm_nt(low, second[:, :span]), h)
                    d_act = term if d_act is None else d_act + term
                else:
                    random_grad[h, t, :span] += ds
            if level == 0:
                d_pre = (d_act * slope).astype(bf16)
                first_bias_grad[...] += jnp.sum(d_pre.astype(f32), axis=0, keepdims=True)
                first_grad[...] += mm_tn(x, d_pre)
                dx[t, :] = mm_nt(d_pre, first)
        d_low = d_values[:span, :].astype(bf16)
        value_grad[...] += mm_tn(rows[k][...], d_low)
        back = mm_nt(d_low, value)
        if level == 0:
            back = back + dx[:span, :]
        d_mixed[k][...] = back.astype(bf16)
    store_groups(counts, y, d_mixed, whole, dx_near, dx_far)
    if level == 0:
        packed = pack_grads(
            heads, 2 * pack_own.shape[0], value_high, value_grad, second_grad, second_bias_grad, first_grad,
            first_bias_grad,
        )
        for side, out in enumerate((pack_own, pack_other)):
            half = out.shape[1] - 16
            pick = wide_rows((out.shape[0], half), heads, scalars[6], scalars[5] ^ side)
            rest, last = (
                mm(pick, part).astype(bf16).reshape(out.shape[0], half, -1) for part in packed
            )
            out[:, :half, :] = rest
            out[:, half:, :] = jnp.zeros((out.shape[0], 16, D), bf16)
            for i in range(half // 16):
                part = slice(i * 128, (i + 1) * 128)
                out[:, half:, part] = last[:, i * 16 : (i + 1) * 16, :]
    if level == 1 and random_parts == 1:
        random_outs[0][...] = random_grad[...].astype(bf16)
    elif level == 1:
        n, lines = random_outs[0].shape[0], random_outs[0].shape[1] // heads
        for side, out in enumerate(random_outs):
            for i in range(n):
                wide = 2 * (scalars[6] ^ i) + (scalars[5] ^ side)
                at = pl.ds(pl.multiple_of(wide * lines, 16), lines)
                for h in range(heads):
                    out[i, h * lines : (h + 1) * lines, :] = random_grad[h, at, :].astype(bf16)


def per_device(
    links,
    tokens_a,
    tokens_b,
    tokens_c,
    lengths_a,
    lengths_b,
    lengths_c,
    cotan_a,
    cotan_b,
    cotan_c,
    ln_gain,
    ln_bias,
    row_bias,
    out_weight,
    up_weight,
    up_bias,
    down_weight,
    synth_first,
    synth_first_bias,
    synth_second,
    synth_second_bias,
    random_scores,
    value_weight,
):
    counts = (tokens_a.shape[0], tokens_b.shape[0], tokens_c.shape[0])
    starts = (0, counts[0], counts[0] + counts[1])
    rows = sum(counts)
    heads = synth_first.shape[0]
    z, x, y, c = links.places()
    nz, n_wide = links.nz, links.n_wide
    chips = 2 * nz
    cols = heads * HD
    out_rows, ff_rows = out_weight.shape[1], up_weight.shape[1]
    size = ff_rows // 2
    units = chips * size
    lead = 16
    half_out = -(-out_rows // 2)
    aligned = size % 16 == 0
    n = 4
    scalars = jnp.stack([y, lengths_a[0], lengths_b[0], lengths_c[0], c, x, z]).astype(jnp.int32)

    def misc_halves(level):
        high = up_bias[level].astype(bf16)
        low = (up_bias[level] - high.astype(f32)).astype(bf16)
        found = []
        for side in range(2):
            w = out_weight[level, side * half_out : (side + 1) * half_out]
            part = slice(side * size, (side + 1) * size)
            line = jnp.pad(jnp.concatenate([high[part], low[part]])[None], ((0, 0), (0, D - ff_rows)))
            w = jnp.pad(w, ((0, half_out - w.shape[0]), (0, 0)))
            found.append(
                jnp.pad(jnp.concatenate([w, line], axis=0), ((0, lead - half_out - 1), (0, 0)))
            )
        return jnp.stack(found)

    misc = jnp.stack([misc_halves(level) for level in range(LAYERS)])
    tokens = (tokens_a, tokens_b, tokens_c, cotan_a, cotan_b, cotan_c)
    wide, half = lead + size, lead + 3 * size
    if aligned:
        (mine,) = lay_out(pack_rows_kernel, [2 * rows], tokens, len(tokens))
        first_rows, rest_rows = lay_out(
            partial(pack_weights_kernel, size),
            [2 * wide, 2 * half],
            (misc, up_weight, down_weight),
            12,
        )
    else:
        mine = jnp.concatenate(tokens, axis=0)
        parts = [slice(0, size), slice(size, 2 * size)]
        first_rows = jnp.concatenate(
            [v for k, p in enumerate(parts) for v in (misc[0, k], up_weight[0, p])]
        )
        rest_rows = jnp.concatenate(
            [
                v
                for k, p in enumerate(parts)
                for v in (misc[1, k], down_weight[0, p], up_weight[1, p], down_weight[1, p])
            ]
        )
    peer = links.swap(mine, c=1)
    first_rows, rest_rows = first_rows[None], rest_rows[None]
    first_got = links.swap(first_rows, z=1)
    rest_got = links.swap(rest_rows, z=1)

    def block_lines(block):
        return block * cols + jnp.arange(cols)

    wanted = jnp.concatenate([block_lines(links.nc * y + c), block_lines(links.nc * (1 - y) + c)])
    their_wanted = jnp.concatenate(
        [block_lines(links.nc * y + 1 - c), block_lines(links.nc * (1 - y) + 1 - c)]
    )

    def misc_numbers(core):
        iz, ix, iy = z ^ jnp.arange(nz), x ^ jnp.arange(2), y ^ jnp.arange(2)
        device = links.number(iz[:, None, None], ix[None, :, None], iy[None, None, :], core)
        i = jnp.arange(lead)
        a_rows = jnp.where(i < half_out, i, -1)
        b_rows = jnp.where(i < out_rows - half_out, half_out + i, -1)
        found = []
        for side, lines in ((0, a_rows), (1, a_rows), (2, b_rows), (3, b_rows)):
            at = device[:, :, side].T if side < 2 else device[:, side - 2, :].T
            found.append(jnp.where(lines < 0, -1, at[..., None] * out_rows + lines).reshape(-1))
        return jnp.concatenate(found)

    own_numbers, peer_numbers = misc_numbers(c), misc_numbers(1 - c)
    near_pick = (wanted[:, None] == own_numbers[None, :]).astype(bf16)
    far_pick = (wanted[:, None] == peer_numbers[None, :]).astype(bf16)
    their_pick = (their_wanted[:, None] == own_numbers[None, :]).astype(bf16)
    pick_cols = (jnp.arange(D)[:, None] == wanted[None, :]).astype(bf16)
    places = jnp.concatenate([wanted, their_wanted])
    place_cols = (places[:, None] == jnp.arange(D)[None, :]).astype(bf16)

    first_bias = synth_first_bias.reshape(1, cols)
    second = synth_second.reshape(cols, LC)
    values = [value_weight[level].reshape(cols, HD) for level in range(LAYERS)]
    first = synth_first.reshape(cols, HD)
    head_weights = [
        (first, first_bias, second, synth_second_bias, first_bias, values[0]),
        (first_bias, first_bias, first_bias, first_bias, random_scores, values[1]),
    ]

    def line(v, level, which):
        return v[level, which][None]

    chip_rows = 2 * rows
    row_low, row_high = ((chip_rows, D), bf16), ((chip_rows, D), f32)
    head_low, vector = ((chip_rows, cols), bf16), ((1, D), f32)
    hidden_low = ((n, chip_rows, units), bf16)
    groups = [pltpu.VMEM((4 * k, cols), bf16) for k in counts]
    group_pair = pltpu.VMEM((2, chip_rows, cols), bf16)

    def refs(blocks, at, length):
        if aligned:
            return list(blocks), at
        return [b[:, at : at + length].reshape(-1, D) for b in blocks], None

    def synthesis(level, own, got, *wait):
        return stage(
            4.5 if level == 0 else 2.3,
            partial(synth_kernel, level, counts),
            [head_low] * 2,
            (scalars, own, got, *head_weights[level]),
            scratch=[group_pair, *groups, *groups],
            smem=1,
            wait=wait,
        )

    def pick(blocks, *wait):
        blocks, at = refs(blocks, 0, lead)
        out = ((2 * cols, D), bf16)
        mine, theirs = stage(
            1.4,
            partial(pick_kernel, at, lead),
            [out, out],
            (near_pick, their_pick, *blocks),
            wait=wait,
        )
        return mine, links.swap(theirs, c=1)

    def join(near, far, mine, got):
        part, weight = stage(
            0.6,
            join_kernel,
            [row_low, ((2 * cols, D), bf16)],
            (near, far, mine, got),
            wait=[space(mine)],
        )
        return part, links.swap(part, c=1), weight

    def ffn_up(level, rows_in, part, got, ups, miscs, *wait):
        ups, at = refs(ups, lead if level == 0 else 0, size)
        miscs, misc_at = refs(miscs, 0, lead)
        return stage(
            3.6,
            partial(ffn_up_kernel, n, at, misc_at, size, lead, half_out),
            [row_high, row_low, hidden_low, hidden_low],
            (
                rows_in,
                part,
                got,
                line(row_bias, level, 0),
                line(ln_gain, level, 1),
                line(ln_bias, level, 1),
                *ups,
                *miscs,
            ),
            wait=[space(part), *wait],
        )

    def ffn_down(level, hidden, downs, *wait):
        downs, at = refs(downs, lead if level == 0 else size, size)
        (ffn,) = stage(1.6, partial(ffn_down_kernel, n, at, size), [row_low], (hidden, *downs), wait=wait)
        return ffn, links.swap(ffn, c=1)

    gain, shift = line(ln_gain, 0, 0), line(ln_bias, 0, 0)
    token_rows, cotan_rows, own_first, far_first = stage(
        1.6,
        first_norm_kernel,
        [row_low, row_low, head_low, head_low],
        (scalars, mine, peer, gain, shift, pick_cols),
        smem=1,
    )
    got_first = links.swap(far_first, y=1)
    def whole(length):
        return [(0, 0, length, 0, 0), (1, 0, length, 1, 0)]

    (first_rows,) = assemble(
        [first_rows, first_got], [((2, 2 * wide), whole(2 * wide))]
    )
    first_z = Spread(links, first_rows)
    first_z.start_z()
    mixed_first, mixed_far = synthesis(0, own_first, got_first, space(own_first))
    mixed_got_first = links.swap(mixed_far, y=1)

    def pieces(start, length):
        return [
            (source, start + side * half, length, source, side * length)
            for source in range(2)
            for side in range(2)
        ]

    second_rows, last_rows = assemble(
        [rest_rows, rest_got],
        [((2, 2 * wide), pieces(0, wide)), ((2, 4 * size), pieces(wide, 2 * size))],
        [mixed_first],
    )
    second_z, last_z = Spread(links, second_rows), Spread(links, last_rows)
    second_z.start_z()
    (first_chunk,) = first_z.end_z([(0, wide, wide)], mixed_first)
    first_chunk.start_near()
    first_chunk.start_far()
    last_z.start_z(mixed_got_first)
    mine_first, got_weight = pick(first_chunk.blocks())
    (second_chunk,) = second_z.end_z([(0, wide, wide)], first_chunk.a, mixed_got_first)
    second_chunk.start_near()
    part, part_got, out_first = join(mixed_first, mixed_got_first, mine_first, got_weight)
    (last_chunk,) = last_z.end_z([(0, 2 * size, 2 * size)], part)
    second_chunk.start_far()
    last_chunk.start_near()
    resid_first, normed_first, *saved_first = ffn_up(
        0, token_rows, part, part_got, first_chunk.blocks(), first_chunk.blocks()
    )
    ffn, ffn_got = ffn_down(0, saved_first[0], second_chunk.blocks())

    rows_second, own_second, far_second = stage(
        1.1,
        next_norm_kernel,
        [row_high, head_low, head_low],
        (
            resid_first,
            ffn,
            ffn_got,
            line(row_bias, 0, 1),
            line(ln_gain, 1, 0),
            line(ln_bias, 1, 0),
            pick_cols,
        ),
        wait=[space(ffn)],
    )
    got_second = links.swap(far_second, y=1)
    mine_second, got_weight = pick(second_chunk.blocks(), rows_second)
    mixed_second, mixed_far = synthesis(1, own_second, got_second, space(own_second))
    mixed_got_second = links.swap(mixed_far, y=1)
    last_chunk.start_far(mixed_got_second)
    part, part_got, out_second = join(mixed_second, mixed_got_second, mine_second, got_weight)
    resid_second, normed_second, *saved_second = ffn_up(
        1, rows_second, part, part_got, last_chunk.blocks(), second_chunk.blocks()
    )

    def ffn_back(level, grad_rows, normed, saved, ups, downs, *wait):
        ups, up_at = refs(ups, lead if level == 0 else 0, size)
        downs, down_at = refs(downs, lead if level == 0 else size, size)
        out = ((chips, 2 * size, D) if aligned else (2, units, D), bf16)
        outs = [out] * n
        if aligned and level == 1:
            part = ((chips, size, D), bf16)
            outs = [out, part, out, out, part]
        hidden, slope = saved
        d_normed, bias_grad, hidden_bias, d_pre = stage(
            3.5,
            partial(ffn_back_kernel, n, up_at, down_at, size),
            [row_low, vector, ((n, units), f32), hidden_low],
            (grad_rows, slope, *ups, *downs),
            wait=wait,
        )
        terms = stage(
            3.0,
            partial(ffn_terms_kernel, n, not aligned, size),
            outs,
            (grad_rows, normed, hidden, d_pre),
        )
        if not aligned:
            terms = [t.reshape(2, chips, size, D) for t in terms]
            parts = list(terms[1])
            terms = [jnp.concatenate(list(t), axis=1) for t in terms]
            if level == 1:
                terms = [terms[0], parts[0], *terms[2:], parts[1]]
        return d_normed, links.swap(d_normed, c=1), bias_grad, hidden_bias, terms

    def join_back(
        level, grad_rows, part, got, resid, weight, near, far, hidden_bias, *wait, earlier=()
    ):
        misc_out = ((n * chips * lead, D), bf16)
        far_out = (((1 + len(earlier)) * n * chips * lead, D), bf16)
        d_resid, d_own, d_far, gain, shift, bias, out_near, out_far = stage(
            3.2,
            partial(join_back_kernel, lead, half_out, size, len(earlier)),
            [row_high, head_low, head_low, vector, vector, vector, misc_out, far_out],
            (
                grad_rows,
                part,
                got,
                resid,
                line(ln_gain, level, 1),
                weight,
                near,
                far,
                near_pick,
                far_pick,
                hidden_bias,
                *earlier,
            ),
            scratch=[pltpu.VMEM((chip_rows, D), bf16)],
            wait=wait,
        )
        return d_resid, d_own, links.swap(d_far, y=1), (gain, shift, bias), out_near, out_far

    lines = LC // n_wide
    random_parts = 2 if lines % 16 == 0 else 1
    lines_each = -(-heads * HD // n_wide // 16) * 16

    def synth_back(level, own, got, d_own, d_got, value_high=(), wait=()):
        square = pltpu.VMEM((cols, cols), f32)
        scratch = [group_pair, pltpu.VMEM((LC, cols), f32), *groups, *groups]
        scratch = scratch + [pltpu.VMEM((LC, cols), f32)]
        if level == 0:
            outs = [((nz, lines_each + 16, D), bf16)] * 2
            scratch = scratch + [
                square,
                pltpu.VMEM((cols, LC), f32),
                pltpu.VMEM((8, LC), f32),
                square,
                pltpu.VMEM((1, cols), f32),
            ]
        else:
            random_out = (nz, heads * lines, LC) if random_parts == 2 else (heads, LC, LC)
            outs = [((cols, cols), f32)] + [(random_out, bf16)] * random_parts
            scratch = scratch + [pltpu.VMEM((heads, LC, LC), f32)]
        dx_own, dx_far, *found = stage(
            10.4 if level == 0 else 4.6,
            partial(synth_back_kernel, level, counts, random_parts),
            [head_low] * 2 + outs,
            (scalars, own, got, d_own, d_got, *head_weights[level], *value_high),
            scratch=scratch,
            smem=1,
            wait=wait,
        )
        return dx_own, links.swap(dx_far, y=1), links.swap(dx_own, c=1), found

    d_normed, d_got, ffn_bias_second, hidden_bias, terms_second = ffn_back(
        1, cotan_rows, normed_second, saved_second, last_chunk.blocks(), last_chunk.blocks()
    )
    x_near = links.swap(terms_second[3], x=1)
    y_down = links.swap(terms_second[1], y=1)
    d_resid, d_own, d_mixed_got, stats_second, near_second, far_second_out = join_back(
        1, cotan_rows, d_normed, d_got, resid_second, out_second, mixed_second, mixed_got_second,
        hidden_bias, space(d_normed),
    )
    y_up = links.swap(after(terms_second[4], d_mixed_got), y=1)
    dx_own, dx_got, dx_peer, found_second = synth_back(
        1, own_second, got_second, d_own, d_mixed_got, wait=[space(d_own)]
    )
    dx_peer_got = links.swap(dx_got, c=1)
    spaced = space(dx_own)
    send, b_keep = fold_first(terms_second[2], [x_near], dx_got, spaced)
    y_far = links.swap(send, y=1)
    send, a_keep = fold_first(terms_second[0], [y_down, y_up], dx_got, spaced)
    x_far = links.swap(send, x=1)
    grad_rows, *stats_rows_second = stage(
        1.5,
        rows_back_kernel,
        [row_high, vector, vector],
        (
            d_resid, dx_own, dx_got, dx_peer, dx_peer_got, place_cols, rows_second,
            line(ln_gain, 1, 0),
        ),
        wait=[a_keep, b_keep, space(dx_got, spaced)],
    )
    if random_parts == 2:
        x_random = links.swap(found_second[2], x=1)

    wait = []
    if random_parts == 2:
        x_random = after(x_random, grad_rows)
        wait.append(x_random)

    d_normed, d_got, ffn_bias_first, hidden_bias, terms_first = ffn_back(
        0, grad_rows, normed_first, saved_first, first_chunk.blocks(), second_chunk.blocks(),
        *wait,
    )
    d_resid, d_own, d_mixed_got, stats_first, near_first, far_out = join_back(
        0, grad_rows, d_normed, d_got, resid_first, out_first, mixed_first, mixed_got_first,
        hidden_bias, space(d_normed), earlier=[far_second_out],
    )
    far_out = links.swap(far_out, c=1)
    second_fold = Fold(links, [(a_keep, x_far), (b_keep, y_far)], d_own, halves=True)
    second_fold.start()
    if aligned:
        terms_first = stage(
            1.5,
            misc_kernel,
            [((chips, 2 * size + 2 * lead, D), bf16)] * n,
            (near_first, near_second, far_out, *terms_first),
        )
    else:
        misc = [v.reshape(n, chips, lead, D) for v in (near_first, near_second)]
        got = list(far_out.reshape(2, n, chips, lead, D))
        misc = jnp.concatenate([a + b for a, b in zip(misc, got)], axis=2)
        terms_first = [jnp.concatenate([t, m], axis=1) for t, m in zip(terms_first, misc)]
    x_near = links.swap(terms_first[3], x=1)
    y_near = links.swap(after(terms_first[1], d_mixed_got), y=1)
    wait = []
    if random_parts == 2:
        random_fold = Fold(
            links, [(found_second[1], x_random)], second_fold.keep, halves=True
        )
        wait.append(random_fold.keep)
    dx_own, dx_got, dx_peer, found_first = synth_back(
        0, own_first, got_first, d_own, d_mixed_got, (found_second[0],),
        (second_fold.keep, terms_first[0], space(d_own), *wait),
    )
    spaced = space(dx_own)
    pack_own, pack_other = found_first
    second_last = second_fold.step(dx_own)
    if random_parts == 2:
        random_fold.start(second_last)
    send, b_keep = fold_first(terms_first[2], [x_near], dx_own, spaced, second_last)
    y_far = links.swap(after(send, y_near), y=1)
    send, a_keep = fold_first(terms_first[0], [y_near], b_keep, rest=[pack_other])
    x_far = links.swap(send, x=1)
    dx_peer_got = links.swap(after(dx_got, a_keep), c=1)
    *grad_parts, gain, shift = stage(
        1.7,
        partial(rows_last_kernel, counts),
        [((k, D), f32) for k in counts] + [vector, vector],
        (
            scalars, d_resid, dx_own, dx_got, dx_peer, dx_peer_got, place_cols, token_rows,
            line(ln_gain, 0, 0),
        ),
        scratch=[pltpu.VMEM((chip_rows, D), f32)],
        smem=1,
        wait=[a_keep, b_keep, space(a_keep)],
    )
    ffn, ffn_got = ffn_down(1, saved_second[0], last_chunk.blocks(), a_keep)
    out_parts = stage(
        1.0,
        partial(last_kernel, counts),
        [((k, D), bf16) for k in counts],
        (scalars, resid_second, ffn, ffn_got, line(row_bias, LAYERS - 1, 1)),
        smem=1,
    )

    (summed,) = stage(
        1.0,
        stats_kernel,
        [((LAYERS * 6, D), f32)],
        [
            row
            for inner, (gain_second, shift_second, bias), ffn_bias in (
                ((gain, shift), stats_first, ffn_bias_first),
                (stats_rows_second, stats_second, ffn_bias_second),
            )
            for row in (inner[0], gain_second, inner[1], shift_second, bias, ffn_bias)
        ],
    )

    pack_at = a_keep.shape[1]
    first_fold = Fold(
        links, [(a_keep, x_far), (b_keep, y_far), (pack_own, x_far, pack_at)]
    )
    first_fold.start()
    summed = links.total(summed, first_fold.keep, first_fold.keep)
    summed = summed.reshape(LAYERS, 6, D)
    if random_parts == 2:
        random_fold.step(a_keep)
        random = random_fold.finish(first_fold.keep)
    else:
        random = found_second[1].reshape(heads, n_wide, lines, LC)
        random = lax.psum_scatter(random, "wide", scatter_dimension=1, tiled=False).astype(f32)
    if aligned and nz <= 4:
        weight = ((LAYERS, 2 * size, D), f32)
        folds = (first_fold, second_fold)
        down_grad, up_grad, misc, pack = stage(
            1.0,
            partial(finish_kernel, size, lead, len(first_fold.gots)),
            [weight, weight, ((LAYERS, 2, lead, D), f32), (pack_own.shape[1:], f32)],
            [f.keep for f in folds] + first_fold.gots + second_fold.gots,
        )
    else:
        found, layer = first_fold.finish(), second_fold.finish().reshape(2, -1, D)
        found, pack = found[: 2 * pack_at].reshape(2, -1, D), found[2 * pack_at :]
        found = [found, layer]
        down_grad = jnp.stack([v[:, :size].reshape(-1, D) for v in found])
        up_grad = jnp.stack([v[:, size : 2 * size].reshape(-1, D) for v in found])
        misc = found[0][:, 2 * size :].reshape(2, LAYERS, lead, D)
        misc = jnp.moveaxis(misc, 0, 1)
    pack_rows = heads * HD // n_wide
    rest = pack[:pack_rows].reshape(heads, HD // n_wide, D)
    first_rows = HD // n_wide
    bias_lines = [
        pack[lines_each + k % 16, 128 * (k // 16) : 128 * (k // 16) + lines]
        for k in range(0, pack_rows, first_rows)
    ]
    out_grad = misc[:, :, :half_out].reshape(LAYERS, -1, D)[:, :out_rows]
    bias_grad = misc[:, :, half_out, :size].reshape(LAYERS, -1)
    return (
        *out_parts,
        *grad_parts,
        summed[:, 0:2],
        summed[:, 2:4],
        summed[:, 4:6],
        out_grad,
        up_grad,
        bias_grad,
        down_grad,
        rest[:, :, LC : LC + HD],
        rest[:, :, LC + 128 + HD],
        rest[:, :, :LC],
        jnp.stack(bias_lines),
        random.reshape(heads, lines, LC),
        jnp.stack([rest[:, :, LC + HD : LC + 128], rest[:, :, LC + 128 : LC + 128 + HD]]),
    )


def solution(mesh):
    placed = (
        P(("wide", "head"), None),
        P(("wide", "head"), None),
        P(("wide", "head"), None),
        P("wide"),
        P("wide"),
        P("wide"),
        P(("wide", "head"), None),
        P(("wide", "head"), None),
        P(("wide", "head"), None),
        P(),
        P(),
        P(),
        P(None, ("wide", "head"), None),
        P(None, ("wide", "head"), None),
        P(None, ("wide", "head")),
        P(None, ("wide", "head"), None),
        P("head", None, None),
        P("head", None),
        P("head", None, None),
        P("head", None),
        P("head", None, None),
        P(None, "head", None, None),
    )
    return jax.shard_map(
        partial(per_device, Links(mesh.shape["wide"], mesh.shape["head"])),
        mesh=mesh,
        in_specs=placed,
        out_specs=(
            P(("wide", "head"), None),
            P(("wide", "head"), None),
            P(("wide", "head"), None),
            P(("wide", "head"), None),
            P(("wide", "head"), None),
            P(("wide", "head"), None),
            P(),
            P(),
            P(),
            P(None, ("wide", "head"), None),
            P(None, ("wide", "head"), None),
            P(None, ("wide", "head")),
            P(None, ("wide", "head"), None),
            P("head", "wide", None),
            P("head", "wide"),
            P("head", "wide", None),
            P("head", "wide"),
            P("head", "wide", None),
            P(None, "head", "wide", None),
        ),
        check_vma=False,
    )
```
